32 devices in a mesh: gz: 8 (over z, x), gx: 4 (over y, core).
Axes of the slice: x: 2, y: 2, z: 4, core: 2. Of those that a mesh axis runs over, the one named last changes fastest.
Arguments:
- atom_velocity: float32 [3, 4096, 128], P(None, ('gz', 'gx')), may hold values from -4.2 to 4.2
- atom_noise: float32 [3, 4096, 128], P(None, ('gz', 'gx')), may hold values from -6 to 6
- atom_plane: int32 [4096, 128], P(('gz', 'gx')), may hold values from 0 to 127, as said below
- atom_column: int32 [4096, 128], P(('gz', 'gx')), may hold values from 0 to 4095
- brick_count: int32 [4096], P(('gz', 'gx')), may hold values from 32 to 128, as said below
- electron_temp: float32 [128, 64, 256], P('gz', 'gx'), may hold values from 0.05 to 3.8
Outputs:
- new_temp: float32 [128, 64, 256], P('gz', 'gx')
- new_velocity: float32 [3, 4096, 128], P(None, ('gz', 'gx'))
The draws below stay inside these ranges and needn't reach their ends.
Inputs may be any that keep to these rules, and one draw needn't show every extreme that they name: `atom_plane`: all 128 entries of a brick lie in one slab of 16 planes (the planes of one gz index). No slab holds more than 32 bricks of one device, and in every draw one slab holds exactly 32 bricks of every device. `brick_count`: every device holds a brick with 128 used slots.
All inputs are finite; a program needn't handle non-finite values.
Results may differ from the reference program's by a relative error of at most 0.00035.
Values sent between devices are 32-bit elements; how exact they have to be, the bound alone decides.
No kernel may reach another device: no remote copies, remote signals or barrier semaphores. Data moves between devices by JAX's collectives and lax.ppermute only.
A program may use at most 128 MiB of HBM per device.

```python
import math
import jax
import jax.numpy as jnp
from jax import lax

CZ = 16
CX = 16
NY = 256
BRICK_DEV = 128
ROW_ATOMS = 128
NZ = 128
NX = 64
BRICKS = 4096
N_GX = 4


def hot_slab_index(key):
    return jax.random.randint(jax.random.fold_in(key, 5), (), 0, NZ // CZ)


def draw_atom_plane(key, part):
    slab_count = NZ // CZ
    device_count = BRICKS // BRICK_DEV
    slot_count = 2 * BRICK_DEV // slab_count
    hot_slab = hot_slab_index(key)
    key_rotation = jax.random.fold_in(jax.random.fold_in(key, 11), 1)
    key_order = jax.random.fold_in(jax.random.fold_in(key, 11), 2)
    key_plane = jax.random.fold_in(jax.random.fold_in(key, 11), 3)
    rotation = jax.random.randint(key_rotation, (device_count, 1), 0, slab_count - 1)
    position = jnp.arange(BRICK_DEV, dtype=jnp.int32)[None, :]
    others = (hot_slab + 1 + jnp.mod(position - slot_count + rotation, slab_count - 1)) % slab_count
    sorted_owner = jnp.where(position < slot_count, hot_slab, others)
    orders = jax.vmap(lambda sub_key: jax.random.permutation(sub_key, BRICK_DEV))(jax.random.split(key_order, device_count))
    owner_slab = jnp.take_along_axis(sorted_owner, orders, axis=1).reshape(BRICKS)
    offsets = jax.random.randint(key_plane, (BRICKS, ROW_ATOMS), 0, CZ)
    return (owner_slab[:, None] * CZ + offsets).astype(jnp.int32)


def draw_brick_count(key, part):
    device_count = BRICKS // BRICK_DEV
    key_base, key_full = jax.random.split(jax.random.fold_in(key, 23))
    counts = jax.random.randint(key_base, (device_count, BRICK_DEV), 32, ROW_ATOMS + 1)
    full_spot = jax.random.randint(key_full, (device_count, 1), 0, BRICK_DEV)
    position = jnp.arange(BRICK_DEV, dtype=jnp.int32)[None, :]
    counts = jnp.where(position == full_spot, ROW_ATOMS, counts)
    counts = jnp.where(position == (full_spot + 1) % BRICK_DEV, 32, counts)
    return counts.reshape(BRICKS).astype(jnp.int32)


def draw_electron_temp(key, part):
    hot_slab = hot_slab_index(key)
    key_phase, key_rough, key_cold = jax.random.split(jax.random.fold_in(key, 37), 3)
    phase = jax.random.uniform(key_phase, (1, NX, NY), jnp.float32, -math.pi, math.pi)
    depth = jnp.arange(NZ, dtype=jnp.float32)[:, None, None]
    profile = jnp.exp(0.69 * jnp.tanh(3.0 * jnp.sin(2.0 * math.pi * depth / 384.0 + phase)))
    roughness = jnp.exp(jax.random.uniform(key_rough, (NZ, NX, NY), jnp.float32, math.log(0.1), math.log(1.9)))
    cold = jax.random.uniform(key_cold, (NZ, NX, NY), jnp.float32, 0.05, 0.15)
    slab_of_plane = jnp.arange(NZ, dtype=jnp.int32)[:, None, None] // CZ
    return jnp.where(slab_of_plane == hot_slab, cold, profile * roughness).astype(jnp.float32)


def touch_ends(drawn, own_key, least, largest):
    dims = drawn.shape
    spot = [jax.random.randint(jax.random.fold_in(own_key, axis), (), 0, dims[axis]) for axis in range(len(dims))]
    drawn = drawn.at[tuple(spot)].set(least)
    longest = dims.index(max(dims))
    spot[longest] = (spot[longest] + 1) % dims[longest]
    return drawn.at[tuple(spot)].set(largest)


def block_scale(stream_key, extent, cuts, low, top_value):
    factor_of = 1.0
    for dim, blocks in cuts:
        draws = jax.random.uniform(jax.random.fold_in(jax.random.fold_in(stream_key, 6), dim), (blocks,), jnp.float32, low / len(cuts), top_value / len(cuts))
        factor_of = factor_of * jnp.repeat(jnp.exp(draws), extent[dim] // blocks).reshape((-1,) + (1,) * (len(extent) - 1 - dim))
    return factor_of


def normal_values(key, shape, deviation, limit, pieces=(), kind=jnp.bfloat16):
    loudness = block_scale(key, shape, pieces, -0.22, 0.18) if pieces else 1.0
    values = jax.random.normal(key, shape, jnp.float32) * deviation * loudness
    return jnp.minimum(jnp.maximum(values, -limit), limit).astype(kind)


def setup_inputs(seed: int = 0) -> dict:
    arg_keys = jax.random.split(jax.random.key(seed), 7)
    return {
        "atom_velocity": normal_values(arg_keys[0], (3, BRICKS, ROW_ATOMS), 0.7, 4.2, ((1, 32),), jnp.float32),
        "atom_noise": normal_values(arg_keys[1], (3, BRICKS, ROW_ATOMS), 1.0, 6.0, ((1, 32),), jnp.float32),
        "atom_plane": draw_atom_plane(jax.random.fold_in(arg_keys[6], 71), 0),
        "atom_column": touch_ends(jax.random.randint(arg_keys[3], (BRICKS, ROW_ATOMS), 0, CX * NY), jax.random.fold_in(arg_keys[3], 1), 0, (CX * NY) - 1).astype(jnp.int32),
        "brick_count": draw_brick_count(jax.random.fold_in(arg_keys[6], 71), 0),
        "electron_temp": draw_electron_temp(jax.random.fold_in(arg_keys[6], 71), 0),
    }


STIFFNESS = 10000.0
LATERAL = 0.1
COUPLE = 0.5
TWO_THIRDS = 2.0 / 3.0
KICK_RATE = 0.2

def chain_solve(lower_band, diagonal, upper_band, right_side):

    def forward(state_pair, entries):
        sweep_ratio, sweep_value = state_pair
        below_band, middle, above_band, source = entries
        pivot_value = middle - below_band * sweep_ratio
        next_ratio = above_band / pivot_value
        next_value = (source - below_band * sweep_value) / pivot_value
        return ((next_ratio, next_value), (next_ratio, next_value))
    zero_start = jnp.zeros_like(diagonal[0])
    _, (ratios, values) = lax.scan(forward, (zero_start, zero_start), (lower_band, diagonal, upper_band, right_side))

    def backward(later_value, entries):
        ratio_here, value_here = entries
        result = value_here - ratio_here * later_value
        return (result, result)
    _, solution = lax.scan(backward, zero_start, (ratios, values), reverse=True)
    return solution

def reference(atom_velocity, atom_noise, atom_plane, atom_column, brick_count, electron_temp):
    cell_total = NZ * NX * NY
    brick_ids = jnp.arange(BRICKS, dtype=jnp.int32)
    column_group = brick_ids // BRICK_DEV % N_GX
    atom_lane = jnp.arange(ROW_ATOMS, dtype=jnp.int32)
    in_use = atom_lane[None, :] < brick_count[:, None]
    x_cell = column_group[:, None] * CX + atom_column // NY
    y_cell = atom_column % NY
    atom_cell = jnp.where(in_use, (atom_plane * NX + x_cell) * NY + y_cell, cell_total).astype(jnp.int32)
    kinetic = 0.5 * lax.optimization_barrier(jnp.sum(atom_velocity * atom_velocity, axis=0))
    flat_cell = atom_cell.reshape(-1)
    energy = jax.ops.segment_sum(kinetic.reshape(-1), flat_cell, cell_total + 1)[:cell_total].reshape(NZ, NX, NY)
    atom_count = jax.ops.segment_sum(jnp.ones_like(kinetic).reshape(-1), flat_cell, cell_total + 1)[:cell_total].reshape(NZ, NX, NY)
    lateral = LATERAL * (jnp.roll(electron_temp, 1, 1) + jnp.roll(electron_temp, -1, 1) + jnp.roll(electron_temp, 1, 2) + jnp.roll(electron_temp, -1, 2) - 4.0 * electron_temp)
    face_value = STIFFNESS * (0.5 * (electron_temp[1:] + electron_temp[:-1]))
    zero_plane = jnp.zeros((1, NX, NY), jnp.float32)
    lower_face = jnp.concatenate([zero_plane, face_value], axis=0)
    upper_face = jnp.concatenate([face_value, zero_plane], axis=0)
    diagonal = electron_temp + lower_face + upper_face + COUPLE * atom_count
    right_side = electron_temp * electron_temp + lateral + COUPLE * TWO_THIRDS * energy
    new_temp = chain_solve(-lower_face, diagonal, -upper_face, right_side)
    flat_temp = jnp.concatenate([new_temp.reshape(-1), jnp.zeros((1,), jnp.float32)])
    atom_temp = flat_temp[atom_cell]
    new_velocity = jnp.where(in_use[None], (1.0 - KICK_RATE) * atom_velocity + jnp.sqrt(2.0 * KICK_RATE * atom_temp)[None] * atom_noise, 0.0)
    return (new_temp, new_velocity)
```

```python
import functools

import jax
import jax.numpy as jnp
from jax import lax
from jax.experimental import pallas as pl
from jax.experimental.pallas import tpu as pltpu
from jax.sharding import PartitionSpec as P

STIFFNESS = 10000.0
LATERAL = 0.1
COUPLE = 0.5
TWO_THIRDS = 2.0 / 3.0
KICK_RATE = 0.2
F32 = jnp.float32
BF16 = jnp.bfloat16
VMEM_LIMIT = 48 * 1024 * 1024


def quotient(value, size):
    if size & (size - 1) == 0:
        return lax.shift_right_logical(value, size.bit_length() - 1)
    return value // size


def iota(shape, dim):
    return lax.broadcasted_iota(jnp.int32, shape, dim)


def split(value, pieces):
    parts = []
    for _ in range(pieces):
        part = value.astype(BF16)
        parts.append(part)
        value = value - part.astype(F32)
    return parts


def merge(left, right):
    g_a, sl_a, rl_a, s_a, r_a = left
    g_b, sl_b, rl_b, s_b, r_b = right
    excess = s_a + sl_b
    source = r_a + rl_b
    inverse = 1.0 / (g_a + g_b + excess)
    to_left = g_a * inverse
    to_right = g_b * inverse
    return (
        g_a * to_right,
        sl_a + to_left * excess,
        rl_a + to_left * source,
        s_b + to_right * excess,
        r_b + to_right * source,
    )


def prefix_step(state, segment):
    gate, sl, rl, s, r = segment
    excess = state[0] + sl
    source = state[1] + rl
    ratio = gate / (gate + excess)
    return (s + ratio * excess, r + ratio * source)


def suffix_step(state, segment):
    gate, sl, rl, s, r = segment
    excess = s + state[0]
    source = r + state[1]
    ratio = gate / (gate + excess)
    return (sl + ratio * excess, rl + ratio * source)


def route_kernel(dims, slabs, rows, velocity, plane, column, count, send, meta):
    planes, width_x, width_y = dims
    bricks, lanes = plane.shape
    lane = iota((bricks, lanes), 1)
    sub_b = iota((bricks, bricks), 0)
    lane_b = iota((bricks, bricks), 1)
    eye = sub_b == lane_b
    owner = quotient(plane[:, 0:1], planes)
    owner_f = jnp.broadcast_to(owner.astype(F32), (bricks, bricks))
    owner_row = jnp.sum(jnp.where(eye, owner_f, 0.0), axis=0, keepdims=True)
    count_row = jnp.broadcast_to(count[...].astype(F32), (bricks, bricks))
    count_col = jnp.sum(jnp.where(eye, count_row, 0.0), axis=1, keepdims=True).astype(jnp.int32)
    ahead = (owner_f == owner_row) & (lane_b < sub_b)
    offset = jnp.sum(jnp.where(ahead, count_row, 0.0), axis=1, keepdims=True).astype(jnp.int32)
    place = owner * (rows * lanes) + offset
    place_f = jnp.broadcast_to(place.astype(F32), (bricks, bricks))
    place_row = jnp.sum(jnp.where(eye, place_f, 0.0), axis=0, keepdims=True).astype(jnp.int32)
    shift = jnp.broadcast_to(place & (lanes - 1), (bricks, lanes))
    meta[...] = jnp.broadcast_to(place * (2 * lanes) + count_col, (bricks, lanes))
    in_use = lane < count_col
    vx, vy, vz = velocity[0], velocity[1], velocity[2]
    kinetic = jnp.where(in_use, 0.5 * (vx * vx + vy * vy + vz * vz), 0.0)
    col = column[...]
    x_cell = quotient(col, width_y)
    y_cell = col - x_cell * width_y
    row = (plane[...] - owner * planes) * width_x + x_cell + 1
    code = jnp.where(in_use, row * width_y + y_cell, 0)
    turned = (lane - shift) & (lanes - 1)
    kinetic = jnp.take_along_axis(kinetic, turned, axis=1)
    code = jnp.take_along_axis(code, turned, axis=1)
    row = quotient(code, width_y)
    y_cell = code - row * width_y
    parts = split(kinetic, 2) + [row.astype(F32).astype(BF16), y_cell.astype(F32).astype(BF16)]
    first = lane >= shift
    zero = jnp.zeros((bricks, lanes), BF16)
    values = jnp.concatenate(
        [
            jnp.concatenate([jnp.where(first, part, zero) for part in parts], axis=1),
            jnp.concatenate([jnp.where(first, zero, part) for part in parts], axis=1),
        ],
        axis=0,
    )
    target = quotient(place_row, lanes)
    slot = iota((slabs * rows, bricks), 0)
    spots = jnp.concatenate([slot == target, slot == target + 1], axis=1)
    moved = jnp.dot(
        jnp.where(spots, 1.0, 0.0).astype(BF16), values, preferred_element_type=F32
    )
    send[:, 0] = (moved[:, :lanes] + moved[:, lanes : 2 * lanes]).reshape(slabs, rows, lanes)
    send[:, 1] = (moved[:, 2 * lanes : 3 * lanes] * width_y + moved[:, 3 * lanes :]).reshape(
        slabs, rows, lanes
    )


def filled_rows(got):
    slabs, _, rows, lanes = got.shape
    codes = got[:, 1]
    heights = iota((slabs, rows, lanes), 1).astype(F32) + 1.0
    return jnp.max(jnp.where(codes > 0.0, heights, 0.0)).astype(jnp.int32)


def decode(code, width_y):
    row = jnp.floor((code + 0.5) * (1.0 / width_y))
    return row, code - row * width_y


def bin_kernel(
    dims, got, temp, below, x_low, x_high, summary, factors, lhs, rhs, totals
):
    planes, width_x, width_y = dims
    slabs, _, rows, lanes = got.shape
    cells = planes * width_x
    one = jnp.ones((), BF16)
    zero = jnp.zeros((), BF16)
    row_id = (iota((cells, lanes), 0) + 1).astype(F32).astype(BF16)
    y_id = iota((width_y, lanes), 0).astype(F32).astype(BF16)
    totals[...] = jnp.zeros(totals.shape, F32)

    def add_rows(turn, carry):
        kinetic = got[:, 0, pl.ds(turn, 1), :].reshape(slabs, lanes)
        code = got[:, 1, pl.ds(turn, 1), :].reshape(slabs, lanes)
        row, y_cell = decode(code, width_y)
        high, low = split(kinetic, 2)
        row = row.astype(BF16)
        y_cell = y_cell.astype(BF16)
        for s in range(slabs):
            here = pl.ds(s * lanes, lanes)
            hit = row_id == row[s : s + 1]
            lhs[pl.ds(0, cells), here] = jnp.where(hit, high[s : s + 1], zero)
            lhs[pl.ds(cells, cells), here] = jnp.where(hit, low[s : s + 1], zero)
            lhs[pl.ds(2 * cells, cells), here] = jnp.where(hit, one, zero)
            rhs[:, here] = jnp.where(y_id == y_cell[s : s + 1], one, zero)
        totals[...] += lax.dot_general(
            lhs[...], rhs[...], (((1,), (1,)), ((), ())), preferred_element_type=F32
        )
        return carry

    lax.fori_loop(0, filled_rows(got), add_rows, 0)

    def plane_terms(z):
        here = temp[z]
        x_minus = jnp.concatenate([x_low[z], here[:-1]], axis=0)
        x_plus = jnp.concatenate([here[1:], x_high[z]], axis=0)
        lateral = LATERAL * (
            x_minus
            + x_plus
            + pltpu.roll(here, 1, 1)
            + pltpu.roll(here, width_y - 1, 1)
            - 4.0 * here
        )
        at = z * width_x
        energy = totals[pl.ds(at, width_x), :] + totals[pl.ds(cells + at, width_x), :]
        count = totals[pl.ds(2 * cells + at, width_x), :]
        return here + COUPLE * count, here * here + lateral + COUPLE * TWO_THIRDS * energy

    start = temp[0]
    gate = jnp.where(
        lax.axis_index("gz") > 0, STIFFNESS * (0.5 * (start + below[0])), jnp.zeros_like(start)
    )
    excess, source = plane_terms(0)
    left_excess = jnp.zeros_like(start)
    left_source = jnp.zeros_like(start)
    for z in range(planes - 1):
        face = STIFFNESS * (0.5 * (temp[z + 1] + temp[z]))
        inverse = 1.0 / (gate + face + excess)
        to_left = gate * inverse
        to_right = face * inverse
        factors[z, 0] = to_left
        factors[z, 1] = to_right
        factors[z, 2] = source * inverse
        next_excess, next_source = plane_terms(z + 1)
        left_excess = left_excess + to_left * excess
        left_source = left_source + to_left * source
        gate = gate * to_right
        excess = next_excess + to_right * excess
        source = next_source + to_right * source
    for i, value in enumerate((gate, left_excess, left_source, excess, source)):
        summary[i] = value


def load_five(ref):
    return tuple(ref[i] for i in range(5))


def merge_kernel(level, last, mine, other, total):
    upper = (lax.axis_index("gz") & (1 << level)) != 0
    own = load_five(mine)
    came = load_five(other)
    low = tuple(jnp.where(upper, b, a) for a, b in zip(own, came))
    high = tuple(jnp.where(upper, a, b) for a, b in zip(own, came))
    joined = merge(low, high)
    if not last:
        for i in range(5):
            total[i] = joined[i]
        return
    in_upper = (lax.axis_index("gz") & (1 << (level + 1))) != 0
    end = jnp.zeros_like(joined[0])
    closed = suffix_step((end, end), joined)
    total[0] = jnp.where(in_upper, closed[0], joined[3])
    total[1] = jnp.where(in_upper, closed[1], joined[4])


def look_kernel(dims, levels, got, factors, *refs):
    planes, width_x, width_y = dims
    others = refs[1:levels]
    own = load_five(refs[0])
    far = refs[levels]
    new_temp, reply, rhs, table = refs[levels + 1 :]
    slabs, _, rows, lanes = got.shape
    cells = planes * width_x
    index = lax.axis_index("gz")
    zeros = jnp.zeros_like(own[0])
    top = (index & (1 << (levels - 1))) != 0
    before = (jnp.where(top, far[0], zeros + 1.0), jnp.where(top, far[1], zeros))
    after = (jnp.where(top, zeros, far[0]), jnp.where(top, zeros, far[1]))
    for level in range(levels - 2, -1, -1):
        upper = (index & (1 << level)) != 0
        segment = load_five(others[level])
        with_before = prefix_step(before, segment)
        with_after = suffix_step(after, segment)
        before = tuple(jnp.where(upper, a, b) for a, b in zip(with_before, before))
        after = tuple(jnp.where(upper, b, a) for a, b in zip(with_after, after))
    through = prefix_step(before, own)
    value = (through[1] + after[1]) / (through[0] + after[0])
    edge = (before[1] + own[2] + own[0] * value) / (before[0] + own[1] + own[0])

    def put(z, value):
        new_temp[z] = value
        high, low = split(value, 2)
        table[pl.ds(z * width_x, width_x), pl.ds(0, width_y)] = high
        table[pl.ds(z * width_x, width_x), pl.ds(width_y, width_y)] = low

    put(planes - 1, value)
    for z in range(planes - 2, -1, -1):
        value = factors[z, 2] + factors[z, 0] * edge + factors[z, 1] * value
        put(z, value)

    one = jnp.ones((), BF16)
    zero = jnp.zeros((), BF16)
    row_id = (iota((cells, lanes), 0) + 1).astype(F32)
    y_id = iota((width_y, lanes), 0).astype(F32).astype(BF16)
    reply[...] = jnp.zeros(reply.shape, F32)

    def find_rows(turn, carry):
        code = got[:, 1, pl.ds(turn, 1), :].reshape(slabs, lanes)
        row, y_cell = decode(code, width_y)
        y_cell = y_cell.astype(BF16)
        for s in range(slabs):
            here = pl.ds(s * lanes, lanes)
            hot = jnp.where(y_id == y_cell[s : s + 1], one, zero)
            rhs[pl.ds(0, width_y), here] = hot
            rhs[pl.ds(width_y, width_y), here] = hot
        picked = jnp.dot(table[...], rhs[...], preferred_element_type=F32)
        for s in range(slabs):
            chosen = jnp.where(row_id == row[s : s + 1], picked[:, s * lanes : (s + 1) * lanes], 0.0)
            reply[s, pl.ds(turn, 1), :] = jnp.sum(chosen, axis=0, keepdims=True)
        return carry

    lax.fori_loop(0, filled_rows(got), find_rows, 0)


def kick_kernel(returned, meta, velocity, noise, out):
    bricks, lanes = meta.shape
    slots = returned.shape[0]
    packed = meta[...]
    lane = iota((bricks, lanes), 1)
    place = quotient(packed, 2 * lanes)
    in_use = lane < packed - place * (2 * lanes)
    shift = place & (lanes - 1)
    target = quotient(place[:, 0:1], lanes)
    slot = iota((bricks, slots), 1)
    spots = jnp.concatenate([slot == target, slot == target + 1], axis=0)
    values = jnp.concatenate(split(returned[...], 3), axis=1)
    moved = jnp.dot(
        jnp.where(spots, 1.0, 0.0).astype(BF16), values, preferred_element_type=F32
    )
    moved = moved[:, :lanes] + moved[:, lanes : 2 * lanes] + moved[:, 2 * lanes :]
    found = jnp.where(lane >= shift, moved[:bricks], moved[bricks:])
    found = jnp.take_along_axis(found, (lane + shift) & (lanes - 1), axis=1)
    root = jnp.sqrt(2.0 * KICK_RATE * found)
    for i in range(3):
        out[i] = jnp.where(in_use, (1.0 - KICK_RATE) * velocity[i] + root * noise[i], 0.0)


def call(kernel, out_shape, scratch=()):
    return pl.pallas_call(
        kernel,
        out_shape=out_shape,
        scratch_shapes=list(scratch),
        compiler_params=pltpu.CompilerParams(vmem_limit_bytes=VMEM_LIMIT),
    )


def struct(*shape, dtype=F32):
    return jax.ShapeDtypeStruct(shape, dtype)


def body(atom_velocity, atom_noise, atom_plane, atom_column, brick_count, electron_temp):
    dims = electron_temp.shape
    planes, width_x, width_y = dims
    cells = planes * width_x
    slabs = lax.axis_size("gz")
    groups = lax.axis_size("gx")
    levels = slabs.bit_length() - 1
    assert slabs == 1 << levels and levels > 0
    bricks, lanes = atom_plane.shape
    rows = 2 * bricks // slabs

    send, meta = call(
        functools.partial(route_kernel, dims, slabs, rows),
        (struct(slabs, 2, rows, lanes), struct(bricks, lanes, dtype=jnp.int32)),
    )(atom_velocity, atom_plane, atom_column, brick_count.reshape(1, bricks))
    got = lax.all_to_all(send, "gz", split_axis=0, concat_axis=0, tiled=True)
    below = lax.ppermute(electron_temp[-1:], "gz", [(i, i + 1) for i in range(slabs - 1)])
    x_low = lax.ppermute(
        electron_temp[:, -1:], "gx", [(i, (i + 1) % groups) for i in range(groups)]
    )
    x_high = lax.ppermute(
        electron_temp[:, :1], "gx", [((i + 1) % groups, i) for i in range(groups)]
    )
    total, factors = call(
        functools.partial(bin_kernel, dims),
        (struct(5, width_x, width_y), struct(planes - 1, 3, width_x, width_y)),
        (
            pltpu.VMEM((3 * cells, slabs * lanes), BF16),
            pltpu.VMEM((width_y, slabs * lanes), BF16),
            pltpu.VMEM((3 * cells, width_y), F32),
        ),
    )(got, electron_temp, below, x_low, x_high)
    pieces = [total]
    for level in range(levels):
        other = lax.ppermute(total, "gz", [(i, i ^ (1 << level)) for i in range(slabs)])
        pieces.append(other)
        if level < levels - 1:
            last = level == levels - 2
            total = call(
                functools.partial(merge_kernel, level, last),
                struct(2 if last else 5, width_x, width_y),
            )(total, other)
    new_temp, reply = call(
        functools.partial(look_kernel, dims, levels),
        (struct(*dims), struct(slabs, rows, lanes)),
        (
            pltpu.VMEM((2 * width_y, slabs * lanes), BF16),
            pltpu.VMEM((cells, 2 * width_y), BF16),
        ),
    )(got, factors, *pieces)
    returned = lax.all_to_all(reply, "gz", split_axis=0, concat_axis=0, tiled=True)
    new_velocity = call(kick_kernel, struct(*atom_velocity.shape))(
        returned.reshape(slabs * rows, lanes), meta, atom_velocity, atom_noise
    )
    return (new_temp, new_velocity)


def solution(mesh):
    placed = (
        P(None, ("gz", "gx"), None),
        P(None, ("gz", "gx"), None),
        P(("gz", "gx"), None),
        P(("gz", "gx"), None),
        P(("gz", "gx")),
        P("gz", "gx", None),
    )
    return jax.shard_map(
        body,
        mesh=mesh,
        in_specs=placed,
        out_specs=(P("gz", "gx", None), P(None, ("gz", "gx"), None)),
        check_vma=False,
    )
```

```python
import functools

import jax
import jax.numpy as jnp
from jax import lax
from jax.experimental import pallas as pl
from jax.experimental.pallas import tpu as pltpu
from jax.sharding import PartitionSpec as P

STIFFNESS = 10000.0
LATERAL = 0.1
COUPLE = 0.5
TWO_THIRDS = 2.0 / 3.0
KICK_RATE = 0.2
F32 = jnp.float32
BF16 = jnp.bfloat16
F8 = jnp.float8_e4m3fn
SCALE = 8.0
STEP = 16.0
PIECES = 3
PARTS = 4
ROUTE_LIMIT = 63 * 1024 * 1024
VMEM_LIMIT = 48 * 1024 * 1024


def quotient(value, size):
    if size & (size - 1) == 0:
        return lax.shift_right_logical(value, size.bit_length() - 1)
    return value // size


def iota(shape, dim):
    return lax.broadcasted_iota(jnp.int32, shape, dim)


def split(value, pieces):
    parts = []
    for _ in range(pieces):
        part = value.astype(BF16)
        parts.append(part)
        value = value - part.astype(F32)
    return parts


def split_small(value):
    value = value * SCALE
    parts = []
    for _ in range(PIECES):
        part = value.astype(F8)
        parts.append(part)
        value = (value - part.astype(F32)) * STEP
    return parts


def join_small(parts):
    total = parts[-1]
    for part in parts[-2::-1]:
        total = part + total * (1.0 / STEP)
    return total * (1.0 / SCALE)


def merge(left, right):
    g_a, sl_a, rl_a, s_a, r_a = left
    g_b, sl_b, rl_b, s_b, r_b = right
    excess = s_a + sl_b
    source = r_a + rl_b
    inverse = 1.0 / (g_a + g_b + excess)
    to_left = g_a * inverse
    to_right = g_b * inverse
    return (
        g_a * to_right,
        sl_a + to_left * excess,
        rl_a + to_left * source,
        s_b + to_right * excess,
        r_b + to_right * source,
    )


def prefix_step(state, segment):
    gate, sl, rl, s, r = segment
    excess = state[0] + sl
    source = state[1] + rl
    ratio = gate / (gate + excess)
    return (s + ratio * excess, r + ratio * source)


def suffix_step(state, segment):
    gate, sl, rl, s, r = segment
    excess = s + state[0]
    source = r + state[1]
    ratio = gate / (gate + excess)
    return (sl + ratio * excess, rl + ratio * source)


def route_kernel(
    dims, slabs, rows, parts, count, velocity_hbm, plane_hbm, column_hbm, send, meta, starts,
    velocity, plane, column, arrived,
):
    copies = [
        pltpu.make_async_copy(source, target, arrived.at[i])
        for i, (source, target) in enumerate(
            ((plane_hbm, plane), (column_hbm, column), (velocity_hbm, velocity))
        )
    ]
    for copy in copies:
        copy.start()
    planes, width_x, width_y = dims
    bricks, lanes = plane.shape
    part_rows = planes * width_x // parts
    lane = iota((bricks, lanes), 1)
    sub_b = iota((bricks, bricks), 0)
    lane_b = iota((bricks, bricks), 1)
    eye = sub_b == lane_b
    count_row = jnp.broadcast_to(count[...].astype(F32), (bricks, bricks))
    count_col = jnp.sum(jnp.where(eye, count_row, 0.0), axis=1, keepdims=True).astype(jnp.int32)
    in_use = lane < count_col
    sub_l = iota((lanes, lanes), 0)
    lane_l = iota((lanes, lanes), 1)
    prefix = jnp.concatenate(
        [jnp.where(sub_l <= lane_l, 1.0, 0.0), jnp.ones((lanes, lanes), F32)], axis=1
    ).astype(BF16)
    copies[0].wait()
    owner = quotient(plane[:, 0:1], planes)
    owner_f = jnp.broadcast_to(owner.astype(F32), (bricks, bricks))
    owner_row = jnp.sum(jnp.where(eye, owner_f, 0.0), axis=0, keepdims=True)
    same = owner_f == owner_row
    ahead = same & (lane_b < sub_b)
    peers = jnp.where(jnp.concatenate([same, ahead], axis=1), 1.0, 0.0).astype(BF16)
    copies[1].wait()
    col = column[...]
    x_cell = quotient(col, width_y)
    y_cell = col - x_cell * width_y
    row = (plane[...] - owner * planes) * width_x + x_cell
    code = jnp.where(in_use, (row + 1) * width_y + y_cell, 0)
    part = jnp.where(in_use, quotient(row, part_rows), parts)
    inside = [jnp.where(part == c, 1.0, 0.0).astype(BF16) for c in range(parts)]
    sums = jnp.dot(jnp.concatenate(inside, axis=0), prefix, preferred_element_type=F32)
    ranks = [sums[c * bricks : (c + 1) * bricks, :lanes] for c in range(parts)]
    sizes = [sums[c * bricks : (c + 1) * bricks, lanes:] for c in range(parts)]
    earlier = [jnp.zeros_like(sizes[0])]
    for c in range(parts - 1):
        earlier.append(earlier[-1] + sizes[c])
    offsets = jnp.dot(
        peers,
        jnp.concatenate(
            [jnp.concatenate(earlier, axis=1), jnp.concatenate(sizes, axis=1)], axis=0
        ).astype(BF16),
        preferred_element_type=F32,
    )
    copies[2].wait()
    vx, vy, vz = velocity[0], velocity[1], velocity[2]
    kinetic = 0.5 * (vx * vx + vy * vy + vz * vz)
    zero = jnp.zeros((bricks, lanes), BF16)
    slot = iota((slabs * rows, bricks), 0)
    values = []
    spots = []
    place = jnp.full((bricks, lanes), -1, jnp.int32)
    for c in range(parts):
        start = offsets[:, c * lanes : (c + 1) * lanes].astype(jnp.int32) + owner * (rows * lanes)
        starts[c] = start
        place = jnp.where(
            part == c, (start + ranks[c].astype(jnp.int32) - 1) * parts + c, place
        )
        shift = start & (lanes - 1)
        wanted = (lane - shift) & (lanes - 1)
        wanted_f = wanted.astype(F32)
        found = jnp.zeros((bricks, lanes), jnp.int32)
        step = lanes // 2
        while step:
            at = jnp.take_along_axis(ranks[c], found + (step - 1), axis=1)
            found = jnp.where(at <= wanted_f, found + step, found)
            step //= 2
        valid = wanted_f < sizes[c]
        kin = jnp.where(valid, jnp.take_along_axis(kinetic, found, axis=1), 0.0)
        cell = jnp.where(valid, jnp.take_along_axis(code, found, axis=1), 0)
        cell_row = quotient(cell, width_y)
        cell_y = cell - cell_row * width_y
        pieces = split(kin, 2) + [cell_row.astype(F32).astype(BF16), cell_y.astype(F32).astype(BF16)]
        first = lane >= shift
        values.append(jnp.concatenate([jnp.where(first, p, zero) for p in pieces], axis=1))
        values.append(jnp.concatenate([jnp.where(first, zero, p) for p in pieces], axis=1))
        start_row = jnp.sum(
            jnp.where(eye, start.astype(F32), 0.0), axis=0, keepdims=True
        ).astype(jnp.int32)
        target = quotient(start_row, lanes)
        spots.append(slot == target)
        spots.append(slot == target + 1)
    meta[...] = place
    moved = jnp.dot(
        jnp.where(jnp.concatenate(spots, axis=1), 1.0, 0.0).astype(BF16),
        jnp.concatenate(values, axis=0),
        preferred_element_type=F32,
    )
    send[:, 0] = (moved[:, :lanes] + moved[:, lanes : 2 * lanes]).reshape(slabs, rows, lanes)
    send[:, 1] = (moved[:, 2 * lanes : 3 * lanes] * width_y + moved[:, 3 * lanes :]).reshape(
        slabs, rows, lanes
    )


def decode(code, width_y):
    row = jnp.floor((code + 0.5) * (1.0 / width_y))
    return row, code - row * width_y


def find_runs(dims, parts, got, runs_vmem, runs, arrived):
    planes, width_x, width_y = dims
    slabs, _, rows, lanes = got.shape
    part_rows = planes * width_x // parts
    codes = got[:, 1]
    lane = iota((slabs, lanes), 1)
    table = jnp.zeros((slabs, lanes), jnp.int32)
    for c in range(1, parts + 1):
        limit = float((c * part_rows + 1) * width_y)
        below = jnp.where((codes > 0.0) & (codes < limit), 1.0, 0.0)
        ends = jnp.sum(jnp.sum(below, axis=1), axis=1, keepdims=True).astype(jnp.int32)
        table = jnp.where(lane == c, ends, table)
    runs_vmem[...] = table
    copy = pltpu.make_async_copy(runs_vmem, runs, arrived.at[0])
    copy.start()
    copy.wait()


def run_bounds(runs, parts, slabs, lanes):
    ends = [[runs[s, c] for s in range(slabs)] for c in range(parts + 1)]
    first = [[quotient(end, lanes) for end in ends[c]] for c in range(parts)]
    last = [[quotient(end + (lanes - 1), lanes) for end in ends[c + 1]] for c in range(parts)]
    longest = last[0][0] - first[0][0]
    for c in range(parts):
        for s in range(slabs):
            longest = jnp.maximum(longest, last[c][s] - first[c][s])
    return first, last, longest


def run_row(got, field, s, spot, last):
    rows = got.shape[2]
    loaded = got[s, field, pl.ds(jnp.minimum(spot, rows - 1), 1), :]
    return jnp.where(spot < last, loaded, 0.0)


def bin_kernel(
    dims, parts, got, temp, below, x_low, x_high, summary, factors,
    lhs, rhs, totals, runs_vmem, runs, arrived,
):
    planes, width_x, width_y = dims
    slabs, _, rows, lanes = got.shape
    part_rows = planes * width_x // parts
    one = jnp.ones((), F8)
    zero = jnp.zeros((), F8)
    y_id = iota((width_y, lanes), 0).astype(F32).astype(BF16)
    totals[...] = jnp.zeros(totals.shape, F32)
    find_runs(dims, parts, got, runs_vmem, runs, arrived)
    first, last, longest = run_bounds(runs, parts, slabs, lanes)

    def add_rows(turn, carry):
        for c in range(parts):
            row_id = (iota((part_rows, lanes), 0) + (c * part_rows + 1)).astype(F32).astype(BF16)
            for s in range(slabs):
                spot = first[c][s] + turn
                pieces = split_small(run_row(got, 0, s, spot, last[c][s]))
                row, y_cell = decode(run_row(got, 1, s, spot, last[c][s]), width_y)
                here = pl.ds(s * lanes, lanes)
                hit = row_id == row.astype(BF16)
                for i, piece in enumerate(pieces):
                    lhs[c, pl.ds(i * part_rows, part_rows), here] = jnp.where(hit, piece, zero)
                lhs[c, pl.ds(PIECES * part_rows, part_rows), here] = jnp.where(hit, one, zero)
                rhs[c, :, here] = jnp.where(y_id == y_cell.astype(BF16), one, zero)
        for c in range(parts):
            totals[c] += lax.dot_general(
                lhs[c], rhs[c], (((1,), (1,)), ((), ())), preferred_element_type=F32
            )
        return carry

    lax.fori_loop(0, longest, add_rows, 0)

    def plane_terms(z):
        here = temp[z]
        x_minus = jnp.concatenate([x_low[z], here[:-1]], axis=0)
        x_plus = jnp.concatenate([here[1:], x_high[z]], axis=0)
        lateral = LATERAL * (
            x_minus
            + x_plus
            + pltpu.roll(here, 1, 1)
            + pltpu.roll(here, width_y - 1, 1)
            - 4.0 * here
        )
        c, at = divmod(z * width_x, part_rows)
        energy = join_small(
            [totals[c, pl.ds(i * part_rows + at, width_x), :] for i in range(PIECES)]
        )
        count = totals[c, pl.ds(PIECES * part_rows + at, width_x), :]
        return here + COUPLE * count, here * here + lateral + COUPLE * TWO_THIRDS * energy

    start = temp[0]
    gate = jnp.where(
        lax.axis_index("gz") > 0, STIFFNESS * (0.5 * (start + below[0])), jnp.zeros_like(start)
    )
    excess, source = plane_terms(0)
    left_excess = jnp.zeros_like(start)
    left_source = jnp.zeros_like(start)
    for z in range(planes - 1):
        face = STIFFNESS * (0.5 * (temp[z + 1] + temp[z]))
        inverse = 1.0 / (gate + face + excess)
        to_left = gate * inverse
        to_right = face * inverse
        factors[z, 0] = to_left
        factors[z, 1] = to_right
        factors[z, 2] = source * inverse
        next_excess, next_source = plane_terms(z + 1)
        left_excess = left_excess + to_left * excess
        left_source = left_source + to_left * source
        gate = gate * to_right
        excess = next_excess + to_right * excess
        source = next_source + to_right * source
    for i, value in enumerate((gate, left_excess, left_source, excess, source)):
        summary[i] = value


def load_five(ref):
    return tuple(ref[i] for i in range(5))


def merge_kernel(level, last, mine, other, total):
    upper = (lax.axis_index("gz") & (1 << level)) != 0
    own = load_five(mine)
    came = load_five(other)
    low = tuple(jnp.where(upper, b, a) for a, b in zip(own, came))
    high = tuple(jnp.where(upper, a, b) for a, b in zip(own, came))
    joined = merge(low, high)
    if not last:
        for i in range(5):
            total[i] = joined[i]
        return
    in_upper = (lax.axis_index("gz") & (1 << (level + 1))) != 0
    end = jnp.zeros_like(joined[0])
    closed = suffix_step((end, end), joined)
    total[0] = jnp.where(in_upper, closed[0], joined[3])
    total[1] = jnp.where(in_upper, closed[1], joined[4])


def look_kernel(dims, parts, levels, got, factors, *refs):
    planes, width_x, width_y = dims
    others = refs[1:levels]
    own = load_five(refs[0])
    far = refs[levels]
    new_temp, reply, rhs, table, runs_vmem, runs, arrived = refs[levels + 1 :]
    slabs, _, rows, lanes = got.shape
    part_rows = planes * width_x // parts
    find_runs(dims, parts, got, runs_vmem, runs, arrived)
    index = lax.axis_index("gz")
    zeros = jnp.zeros_like(own[0])
    top = (index & (1 << (levels - 1))) != 0
    before = (jnp.where(top, far[0], zeros + 1.0), jnp.where(top, far[1], zeros))
    after = (jnp.where(top, zeros, far[0]), jnp.where(top, zeros, far[1]))
    for level in range(levels - 2, -1, -1):
        upper = (index & (1 << level)) != 0
        segment = load_five(others[level])
        with_before = prefix_step(before, segment)
        with_after = suffix_step(after, segment)
        before = tuple(jnp.where(upper, a, b) for a, b in zip(with_before, before))
        after = tuple(jnp.where(upper, b, a) for a, b in zip(with_after, after))
    through = prefix_step(before, own)
    value = (through[1] + after[1]) / (through[0] + after[0])
    edge = (before[1] + own[2] + own[0] * value) / (before[0] + own[1] + own[0])

    def put(z, value):
        new_temp[z] = value

    put(planes - 1, value)
    for z in range(planes - 2, -1, -1):
        value = factors[z, 2] + factors[z, 0] * edge + factors[z, 1] * value
        put(z, value)

    for c in range(parts):
        depth = planes // parts
        block = new_temp[pl.ds(c * depth, depth)].reshape(part_rows, width_y)
        for i, piece in enumerate(split_small(block)):
            table[c, pl.ds(i * part_rows, part_rows), :] = piece

    one = jnp.ones((), F8)
    zero = jnp.zeros((), F8)
    y_id = iota((width_y, lanes), 0).astype(F32).astype(BF16)
    reply[...] = jnp.zeros(reply.shape, F32)
    first, last, longest = run_bounds(runs, parts, slabs, lanes)

    def find_rows(turn, carry):
        wanted = []
        for c in range(parts):
            for s in range(slabs):
                row, y_cell = decode(run_row(got, 1, s, first[c][s] + turn, last[c][s]), width_y)
                wanted.append(row)
                rhs[c, :, pl.ds(s * lanes, lanes)] = jnp.where(
                    y_id == y_cell.astype(BF16), one, zero
                )
        for c in range(parts):
            row_id = (iota((part_rows, lanes), 0) + (c * part_rows + 1)).astype(F32)
            picked = jnp.dot(table[c], rhs[c], preferred_element_type=F32)
            picked = join_small(
                [picked[i * part_rows : (i + 1) * part_rows] for i in range(PIECES)]
            )
            for s in range(slabs):
                chosen = jnp.where(
                    row_id == wanted[c * slabs + s], picked[:, s * lanes : (s + 1) * lanes], 0.0
                )
                spot = pl.ds(jnp.minimum(first[c][s] + turn, rows - 1), 1)
                reply[s, spot, :] += jnp.sum(chosen, axis=0, keepdims=True)
        return carry

    lax.fori_loop(0, longest, find_rows, 0)


def kick_kernel(parts, returned, meta, starts, velocity, noise, out):
    bricks, lanes = meta.shape
    slots = returned.shape[0]
    packed = meta[...]
    lane = iota((bricks, lanes), 1)
    in_use = packed >= 0
    place = quotient(jnp.maximum(packed, 0), parts)
    part = jnp.maximum(packed, 0) - place * parts
    slot = iota((bricks, slots), 1)
    spots = []
    for c in range(parts):
        target = quotient(starts[c][:, 0:1], lanes)
        spots.append(slot == target)
        spots.append(slot == target + 1)
    values = jnp.concatenate(split(returned[...], 3), axis=1)
    moved = jnp.dot(
        jnp.where(jnp.concatenate(spots, axis=0), 1.0, 0.0).astype(BF16),
        values,
        preferred_element_type=F32,
    )
    moved = moved[:, :lanes] + moved[:, lanes : 2 * lanes] + moved[:, 2 * lanes :]
    at = place & (lanes - 1)
    temp = jnp.zeros((bricks, lanes), F32)
    for c in range(parts):
        here = moved[2 * c * bricks : (2 * c + 1) * bricks]
        after = moved[(2 * c + 1) * bricks : (2 * c + 2) * bricks]
        whole = jnp.where(lane >= (starts[c] & (lanes - 1)), here, after)
        temp = jnp.where(part == c, jnp.take_along_axis(whole, at, axis=1), temp)
    root = jnp.sqrt(2.0 * KICK_RATE * temp)
    for i in range(3):
        out[i] = jnp.where(in_use, (1.0 - KICK_RATE) * velocity[i] + root * noise[i], 0.0)


def call(kernel, out_shape, scratch=(), spaces=None, limit=VMEM_LIMIT):
    extra = {} if spaces is None else {"in_specs": [pl.BlockSpec(memory_space=m) for m in spaces]}
    return pl.pallas_call(
        kernel,
        out_shape=out_shape,
        **extra,
        scratch_shapes=list(scratch),
        compiler_params=pltpu.CompilerParams(vmem_limit_bytes=limit),
    )


def struct(*shape, dtype=F32):
    return jax.ShapeDtypeStruct(shape, dtype)


def body(atom_velocity, atom_noise, atom_plane, atom_column, brick_count, electron_temp):
    dims = electron_temp.shape
    planes, width_x, width_y = dims
    cells = planes * width_x
    slabs = lax.axis_size("gz")
    groups = lax.axis_size("gx")
    levels = slabs.bit_length() - 1
    assert slabs == 1 << levels and levels > 0
    bricks, lanes = atom_plane.shape
    rows = 2 * bricks // slabs
    parts = PARTS
    assert planes % parts == 0
    run_scratch = (
        pltpu.VMEM((slabs, lanes), jnp.int32),
        pltpu.SMEM((slabs, lanes), jnp.int32),
        pltpu.SemaphoreType.DMA((1,)),
    )

    send, meta, starts = call(
        functools.partial(route_kernel, dims, slabs, rows, parts),
        (
            struct(slabs, 2, rows, lanes),
            struct(bricks, lanes, dtype=jnp.int32),
            struct(parts, bricks, lanes, dtype=jnp.int32),
        ),
        (
            pltpu.VMEM(atom_velocity.shape, F32),
            pltpu.VMEM(atom_plane.shape, jnp.int32),
            pltpu.VMEM(atom_column.shape, jnp.int32),
            pltpu.SemaphoreType.DMA((3,)),
        ),
        (pltpu.VMEM, pltpu.HBM, pltpu.HBM, pltpu.HBM),
        ROUTE_LIMIT,
    )(brick_count.reshape(1, bricks), atom_velocity, atom_plane, atom_column)
    got = lax.all_to_all(send, "gz", split_axis=0, concat_axis=0, tiled=True)
    below = lax.ppermute(electron_temp[-1:], "gz", [(i, i + 1) for i in range(slabs - 1)])
    x_low = lax.ppermute(
        electron_temp[:, -1:], "gx", [(i, (i + 1) % groups) for i in range(groups)]
    )
    x_high = lax.ppermute(
        electron_temp[:, :1], "gx", [((i + 1) % groups, i) for i in range(groups)]
    )
    total, factors = call(
        functools.partial(bin_kernel, dims, parts),
        (struct(5, width_x, width_y), struct(planes - 1, 3, width_x, width_y)),
        (
            pltpu.VMEM((parts, (PIECES + 1) * cells // parts, slabs * lanes), F8),
            pltpu.VMEM((parts, width_y, slabs * lanes), F8),
            pltpu.VMEM((parts, (PIECES + 1) * cells // parts, width_y), F32),
        )
        + run_scratch,
    )(got, electron_temp, below, x_low, x_high)
    pieces = [total]
    for level in range(levels):
        other = lax.ppermute(total, "gz", [(i, i ^ (1 << level)) for i in range(slabs)])
        pieces.append(other)
        if level < levels - 1:
            last = level == levels - 2
            total = call(
                functools.partial(merge_kernel, level, last),
                struct(2 if last else 5, width_x, width_y),
            )(total, other)
    new_temp, reply = call(
        functools.partial(look_kernel, dims, parts, levels),
        (struct(*dims), struct(slabs, rows, lanes)),
        (
            pltpu.VMEM((parts, width_y, slabs * lanes), F8),
            pltpu.VMEM((parts, PIECES * cells // parts, width_y), F8),
        )
        + run_scratch,
    )(got, factors, *pieces)
    returned = lax.all_to_all(reply, "gz", split_axis=0, concat_axis=0, tiled=True)
    new_velocity = call(functools.partial(kick_kernel, parts), struct(*atom_velocity.shape))(
        returned.reshape(slabs * rows, lanes), meta, starts, atom_velocity, atom_noise
    )
    return (new_temp, new_velocity)


def solution(mesh):
    placed = (
        P(None, ("gz", "gx"), None),
        P(None, ("gz", "gx"), None),
        P(("gz", "gx"), None),
        P(("gz", "gx"), None),
        P(("gz", "gx")),
        P("gz", "gx", None),
    )
    return jax.shard_map(
        body,
        mesh=mesh,
        in_specs=placed,
        out_specs=(P("gz", "gx", None), P(None, ("gz", "gx"), None)),
        check_vma=False,
    )
```

```python
import functools

import jax
import jax.numpy as jnp
from jax import lax
from jax.experimental import pallas as pl
from jax.experimental.pallas import tpu as pltpu
from jax.sharding import PartitionSpec as P

STIFFNESS = 10000.0
LATERAL = 0.1
COUPLE = 0.5
TWO_THIRDS = 2.0 / 3.0
KICK_RATE = 0.2
F32 = jnp.float32
BF16 = jnp.bfloat16
F8 = jnp.float8_e4m3fn
SCALE = 8.0
STEP = 16.0
PIECES = 3
PARTS = 4
ROUTE_LIMIT = 32 * 1024 * 1024
VMEM_LIMIT = 32 * 1024 * 1024
LOOK_COST = pl.CostEstimate(flops=2 * 10**9, bytes_accessed=10**7, transcendentals=0)


def quotient(value, size):
    if size & (size - 1) == 0:
        return lax.shift_right_logical(value, size.bit_length() - 1)
    return value // size


def iota(shape, dim):
    return lax.broadcasted_iota(jnp.int32, shape, dim)


def split(value, pieces):
    parts = []
    for _ in range(pieces):
        part = value.astype(BF16)
        parts.append(part)
        value = value - part.astype(F32)
    return parts


def split_small(value):
    value = value * SCALE
    parts = []
    for _ in range(PIECES):
        part = value.astype(F8)
        parts.append(part)
        value = (value - part.astype(F32)) * STEP
    return parts


def join_small(parts):
    total = parts[-1]
    for part in parts[-2::-1]:
        total = part + total * (1.0 / STEP)
    return total * (1.0 / SCALE)


def merge(left, right):
    g_a, sl_a, rl_a, s_a, r_a = left
    g_b, sl_b, rl_b, s_b, r_b = right
    excess = s_a + sl_b
    source = r_a + rl_b
    inverse = 1.0 / (g_a + g_b + excess)
    to_left = g_a * inverse
    to_right = g_b * inverse
    return (
        g_a * to_right,
        sl_a + to_left * excess,
        rl_a + to_left * source,
        s_b + to_right * excess,
        r_b + to_right * source,
    )


def prefix_step(state, segment):
    gate, sl, rl, s, r = segment
    excess = state[0] + sl
    source = state[1] + rl
    ratio = gate / (gate + excess)
    return (s + ratio * excess, r + ratio * source)


def suffix_step(state, segment):
    gate, sl, rl, s, r = segment
    excess = s + state[0]
    source = r + state[1]
    ratio = gate / (gate + excess)
    return (sl + ratio * excess, rl + ratio * source)


def route_kernel(
    dims, slabs, rows, parts, count_hbm, velocity_hbm, plane_hbm, column_hbm, send, meta, starts,
    velocity, plane, column, count, arrived,
):
    copies = [
        pltpu.make_async_copy(source, target, arrived.at[i])
        for i, (source, target) in enumerate(
            (
                (count_hbm, count),
                (plane_hbm, plane),
                (column_hbm, column),
                (velocity_hbm, velocity),
            )
        )
    ]
    for copy in copies:
        copy.start()
    planes, width_x, width_y = dims
    bricks, lanes = plane.shape
    part_rows = planes * width_x // parts
    lane = iota((bricks, lanes), 1)
    sub_b = iota((bricks, bricks), 0)
    lane_b = iota((bricks, bricks), 1)
    eye = sub_b == lane_b
    sub_l = iota((lanes, lanes), 0)
    lane_l = iota((lanes, lanes), 1)
    prefix = jnp.concatenate(
        [jnp.where(sub_l <= lane_l, 1.0, 0.0), jnp.ones((lanes, lanes), F32)], axis=1
    ).astype(BF16)
    copies[0].wait()
    count_row = jnp.broadcast_to(count[...].astype(F32), (bricks, bricks))
    count_col = jnp.sum(jnp.where(eye, count_row, 0.0), axis=1, keepdims=True).astype(jnp.int32)
    in_use = lane < count_col
    copies[1].wait()
    owner = quotient(plane[:, 0:1], planes)
    owner_f = jnp.broadcast_to(owner.astype(F32), (bricks, bricks))
    owner_row = jnp.sum(jnp.where(eye, owner_f, 0.0), axis=0, keepdims=True)
    same = owner_f == owner_row
    ahead = same & (lane_b < sub_b)
    peers = jnp.where(jnp.concatenate([same, ahead], axis=1), 1.0, 0.0).astype(BF16)
    copies[2].wait()
    col = column[...]
    x_cell = quotient(col, width_y)
    y_cell = col - x_cell * width_y
    row = x_cell * planes + plane[...] - owner * planes
    code = jnp.where(in_use, (row + 1) * width_y + y_cell, 0)
    part = jnp.where(in_use, quotient(row, part_rows), parts)
    inside = [jnp.where(part == c, 1.0, 0.0).astype(BF16) for c in range(parts)]
    sums = jnp.dot(jnp.concatenate(inside, axis=0), prefix, preferred_element_type=F32)
    ranks = [sums[c * bricks : (c + 1) * bricks, :lanes] for c in range(parts)]
    sizes = [sums[c * bricks : (c + 1) * bricks, lanes:] for c in range(parts)]
    earlier = [jnp.zeros_like(sizes[0])]
    for c in range(parts - 1):
        earlier.append(earlier[-1] + sizes[c])
    offsets = jnp.dot(
        peers,
        jnp.concatenate(
            [jnp.concatenate(earlier, axis=1), jnp.concatenate(sizes, axis=1)], axis=0
        ).astype(BF16),
        preferred_element_type=F32,
    )
    copies[3].wait()
    vx, vy, vz = velocity[0], velocity[1], velocity[2]
    kinetic = 0.5 * (vx * vx + vy * vy + vz * vz)
    begins = [
        offsets[:, c * lanes : (c + 1) * lanes].astype(jnp.int32) + owner * (rows * lanes)
        for c in range(parts)
    ]
    shifts = [begin & (lanes - 1) for begin in begins]
    packed = ranks[0].astype(jnp.int32)
    run = jnp.zeros((bricks, lanes), jnp.int32)
    base = jnp.zeros((bricks, lanes), F32)
    lane_f = lane.astype(F32)
    for c in range(1, parts):
        packed = packed | (ranks[c].astype(jnp.int32) << (8 * c))
        run = jnp.where(lane_f >= earlier[c], 8 * c, run)
        base = jnp.where(lane_f >= earlier[c], earlier[c], base)
    wanted = lane - base.astype(jnp.int32)
    found = jnp.zeros((bricks, lanes), jnp.int32)
    step = lanes // 2
    while step:
        at = jnp.take_along_axis(packed, found + (step - 1), axis=1)
        at = lax.shift_right_logical(at, run) & 255
        found = jnp.where(at <= wanted, found + step, found)
        step //= 2
    kinetic = jnp.take_along_axis(kinetic, found, axis=1)
    code = jnp.take_along_axis(code, found, axis=1)
    zero = jnp.zeros((bricks, lanes), BF16)
    slot = iota((slabs * rows, bricks), 0).astype(F32).astype(BF16)
    values = []
    spots = []
    place = jnp.full((bricks, lanes), -1, jnp.int32)
    table = jnp.zeros((bricks, lanes), jnp.int32)
    for c in range(parts):
        table = jnp.where(lane == c, begins[c], table)
        place = jnp.where(
            part == c, (begins[c] + ranks[c].astype(jnp.int32) - 1) * parts + c, place
        )
        turn = (lane - shifts[c]) & (lanes - 1)
        valid = turn.astype(F32) < sizes[c]
        turn = (turn + earlier[c].astype(jnp.int32)) & (lanes - 1)
        kin = jnp.where(valid, jnp.take_along_axis(kinetic, turn, axis=1), 0.0)
        cell = jnp.where(valid, jnp.take_along_axis(code, turn, axis=1), 0)
        cell_row = quotient(cell, width_y)
        cell_y = cell - cell_row * width_y
        pieces = split(kin, 2) + [cell_row.astype(F32).astype(BF16), cell_y.astype(F32).astype(BF16)]
        first = lane >= shifts[c]
        values.append(jnp.concatenate([jnp.where(first, p, zero) for p in pieces], axis=1))
        values.append(jnp.concatenate([jnp.where(first, zero, p) for p in pieces], axis=1))
        begin_row = jnp.sum(
            jnp.where(eye, begins[c].astype(F32), 0.0), axis=0, keepdims=True
        ).astype(jnp.int32)
        target = quotient(begin_row, lanes).astype(F32)
        spots.append(slot == target.astype(BF16))
        spots.append(slot == (target + 1.0).astype(BF16))
    starts[...] = table
    meta[...] = place
    one = jnp.ones((), BF16)
    moved = jnp.dot(
        jnp.concatenate([jnp.where(spot, one, jnp.zeros((), BF16)) for spot in spots], axis=1),
        jnp.concatenate(values, axis=0),
        preferred_element_type=F32,
    )
    send[:, 0] = (moved[:, :lanes] + moved[:, lanes : 2 * lanes]).reshape(slabs, rows, lanes)
    send[:, 1] = (moved[:, 2 * lanes : 3 * lanes] * width_y + moved[:, 3 * lanes :]).reshape(
        slabs, rows, lanes
    )


def decode(code, width_y):
    row = jnp.floor((code + 0.5) * (1.0 / width_y))
    return row, code - row * width_y


def find_runs(dims, parts, got, runs_vmem):
    planes, width_x, width_y = dims
    slabs, _, rows, lanes = got.shape
    part_rows = planes * width_x // parts
    codes = got[:, 1]
    codes = jnp.where(codes > 0.0, codes, float((parts * part_rows + 1) * width_y + 1))
    longest = jnp.zeros((slabs, lanes), F32)
    first = jnp.zeros((slabs, lanes), F32)
    table = jnp.zeros((slabs, lanes), F32)
    lane = iota((slabs, lanes), 1)
    for c in range(parts):
        limit = float(((c + 1) * part_rows + 1) * width_y)
        last = jnp.sum(jnp.where(codes < limit, 1.0, 0.0), axis=1)
        longest = jnp.maximum(longest, last - first)
        table = jnp.where(lane == 2 * c, pltpu.roll(first, 2 * c, 1) if c else first, table)
        table = jnp.where(lane == 2 * c + 1, pltpu.roll(last, 2 * c + 1, 1), table)
        first = pltpu.roll(last, 1, 1)
    longest = jnp.max(jnp.where(lane == 0, longest, 0.0), keepdims=True)
    runs_vmem[...] = jnp.where(lane == 2 * parts, longest, table).astype(jnp.int32)


def run_row(got, field, s, spot, last):
    rows = got.shape[2]
    loaded = got[s, field, pl.ds(jnp.minimum(spot, rows - 1), 1), :]
    return jnp.where(spot < last, loaded, 0.0)


def bin_kernel(dims, parts, levels, got, totals, codes, runs_vmem, lhs, rhs, runs, arrived):
    planes, width_x, width_y = dims
    slabs, _, rows, lanes = got.shape
    part_rows = planes * width_x // parts
    find_runs(dims, parts, got, runs_vmem)
    copy = pltpu.make_async_copy(runs_vmem, runs, arrived.at[0])
    copy.start()
    one = jnp.ones((), F8)
    zero = jnp.zeros((), F8)
    y_id = iota((width_y, lanes), 0).astype(F32).astype(BF16)
    totals[...] = jnp.zeros(totals.shape, F32)
    copy.wait()
    longest = runs[0, 2 * parts]

    def add_rows(turn, carry):
        for c in range(parts):
            row_id = (iota((part_rows, lanes), 0) + (c * part_rows + 1)).astype(F32).astype(BF16)
            for s in range(slabs):
                spot = runs[s, 2 * c] + turn
                last = runs[s, 2 * c + 1]
                pieces = split_small(run_row(got, 0, s, spot, last))
                code = run_row(got, 1, s, spot, last)
                codes[turn * parts + c, pl.ds(s, 1), :] = code
                row, y_cell = decode(code, width_y)
                here = pl.ds(s * lanes, lanes)
                hit = row_id == row.astype(BF16)
                for i, piece in enumerate(pieces):
                    lhs[c, pl.ds(i * part_rows, part_rows), here] = jnp.where(hit, piece, zero)
                lhs[c, pl.ds(PIECES * part_rows, part_rows), here] = jnp.where(hit, one, zero)
                rhs[c, :, here] = jnp.where(y_id == y_cell.astype(BF16), one, zero)
        for c in range(parts):
            added = lax.dot_general(
                lhs[c], rhs[c], (((1,), (1,)), ((), ())), preferred_element_type=F32
            )
            for i in range(PIECES + 1):
                for h in range(width_y // lanes):
                    totals[i, h, pl.ds(c * part_rows, part_rows), :] += added[
                        i * part_rows : (i + 1) * part_rows, h * lanes : (h + 1) * lanes
                    ]
        return carry

    lax.fori_loop(0, longest, add_rows, 0)
    for i in range((levels - 1) * parts):
        codes[longest * parts + i] = jnp.zeros((slabs, lanes), F32)


def solve_kernel(dims, totals, temp, below, x_low, x_high, summary, factors):
    planes, width_x, width_y = dims
    lanes = totals.shape[3]

    def plane_terms(z):
        here = temp[z]
        x_minus = jnp.concatenate([x_low[z], here[:-1]], axis=0)
        x_plus = jnp.concatenate([here[1:], x_high[z]], axis=0)
        lateral = LATERAL * (
            x_minus
            + x_plus
            + pltpu.roll(here, 1, 1)
            + pltpu.roll(here, width_y - 1, 1)
            - 4.0 * here
        )
        at = pl.ds(z, width_x, stride=planes)
        sums = [
            jnp.concatenate([totals[i, h, at, :] for h in range(width_y // lanes)], axis=1)
            for i in range(PIECES + 1)
        ]
        energy = join_small(sums[:PIECES])
        count = sums[PIECES]
        return here + COUPLE * count, here * here + lateral + COUPLE * TWO_THIRDS * energy

    start = temp[0]
    gate = jnp.where(
        lax.axis_index("gz") > 0, STIFFNESS * (0.5 * (start + below[0])), jnp.zeros_like(start)
    )
    excess, source = plane_terms(0)
    left_excess = jnp.zeros_like(start)
    left_source = jnp.zeros_like(start)
    for z in range(planes - 1):
        face = STIFFNESS * (0.5 * (temp[z + 1] + temp[z]))
        inverse = 1.0 / (gate + face + excess)
        to_left = gate * inverse
        to_right = face * inverse
        factors[z, 0] = to_left
        factors[z, 1] = to_right
        factors[z, 2] = source * inverse
        next_excess, next_source = plane_terms(z + 1)
        left_excess = left_excess + to_left * excess
        left_source = left_source + to_left * source
        gate = gate * to_right
        excess = next_excess + to_right * excess
        source = next_source + to_right * source
    for i, value in enumerate((gate, left_excess, left_source, excess, source)):
        summary[i] = value


def load_five(ref):
    return tuple(ref[i] for i in range(5))


def merge_kernel(level, last, mine, other, _, total):
    upper = (lax.axis_index("gz") & (1 << level)) != 0
    own = load_five(mine)
    came = load_five(other)
    low = tuple(jnp.where(upper, b, a) for a, b in zip(own, came))
    high = tuple(jnp.where(upper, a, b) for a, b in zip(own, came))
    joined = merge(low, high)
    if not last:
        for i in range(5):
            total[i] = joined[i]
        return
    in_upper = (lax.axis_index("gz") & (1 << (level + 1))) != 0
    end = jnp.zeros_like(joined[0])
    closed = suffix_step((end, end), joined)
    total[0] = jnp.where(in_upper, closed[0], joined[3])
    total[1] = jnp.where(in_upper, closed[1], joined[4])


def table_kernel(dims, parts, factors, table, spread):
    planes, width_x, width_y = dims
    part_rows = planes * width_x // parts
    lanes = spread.shape[3]
    zeros = jnp.zeros((width_x, width_y), F32)
    state = (zeros, zeros, zeros + 1.0)
    for z in range(planes - 1, -1, -1):
        if z < planes - 1:
            to_left, to_right, fixed = factors[z, 0], factors[z, 1], factors[z, 2]
            state = (
                fixed + to_right * state[0],
                to_left + to_right * state[1],
                to_right * state[2],
            )
        for t in range(3):
            for h in range(spread.shape[1]):
                spread[t, h, pl.ds(z, width_x, stride=planes), :] = state[t][
                    :, h * lanes : (h + 1) * lanes
                ]
    for c in range(parts):
        for t in range(3):
            for h in range(spread.shape[1]):
                block = spread[t, h, pl.ds(c * part_rows, part_rows), :]
                for i, piece in enumerate(split_small(block)):
                    at = pl.ds((t * PIECES + i) * part_rows, part_rows)
                    table[c, at, pl.ds(h * lanes, lanes)] = piece


def look_kernel(dims, parts, levels, phase, codes, runs, *refs):
    if phase == 0:
        factors, found, keys, spots, table, spread, rhs = refs
        table_kernel(dims, parts, factors, table, spread)
    else:
        table, _, found, keys, spots, rhs = refs
    planes, width_x, width_y = dims
    _, slabs, lanes = codes.shape
    part_rows = planes * width_x // parts
    halves = width_y // lanes
    one = jnp.ones((), F8)
    zero = jnp.zeros((), F8)
    y_id = iota((width_y, lanes), 0).astype(F32).astype(BF16)
    last_lane = iota((1, lanes), 1) == 2 * parts
    turns = jnp.max(jnp.where(last_lane, runs[0:1, :].astype(F32), 0.0)).astype(jnp.int32)

    def find_rows(step, carry):
        wanted = []
        for c in range(parts):
            block = step * parts + c
            row, y_cell = decode(codes[(step * levels + phase) * parts + c], width_y)
            wanted.append(row)
            hot = y_cell.astype(BF16)
            for s in range(slabs):
                rhs[c, :, pl.ds(s * lanes, lanes)] = jnp.where(
                    y_id == hot[s : s + 1], one, zero
                )
            x_cell = jnp.floor((row - (c * part_rows + 0.5)) * (1.0 / planes))
            half = jnp.floor((y_cell + 0.5) * (1.0 / lanes))
            keys[block] = jnp.where(row > c * part_rows, x_cell * halves + half, -1.0)
            spots[block] = (y_cell - half * lanes).astype(jnp.int32)
        for c in range(parts):
            block = step * parts + c
            row_id = (iota((part_rows, lanes), 0) + (c * part_rows + 1)).astype(F32)
            picked = jnp.dot(table[c], rhs[c], preferred_element_type=F32)
            for s in range(slabs):
                hit = row_id == wanted[c][s : s + 1]
                for t in range(3):
                    pieces = [
                        picked[
                            (t * PIECES + i) * part_rows : (t * PIECES + i + 1) * part_rows,
                            s * lanes : (s + 1) * lanes,
                        ]
                        for i in range(PIECES)
                    ]
                    total = pieces[-1]
                    for piece in pieces[-2::-1]:
                        total = piece + total * (1.0 / STEP)
                    chosen = jnp.sum(jnp.where(hit, total, 0.0), axis=0, keepdims=True)
                    found[t, block, pl.ds(s, 1), :] = chosen * (1.0 / SCALE)
        return carry

    lax.fori_loop(0, quotient_up(turns, levels), find_rows, 0)


def quotient_up(value, size):
    return (value + (size - 1)) // size


def join_kernel(dims, parts, levels, runs_vmem, *refs):
    planes, width_x, width_y = dims
    own = load_five(refs[0])
    others = refs[1:levels]
    far = refs[levels]
    found = refs[levels + 1 : 2 * levels + 1]
    keys = refs[2 * levels + 1 : 3 * levels + 1]
    lane_of = refs[3 * levels + 1 : 4 * levels + 1]
    edges, reply, temps, runs, arrived = refs[4 * levels + 1 :]
    slabs, rows, lanes = reply.shape
    part_x = width_x // parts
    halves = width_y // lanes
    copy = pltpu.make_async_copy(runs_vmem, runs, arrived.at[0])
    copy.start()
    reply[...] = jnp.zeros(reply.shape, F32)
    index = lax.axis_index("gz")
    zeros = jnp.zeros_like(own[0])
    top = (index & (1 << (levels - 1))) != 0
    before = (jnp.where(top, far[0], zeros + 1.0), jnp.where(top, far[1], zeros))
    after = (jnp.where(top, zeros, far[0]), jnp.where(top, zeros, far[1]))
    for level in range(levels - 2, -1, -1):
        upper = (index & (1 << level)) != 0
        segment = load_five(others[level])
        with_before = prefix_step(before, segment)
        with_after = suffix_step(after, segment)
        before = tuple(jnp.where(upper, a, b) for a, b in zip(with_before, before))
        after = tuple(jnp.where(upper, b, a) for a, b in zip(with_after, after))
    through = prefix_step(before, own)
    value = (through[1] + after[1]) / (through[0] + after[0])
    edges[0] = (before[1] + own[2] + own[0] * value) / (before[0] + own[1] + own[0])
    edges[1] = value
    copy.wait()

    def fill_rows(step, carry):
        for phase in range(levels):
            for c in range(parts):
                block = step * parts + c
                key = keys[phase][block]
                lane = lane_of[phase][block]
                ends = [jnp.zeros((slabs, lanes), F32), jnp.zeros((slabs, lanes), F32)]
                for x in range(part_x):
                    for h in range(halves):
                        hit = key == float(x * halves + h)
                        for e in range(2):
                            line = edges[e, pl.ds(c * part_x + x, 1), pl.ds(h * lanes, lanes)]
                            line = jnp.broadcast_to(line, (slabs, lanes))
                            ends[e] = jnp.where(
                                hit, jnp.take_along_axis(line, lane, axis=1), ends[e]
                            )
                temps[phase * parts + c] = (
                    found[phase][0, block]
                    + found[phase][1, block] * ends[0]
                    + found[phase][2, block] * ends[1]
                )
        for phase in range(levels):
            for c in range(parts):
                for s in range(slabs):
                    spot = runs[s, 2 * c] + (step * levels + phase)
                    here = pl.ds(jnp.minimum(spot, rows - 1), 1)
                    reply[s, here, :] += temps[phase * parts + c, pl.ds(s, 1), :]
        return carry

    lax.fori_loop(0, quotient_up(runs[0, 2 * parts], levels), fill_rows, 0)


def fill_kernel(factors, edges, new_temp):
    planes = new_temp.shape[0]
    edge = edges[0]
    value = edges[1]
    new_temp[planes - 1] = value
    for z in range(planes - 2, -1, -1):
        value = factors[z, 2] + factors[z, 0] * edge + factors[z, 1] * value
        new_temp[z] = value


def kick_kernel(parts, returned, meta, starts, velocity, noise, out):
    bricks, lanes = meta.shape
    slots = returned.shape[0]
    packed = meta[...]
    lane = iota((bricks, lanes), 1)
    in_use = packed >= 0
    place = quotient(jnp.maximum(packed, 0), parts)
    part = jnp.maximum(packed, 0) - place * parts
    slot = iota((bricks, slots), 1)
    spots = []
    shifts = []
    for c in range(parts):
        begin = jnp.broadcast_to(starts[:, c : c + 1], (bricks, lanes))
        target = quotient(begin[:, 0:1], lanes)
        shifts.append(begin & (lanes - 1))
        spots.append(slot == target)
        spots.append(slot == target + 1)
    values = jnp.concatenate(split(returned[...], 2), axis=1)
    moved = jnp.dot(
        jnp.where(jnp.concatenate(spots, axis=0), 1.0, 0.0).astype(BF16),
        values,
        preferred_element_type=F32,
    )
    moved = moved[:, :lanes] + moved[:, lanes:]
    at = place & (lanes - 1)
    temp = jnp.zeros((bricks, lanes), F32)
    for c in range(parts):
        here = moved[2 * c * bricks : (2 * c + 1) * bricks]
        after = moved[(2 * c + 1) * bricks : (2 * c + 2) * bricks]
        whole = jnp.where(lane >= shifts[c], here, after)
        temp = jnp.where(part == c, jnp.take_along_axis(whole, at, axis=1), temp)
    root = jnp.sqrt(2.0 * KICK_RATE * temp)
    for i in range(3):
        out[i] = jnp.where(in_use, (1.0 - KICK_RATE) * velocity[i] + root * noise[i], 0.0)


def call(kernel, out_shape, scratch=(), spaces=None, limit=VMEM_LIMIT, cost=None):
    extra = {} if cost is None else {"cost_estimate": cost}
    if spaces is not None:
        extra["in_specs"] = [pl.BlockSpec(memory_space=m) for m in spaces]
    return pl.pallas_call(
        kernel,
        out_shape=out_shape,
        **extra,
        scratch_shapes=list(scratch),
        compiler_params=pltpu.CompilerParams(vmem_limit_bytes=limit),
    )


def struct(*shape, dtype=F32):
    return jax.ShapeDtypeStruct(shape, dtype)


def route_call(dims, slabs, rows, parts, velocity_shape, plane_shape):
    bricks, lanes = plane_shape
    return call(
        functools.partial(route_kernel, dims, slabs, rows, parts),
        (
            struct(slabs, 2, rows, lanes),
            struct(bricks, lanes, dtype=jnp.int32),
            struct(bricks, lanes, dtype=jnp.int32),
        ),
        (
            pltpu.VMEM(velocity_shape, F32),
            pltpu.VMEM(plane_shape, jnp.int32),
            pltpu.VMEM(plane_shape, jnp.int32),
            pltpu.VMEM((1, bricks), jnp.int32),
            pltpu.SemaphoreType.DMA((4,)),
        ),
        (pltpu.HBM,) * 4,
        ROUTE_LIMIT,
    )


def body(atom_velocity, atom_noise, atom_plane, atom_column, brick_count, electron_temp):
    dims = electron_temp.shape
    planes, width_x, width_y = dims
    cells = planes * width_x
    slabs = lax.axis_size("gz")
    groups = lax.axis_size("gx")
    levels = slabs.bit_length() - 1
    assert slabs == 1 << levels and levels > 0
    bricks, lanes = atom_plane.shape
    rows = 2 * bricks // slabs
    parts = PARTS
    assert width_x % parts == 0 and parts <= 4 and lanes <= 128
    run_shape = (slabs, lanes)
    run_scratch = (pltpu.SMEM(run_shape, jnp.int32), pltpu.SemaphoreType.DMA((1,)))

    send, meta, starts = route_call(
        dims, slabs, rows, parts, atom_velocity.shape, atom_plane.shape
    )(
        *(
            pltpu.with_memory_space_constraint(x, pltpu.HBM)
            for x in (brick_count.reshape(1, bricks), atom_velocity, atom_plane, atom_column)
        )
    )
    got = lax.all_to_all(send, "gz", split_axis=0, concat_axis=0, tiled=True)
    below = lax.ppermute(electron_temp[-1:], "gz", [(i, i + 1) for i in range(slabs - 1)])
    x_low = lax.ppermute(
        electron_temp[:, -1:], "gx", [(i, (i + 1) % groups) for i in range(groups)]
    )
    x_high = lax.ppermute(
        electron_temp[:, :1], "gx", [((i + 1) % groups, i) for i in range(groups)]
    )
    totals, codes, runs = call(
        functools.partial(bin_kernel, dims, parts, levels),
        (
            struct(PIECES + 1, width_y // lanes, cells, lanes),
            struct(parts * (rows + levels - 1), slabs, lanes),
            struct(*run_shape, dtype=jnp.int32),
        ),
        (
            pltpu.VMEM((parts, (PIECES + 1) * cells // parts, slabs * lanes), F8),
            pltpu.VMEM((parts, width_y, slabs * lanes), F8),
        )
        + run_scratch,
    )(got)
    total, factors = call(
        functools.partial(solve_kernel, dims),
        (struct(5, width_x, width_y), struct(planes - 1, 3, width_x, width_y)),
    )(totals, electron_temp, below, x_low, x_high)
    blocks = parts * quotient_up(rows, levels)
    found_shapes = (
        struct(3, blocks, slabs, lanes),
        struct(blocks, slabs, lanes),
        struct(blocks, slabs, lanes, dtype=jnp.int32),
    )
    table_shape = (parts, 3 * PIECES * cells // parts, width_y)
    pieces = [total]
    found = []
    for level in range(levels):
        other = lax.ppermute(total, "gz", [(i, i ^ (1 << level)) for i in range(slabs)])
        outs = call(
            functools.partial(look_kernel, dims, parts, levels, level),
            found_shapes + ((struct(*table_shape, dtype=F8),) if level == 0 else ()),
            (() if level else (pltpu.VMEM((3, width_y // lanes, cells, lanes), F32),))
            + (pltpu.VMEM((parts, width_y, slabs * lanes), F8),),
            cost=LOOK_COST,
        )(codes, runs, *((table, total) if level else (factors,)))
        if level == 0:
            table = outs[3]
        found.append(outs[:3])
        pieces.append(other)
        if level < levels - 1:
            last = level == levels - 2
            total = call(
                functools.partial(merge_kernel, level, last),
                struct(2 if last else 5, width_x, width_y),
            )(total, other, outs[1])
    edges, reply = call(
        functools.partial(join_kernel, dims, parts, levels),
        (struct(2, width_x, width_y), struct(slabs, rows, lanes)),
        (pltpu.VMEM((levels * parts, slabs, lanes), F32),) + run_scratch,
    )(runs, *pieces, *(phase[i] for i in range(3) for phase in found))
    new_temp = call(fill_kernel, struct(*dims))(factors, edges)
    returned = lax.all_to_all(reply, "gz", split_axis=0, concat_axis=0, tiled=True)
    new_velocity = call(functools.partial(kick_kernel, parts), struct(*atom_velocity.shape))(
        returned.reshape(slabs * rows, lanes), meta, starts, atom_velocity, atom_noise
    )
    return (new_temp, new_velocity)


def solution(mesh):
    placed = (
        P(None, ("gz", "gx"), None),
        P(None, ("gz", "gx"), None),
        P(("gz", "gx"), None),
        P(("gz", "gx"), None),
        P(("gz", "gx")),
        P("gz", "gx", None),
    )
    return jax.shard_map(
        body,
        mesh=mesh,
        in_specs=placed,
        out_specs=(P("gz", "gx", None), P(None, ("gz", "gx"), None)),
        check_vma=False,
    )
```

```python
import functools

import jax
import jax.numpy as jnp
from jax import lax
from jax.experimental import pallas as pl
from jax.experimental.pallas import tpu as pltpu
from jax.sharding import PartitionSpec as P

STIFFNESS = 10000.0
LATERAL = 0.1
COUPLE = 0.5
TWO_THIRDS = 2.0 / 3.0
KICK_RATE = 0.2
F32 = jnp.float32
BF16 = jnp.bfloat16
F8 = jnp.float8_e4m3fn
SCALE = 8.0
STEP = 16.0
PIECES = 3
PARTS = 4
ROUTE_LIMIT = 32 * 1024 * 1024
VMEM_LIMIT = 32 * 1024 * 1024
LOOK_COST = pl.CostEstimate(flops=2 * 10**9, bytes_accessed=10**7, transcendentals=0)


def quotient(value, size):
    if size & (size - 1) == 0:
        return lax.shift_right_logical(value, size.bit_length() - 1)
    return value // size


def iota(shape, dim):
    return lax.broadcasted_iota(jnp.int32, shape, dim)


def split(value, pieces):
    parts = []
    for _ in range(pieces):
        part = value.astype(BF16)
        parts.append(part)
        value = value - part.astype(F32)
    return parts


def split_small(value):
    value = value * SCALE
    parts = []
    for _ in range(PIECES):
        part = value.astype(F8)
        parts.append(part)
        value = (value - part.astype(F32)) * STEP
    return parts


def join_small(parts):
    total = parts[-1]
    for part in parts[-2::-1]:
        total = part + total * (1.0 / STEP)
    return total * (1.0 / SCALE)


def merge(left, right):
    g_a, sl_a, rl_a, s_a, r_a = left
    g_b, sl_b, rl_b, s_b, r_b = right
    excess = s_a + sl_b
    source = r_a + rl_b
    inverse = 1.0 / (g_a + g_b + excess)
    to_left = g_a * inverse
    to_right = g_b * inverse
    return (
        g_a * to_right,
        sl_a + to_left * excess,
        rl_a + to_left * source,
        s_b + to_right * excess,
        r_b + to_right * source,
    )


def prefix_step(state, segment):
    gate, sl, rl, s, r = segment
    excess = state[0] + sl
    source = state[1] + rl
    ratio = gate / (gate + excess)
    return (s + ratio * excess, r + ratio * source)


def suffix_step(state, segment):
    gate, sl, rl, s, r = segment
    excess = s + state[0]
    source = r + state[1]
    ratio = gate / (gate + excess)
    return (sl + ratio * excess, rl + ratio * source)


def route_kernel(
    dims, slabs, rows, parts, count_hbm, velocity_hbm, plane_hbm, column_hbm, send, meta, starts,
    velocity, plane, column, count, arrived,
):
    copies = [
        pltpu.make_async_copy(source, target, arrived.at[i])
        for i, (source, target) in enumerate(
            (
                (count_hbm, count),
                (plane_hbm, plane),
                (column_hbm, column),
                (velocity_hbm, velocity),
            )
        )
    ]
    for copy in copies:
        copy.start()
    planes, width_x, width_y = dims
    bricks, lanes = plane.shape
    part_rows = planes * width_x // parts
    lane = iota((bricks, lanes), 1)
    sub_b = iota((bricks, bricks), 0)
    lane_b = iota((bricks, bricks), 1)
    eye = sub_b == lane_b
    sub_l = iota((lanes, lanes), 0)
    lane_l = iota((lanes, lanes), 1)
    prefix = jnp.concatenate(
        [jnp.where(sub_l <= lane_l, 1.0, 0.0), jnp.ones((lanes, lanes), F32)], axis=1
    ).astype(BF16)
    copies[0].wait()
    count_row = jnp.broadcast_to(count[...].astype(F32), (bricks, bricks))
    count_col = jnp.sum(jnp.where(eye, count_row, 0.0), axis=1, keepdims=True).astype(jnp.int32)
    in_use = lane < count_col
    copies[1].wait()
    owner = quotient(plane[:, 0:1], planes)
    owner_f = jnp.broadcast_to(owner.astype(F32), (bricks, bricks))
    owner_row = jnp.sum(jnp.where(eye, owner_f, 0.0), axis=0, keepdims=True)
    same = owner_f == owner_row
    ahead = same & (lane_b < sub_b)
    peers = jnp.where(jnp.concatenate([same, ahead], axis=1), 1.0, 0.0).astype(BF16)
    copies[2].wait()
    col = column[...]
    x_cell = quotient(col, width_y)
    y_cell = col - x_cell * width_y
    row = x_cell * planes + plane[...] - owner * planes
    code = jnp.where(in_use, (row + 1) * width_y + y_cell, 0)
    part = jnp.where(in_use, quotient(row, part_rows), parts)
    inside = [jnp.where(part == c, 1.0, 0.0).astype(BF16) for c in range(parts)]
    sums = jnp.dot(jnp.concatenate(inside, axis=0), prefix, preferred_element_type=F32)
    ranks = [sums[c * bricks : (c + 1) * bricks, :lanes] for c in range(parts)]
    sizes = [sums[c * bricks : (c + 1) * bricks, lanes:] for c in range(parts)]
    earlier = [jnp.zeros_like(sizes[0])]
    for c in range(parts - 1):
        earlier.append(earlier[-1] + sizes[c])
    offsets = jnp.dot(
        peers,
        jnp.concatenate(
            [jnp.concatenate(earlier, axis=1), jnp.concatenate(sizes, axis=1)], axis=0
        ).astype(BF16),
        preferred_element_type=F32,
    )
    copies[3].wait()
    vx, vy, vz = velocity[0], velocity[1], velocity[2]
    kinetic = 0.5 * (vx * vx + vy * vy + vz * vz)
    begins = [
        offsets[:, c * lanes : (c + 1) * lanes].astype(jnp.int32) + owner * (rows * lanes)
        for c in range(parts)
    ]
    shifts = [begin & (lanes - 1) for begin in begins]
    packed = ranks[0].astype(jnp.int32)
    run = jnp.zeros((bricks, lanes), jnp.int32)
    base = jnp.zeros((bricks, lanes), F32)
    lane_f = lane.astype(F32)
    for c in range(1, parts):
        packed = packed | (ranks[c].astype(jnp.int32) << (8 * c))
        run = jnp.where(lane_f >= earlier[c], 8 * c, run)
        base = jnp.where(lane_f >= earlier[c], earlier[c], base)
    wanted = lane - base.astype(jnp.int32)
    found = jnp.zeros((bricks, lanes), jnp.int32)
    step = lanes // 2
    while step:
        at = jnp.take_along_axis(packed, found + (step - 1), axis=1)
        at = lax.shift_right_logical(at, run) & 255
        found = jnp.where(at <= wanted, found + step, found)
        step //= 2
    kinetic = jnp.take_along_axis(kinetic, found, axis=1)
    code = jnp.take_along_axis(code, found, axis=1)
    zero = jnp.zeros((bricks, lanes), BF16)
    slot = iota((slabs * rows, bricks), 0).astype(F32).astype(BF16)
    values = []
    spots = []
    place = jnp.full((bricks, lanes), -1, jnp.int32)
    table = jnp.zeros((bricks, lanes), jnp.int32)
    for c in range(parts):
        table = jnp.where(lane == c, begins[c], table)
        place = jnp.where(
            part == c, (begins[c] + ranks[c].astype(jnp.int32) - 1) * parts + c, place
        )
        turn = (lane - shifts[c]) & (lanes - 1)
        valid = turn.astype(F32) < sizes[c]
        turn = (turn + earlier[c].astype(jnp.int32)) & (lanes - 1)
        kin = jnp.where(valid, jnp.take_along_axis(kinetic, turn, axis=1), 0.0)
        cell = jnp.where(valid, jnp.take_along_axis(code, turn, axis=1), 0)
        cell_row = quotient(cell, width_y)
        cell_y = cell - cell_row * width_y
        pieces = split(kin, 2) + [cell_row.astype(F32).astype(BF16), cell_y.astype(F32).astype(BF16)]
        first = lane >= shifts[c]
        values.append(jnp.concatenate([jnp.where(first, p, zero) for p in pieces], axis=1))
        values.append(jnp.concatenate([jnp.where(first, zero, p) for p in pieces], axis=1))
        begin_row = jnp.sum(
            jnp.where(eye, begins[c].astype(F32), 0.0), axis=0, keepdims=True
        ).astype(jnp.int32)
        target = quotient(begin_row, lanes).astype(F32)
        spots.append(slot == target.astype(BF16))
        spots.append(slot == (target + 1.0).astype(BF16))
    starts[...] = table
    meta[...] = place
    one = jnp.ones((), BF16)
    moved = jnp.dot(
        jnp.concatenate([jnp.where(spot, one, jnp.zeros((), BF16)) for spot in spots], axis=1),
        jnp.concatenate(values, axis=0),
        preferred_element_type=F32,
    )
    send[:, 0] = (moved[:, :lanes] + moved[:, lanes : 2 * lanes]).reshape(slabs, rows, lanes)
    send[:, 1] = (moved[:, 2 * lanes : 3 * lanes] * width_y + moved[:, 3 * lanes :]).reshape(
        slabs, rows, lanes
    )


def decode(code, width_y):
    row = jnp.floor((code + 0.5) * (1.0 / width_y))
    return row, code - row * width_y


def find_runs(dims, parts, got, runs_vmem):
    planes, width_x, width_y = dims
    slabs, _, rows, lanes = got.shape
    part_rows = planes * width_x // parts
    codes = got[:, 1]
    codes = jnp.where(codes > 0.0, codes, float((parts * part_rows + 1) * width_y + 1))
    longest = jnp.zeros((slabs, lanes), F32)
    first = jnp.zeros((slabs, lanes), F32)
    table = jnp.zeros((slabs, lanes), F32)
    lane = iota((slabs, lanes), 1)
    for c in range(parts):
        limit = float(((c + 1) * part_rows + 1) * width_y)
        last = jnp.sum(jnp.where(codes < limit, 1.0, 0.0), axis=1)
        longest = jnp.maximum(longest, last - first)
        table = jnp.where(lane == 2 * c, pltpu.roll(first, 2 * c, 1) if c else first, table)
        table = jnp.where(lane == 2 * c + 1, pltpu.roll(last, 2 * c + 1, 1), table)
        first = pltpu.roll(last, 1, 1)
    longest = jnp.max(jnp.where(lane == 0, longest, 0.0), keepdims=True)
    runs_vmem[...] = jnp.where(lane == 2 * parts, longest, table).astype(jnp.int32)


def run_row(got, field, s, spot, last):
    rows = got.shape[2]
    loaded = got[s, field, pl.ds(jnp.minimum(spot, rows - 1), 1), :]
    return jnp.where(spot < last, loaded, 0.0)


def bin_kernel(dims, parts, got, totals, codes, runs_vmem, lhs, rhs):
    planes, width_x, width_y = dims
    slabs, _, rows, lanes = got.shape
    part_rows = planes * width_x // parts
    find_runs(dims, parts, got, runs_vmem)
    runs = runs_vmem[...]
    first = [[runs[s, 2 * c] for s in range(slabs)] for c in range(parts)]
    last = [[runs[s, 2 * c + 1] for s in range(slabs)] for c in range(parts)]
    longest = runs[0, 2 * parts]
    one = jnp.ones((), F8)
    zero = jnp.zeros((), F8)
    y_id = iota((width_y, lanes), 0).astype(F32).astype(BF16)
    totals[...] = jnp.zeros(totals.shape, F32)

    def add_rows(turn, carry):
        for c in range(parts):
            row_id = (iota((part_rows, lanes), 0) + (c * part_rows + 1)).astype(F32).astype(BF16)
            for s in range(slabs):
                spot = first[c][s] + turn
                pieces = split_small(run_row(got, 0, s, spot, last[c][s]))
                code = run_row(got, 1, s, spot, last[c][s])
                codes[turn * parts + c, pl.ds(s, 1), :] = code
                row, y_cell = decode(code, width_y)
                here = pl.ds(s * lanes, lanes)
                hit = row_id == row.astype(BF16)
                for i, piece in enumerate(pieces):
                    lhs[c, pl.ds(i * part_rows, part_rows), here] = jnp.where(hit, piece, zero)
                lhs[c, pl.ds(PIECES * part_rows, part_rows), here] = jnp.where(hit, one, zero)
                rhs[c, :, here] = jnp.where(y_id == y_cell.astype(BF16), one, zero)
        for c in range(parts):
            added = lax.dot_general(
                lhs[c], rhs[c], (((1,), (1,)), ((), ())), preferred_element_type=F32
            )
            for i in range(PIECES + 1):
                for h in range(width_y // lanes):
                    totals[i, h, pl.ds(c * part_rows, part_rows), :] += added[
                        i * part_rows : (i + 1) * part_rows, h * lanes : (h + 1) * lanes
                    ]
        return carry

    lax.fori_loop(0, longest, add_rows, 0)


def solve_kernel(dims, totals, temp, below, x_low, x_high, summary, factors):
    planes, width_x, width_y = dims
    lanes = totals.shape[3]

    def plane_terms(z):
        here = temp[z]
        x_minus = jnp.concatenate([x_low[z], here[:-1]], axis=0)
        x_plus = jnp.concatenate([here[1:], x_high[z]], axis=0)
        lateral = LATERAL * (
            x_minus
            + x_plus
            + pltpu.roll(here, 1, 1)
            + pltpu.roll(here, width_y - 1, 1)
            - 4.0 * here
        )
        at = pl.ds(z, width_x, stride=planes)
        sums = [
            jnp.concatenate([totals[i, h, at, :] for h in range(width_y // lanes)], axis=1)
            for i in range(PIECES + 1)
        ]
        energy = join_small(sums[:PIECES])
        count = sums[PIECES]
        return here + COUPLE * count, here * here + lateral + COUPLE * TWO_THIRDS * energy

    start = temp[0]
    gate = jnp.where(
        lax.axis_index("gz") > 0, STIFFNESS * (0.5 * (start + below[0])), jnp.zeros_like(start)
    )
    excess, source = plane_terms(0)
    left_excess = jnp.zeros_like(start)
    left_source = jnp.zeros_like(start)
    for z in range(planes - 1):
        face = STIFFNESS * (0.5 * (temp[z + 1] + temp[z]))
        inverse = 1.0 / (gate + face + excess)
        to_left = gate * inverse
        to_right = face * inverse
        factors[z, 0] = to_left
        factors[z, 1] = to_right
        factors[z, 2] = source * inverse
        next_excess, next_source = plane_terms(z + 1)
        left_excess = left_excess + to_left * excess
        left_source = left_source + to_left * source
        gate = gate * to_right
        excess = next_excess + to_right * excess
        source = next_source + to_right * source
    for i, value in enumerate((gate, left_excess, left_source, excess, source)):
        summary[i] = value


def load_five(ref):
    return tuple(ref[i] for i in range(5))


def merge_kernel(level, last, mine, other, _, total):
    upper = (lax.axis_index("gz") & (1 << level)) != 0
    own = load_five(mine)
    came = load_five(other)
    low = tuple(jnp.where(upper, b, a) for a, b in zip(own, came))
    high = tuple(jnp.where(upper, a, b) for a, b in zip(own, came))
    joined = merge(low, high)
    if not last:
        for i in range(5):
            total[i] = joined[i]
        return
    in_upper = (lax.axis_index("gz") & (1 << (level + 1))) != 0
    end = jnp.zeros_like(joined[0])
    closed = suffix_step((end, end), joined)
    total[0] = jnp.where(in_upper, closed[0], joined[3])
    total[1] = jnp.where(in_upper, closed[1], joined[4])


def table_kernel(dims, parts, factors, table, spread):
    planes, width_x, width_y = dims
    part_rows = planes * width_x // parts
    lanes = spread.shape[3]
    zeros = jnp.zeros((width_x, width_y), F32)
    state = (zeros, zeros, zeros + 1.0)
    for z in range(planes - 1, -1, -1):
        if z < planes - 1:
            to_left, to_right, fixed = factors[z, 0], factors[z, 1], factors[z, 2]
            state = (
                fixed + to_right * state[0],
                to_left + to_right * state[1],
                to_right * state[2],
            )
        for t in range(3):
            for h in range(spread.shape[1]):
                spread[t, h, pl.ds(z, width_x, stride=planes), :] = state[t][
                    :, h * lanes : (h + 1) * lanes
                ]
    for c in range(parts):
        for t in range(3):
            for h in range(spread.shape[1]):
                block = spread[t, h, pl.ds(c * part_rows, part_rows), :]
                for i, piece in enumerate(split_small(block)):
                    at = pl.ds((t * PIECES + i) * part_rows, part_rows)
                    table[c, at, pl.ds(h * lanes, lanes)] = piece


def look_kernel(dims, parts, levels, phase, codes, runs, *refs):
    if phase == 0:
        factors, found, keys, spots, table, spread, rhs = refs
        table_kernel(dims, parts, factors, table, spread)
    else:
        table, _, found, keys, spots, rhs = refs
    planes, width_x, width_y = dims
    _, slabs, lanes = codes.shape
    part_rows = planes * width_x // parts
    halves = width_y // lanes
    one = jnp.ones((), F8)
    zero = jnp.zeros((), F8)
    y_id = iota((width_y, lanes), 0).astype(F32).astype(BF16)
    order = levels - 1 - phase
    turns = runs[0:1, :][0, 2 * parts]

    def find_rows(step, carry):
        wanted = []
        for c in range(parts):
            block = step * parts + c
            row, y_cell = decode(codes[(step * levels + order) * parts + c], width_y)
            wanted.append(row)
            hot = y_cell.astype(BF16)
            for s in range(slabs):
                rhs[c, :, pl.ds(s * lanes, lanes)] = jnp.where(
                    y_id == hot[s : s + 1], one, zero
                )
            x_cell = jnp.floor((row - (c * part_rows + 0.5)) * (1.0 / planes))
            half = jnp.floor((y_cell + 0.5) * (1.0 / lanes))
            keys[block] = jnp.where(row > c * part_rows, x_cell * halves + half, -1.0)
            spots[block] = (y_cell - half * lanes).astype(jnp.int32)
        for c in range(parts):
            block = step * parts + c
            row_id = (iota((part_rows, lanes), 0) + (c * part_rows + 1)).astype(F32)
            picked = jnp.dot(table[c], rhs[c], preferred_element_type=F32)
            for s in range(slabs):
                hit = row_id == wanted[c][s : s + 1]
                for t in range(3):
                    pieces = [
                        picked[
                            (t * PIECES + i) * part_rows : (t * PIECES + i + 1) * part_rows,
                            s * lanes : (s + 1) * lanes,
                        ]
                        for i in range(PIECES)
                    ]
                    total = pieces[-1]
                    for piece in pieces[-2::-1]:
                        total = piece + total * (1.0 / STEP)
                    chosen = jnp.sum(jnp.where(hit, total, 0.0), axis=0, keepdims=True)
                    found[t, block, pl.ds(s, 1), :] = chosen * (1.0 / SCALE)
        return carry

    lax.fori_loop(0, quotient_up(turns - order, levels), find_rows, 0)


def quotient_up(value, size):
    return (value + (size - 1)) // size


def join_kernel(dims, parts, levels, runs_vmem, *refs):
    planes, width_x, width_y = dims
    own = load_five(refs[0])
    others = refs[1:levels]
    far = refs[levels]
    found = refs[levels + 1 : 2 * levels + 1]
    keys = refs[2 * levels + 1 : 3 * levels + 1]
    lane_of = refs[3 * levels + 1 : 4 * levels + 1]
    edges, reply, temps, spread = refs[4 * levels + 1 :]
    slabs, rows, lanes = reply.shape
    part_x = width_x // parts
    halves = width_y // lanes
    runs = runs_vmem[...]
    first = [[runs[s, 2 * c] for s in range(slabs)] for c in range(parts)]
    longest = runs[0, 2 * parts]
    spread[:, :, pl.ds(0, rows), :] = jnp.zeros((parts, slabs, rows, lanes), F32)
    index = lax.axis_index("gz")
    zeros = jnp.zeros_like(own[0])
    top = (index & (1 << (levels - 1))) != 0
    before = (jnp.where(top, far[0], zeros + 1.0), jnp.where(top, far[1], zeros))
    after = (jnp.where(top, zeros, far[0]), jnp.where(top, zeros, far[1]))
    for level in range(levels - 2, -1, -1):
        upper = (index & (1 << level)) != 0
        segment = load_five(others[level])
        with_before = prefix_step(before, segment)
        with_after = suffix_step(after, segment)
        before = tuple(jnp.where(upper, a, b) for a, b in zip(with_before, before))
        after = tuple(jnp.where(upper, b, a) for a, b in zip(with_after, after))
    through = prefix_step(before, own)
    value = (through[1] + after[1]) / (through[0] + after[0])
    edges[0] = (before[1] + own[2] + own[0] * value) / (before[0] + own[1] + own[0])
    edges[1] = value

    def fill_rows(step, carry):
        for phase in range(levels):
            done = step * levels + (levels - 1 - phase) < longest
            for c in range(parts):
                block = step * parts + c
                key = keys[phase][block]
                lane = lane_of[phase][block] & (lanes - 1)
                ends = [jnp.zeros((slabs, lanes), F32), jnp.zeros((slabs, lanes), F32)]
                for x in range(part_x):
                    for h in range(halves):
                        hit = key == float(x * halves + h)
                        for e in range(2):
                            line = edges[e, pl.ds(c * part_x + x, 1), pl.ds(h * lanes, lanes)]
                            line = jnp.broadcast_to(line, (slabs, lanes))
                            ends[e] = jnp.where(
                                hit, jnp.take_along_axis(line, lane, axis=1), ends[e]
                            )
                temps[phase * parts + c] = jnp.where(
                    done,
                    found[phase][0, block]
                    + found[phase][1, block] * ends[0]
                    + found[phase][2, block] * ends[1],
                    0.0,
                )
        for phase in range(levels):
            for c in range(parts):
                for s in range(slabs):
                    spot = first[c][s] + step * levels + (levels - 1 - phase)
                    spread[c, s, pl.ds(spot, 1), :] = temps[phase * parts + c, pl.ds(s, 1), :]
        return carry

    lax.fori_loop(0, quotient_up(longest, levels), fill_rows, 0)
    total = spread[0, :, pl.ds(0, rows), :]
    for c in range(1, parts):
        total = total + spread[c, :, pl.ds(0, rows), :]
    reply[...] = total


def fill_kernel(factors, edges, new_temp):
    planes = new_temp.shape[0]
    edge = edges[0]
    value = edges[1]
    new_temp[planes - 1] = value
    for z in range(planes - 2, -1, -1):
        value = factors[z, 2] + factors[z, 0] * edge + factors[z, 1] * value
        new_temp[z] = value


def kick_kernel(parts, returned, meta, starts, velocity, noise, out):
    bricks, lanes = meta.shape
    slots = returned.shape[0]
    packed = meta[...]
    lane = iota((bricks, lanes), 1)
    in_use = packed >= 0
    place = quotient(jnp.maximum(packed, 0), parts)
    part = jnp.maximum(packed, 0) - place * parts
    slot = iota((bricks, slots), 1)
    spots = []
    shifts = []
    for c in range(parts):
        begin = jnp.broadcast_to(starts[:, c : c + 1], (bricks, lanes))
        target = quotient(begin[:, 0:1], lanes)
        shifts.append(begin & (lanes - 1))
        spots.append(slot == target)
        spots.append(slot == target + 1)
    values = jnp.concatenate(split(returned[...], 2), axis=1)
    moved = jnp.dot(
        jnp.where(jnp.concatenate(spots, axis=0), 1.0, 0.0).astype(BF16),
        values,
        preferred_element_type=F32,
    )
    moved = moved[:, :lanes] + moved[:, lanes:]
    at = place & (lanes - 1)
    temp = jnp.zeros((bricks, lanes), F32)
    for c in range(parts):
        here = moved[2 * c * bricks : (2 * c + 1) * bricks]
        after = moved[(2 * c + 1) * bricks : (2 * c + 2) * bricks]
        whole = jnp.where(lane >= shifts[c], here, after)
        temp = jnp.where(part == c, jnp.take_along_axis(whole, at, axis=1), temp)
    root = jnp.sqrt(2.0 * KICK_RATE * temp)
    for i in range(3):
        out[i] = jnp.where(in_use, (1.0 - KICK_RATE) * velocity[i] + root * noise[i], 0.0)


def call(kernel, out_shape, scratch=(), spaces=None, limit=VMEM_LIMIT, cost=None):
    extra = {} if cost is None else {"cost_estimate": cost}
    if spaces is not None:
        extra["in_specs"] = [pl.BlockSpec(memory_space=m) for m in spaces]
    return pl.pallas_call(
        kernel,
        out_shape=out_shape,
        **extra,
        scratch_shapes=list(scratch),
        compiler_params=pltpu.CompilerParams(vmem_limit_bytes=limit),
    )


def struct(*shape, dtype=F32):
    return jax.ShapeDtypeStruct(shape, dtype)


def route_call(dims, slabs, rows, parts, velocity_shape, plane_shape):
    bricks, lanes = plane_shape
    return call(
        functools.partial(route_kernel, dims, slabs, rows, parts),
        (
            struct(slabs, 2, rows, lanes),
            struct(bricks, lanes, dtype=jnp.int32),
            struct(bricks, lanes, dtype=jnp.int32),
        ),
        (
            pltpu.VMEM(velocity_shape, F32),
            pltpu.VMEM(plane_shape, jnp.int32),
            pltpu.VMEM(plane_shape, jnp.int32),
            pltpu.VMEM((1, bricks), jnp.int32),
            pltpu.SemaphoreType.DMA((4,)),
        ),
        (pltpu.HBM,) * 4,
        ROUTE_LIMIT,
    )


def body(atom_velocity, atom_noise, atom_plane, atom_column, brick_count, electron_temp):
    dims = electron_temp.shape
    planes, width_x, width_y = dims
    cells = planes * width_x
    slabs = lax.axis_size("gz")
    groups = lax.axis_size("gx")
    levels = slabs.bit_length() - 1
    assert slabs == 1 << levels and levels > 0
    bricks, lanes = atom_plane.shape
    rows = 2 * bricks // slabs
    parts = PARTS
    assert width_x % parts == 0 and parts <= 4 and lanes <= 128
    send, meta, starts = route_call(
        dims, slabs, rows, parts, atom_velocity.shape, atom_plane.shape
    )(
        *(
            pltpu.with_memory_space_constraint(x, pltpu.HBM)
            for x in (brick_count.reshape(1, bricks), atom_velocity, atom_plane, atom_column)
        )
    )
    got = lax.all_to_all(send, "gz", split_axis=0, concat_axis=0, tiled=True)
    below = lax.ppermute(electron_temp[-1:], "gz", [(i, i + 1) for i in range(slabs - 1)])
    x_low = lax.ppermute(
        electron_temp[:, -1:], "gx", [(i, (i + 1) % groups) for i in range(groups)]
    )
    x_high = lax.ppermute(
        electron_temp[:, :1], "gx", [((i + 1) % groups, i) for i in range(groups)]
    )
    totals, codes, runs = call(
        functools.partial(bin_kernel, dims, parts),
        (
            struct(PIECES + 1, width_y // lanes, cells, lanes),
            struct(parts * (rows + 1), slabs, lanes),
            struct(slabs, lanes, dtype=jnp.int32),
        ),
        (
            pltpu.VMEM((parts, (PIECES + 1) * cells // parts, slabs * lanes), F8),
            pltpu.VMEM((parts, width_y, slabs * lanes), F8),
        ),
    )(got)
    total, factors = call(
        functools.partial(solve_kernel, dims),
        (struct(5, width_x, width_y), struct(planes - 1, 3, width_x, width_y)),
    )(totals, electron_temp, below, x_low, x_high)
    blocks = parts * quotient_up(rows, levels)
    found_shapes = (
        struct(3, blocks, slabs, lanes),
        struct(blocks, slabs, lanes),
        struct(blocks, slabs, lanes, dtype=jnp.int32),
    )
    table_shape = (parts, 3 * PIECES * cells // parts, width_y)
    pieces = [total]
    found = []
    for level in range(levels):
        other = lax.ppermute(total, "gz", [(i, i ^ (1 << level)) for i in range(slabs)])
        outs = call(
            functools.partial(look_kernel, dims, parts, levels, level),
            found_shapes + ((struct(*table_shape, dtype=F8),) if level == 0 else ()),
            (() if level else (pltpu.VMEM((3, width_y // lanes, cells, lanes), F32),))
            + (pltpu.VMEM((parts, width_y, slabs * lanes), F8),),
            cost=LOOK_COST,
        )(codes, runs, *((table, total) if level else (factors,)))
        if level == 0:
            table = outs[3]
        found.append(outs[:3])
        pieces.append(other)
        if level < levels - 1:
            last = level == levels - 2
            total = call(
                functools.partial(merge_kernel, level, last),
                struct(2 if last else 5, width_x, width_y),
            )(total, other, outs[1])
    edges, reply = call(
        functools.partial(join_kernel, dims, parts, levels),
        (struct(2, width_x, width_y), struct(slabs, rows, lanes)),
        (
            pltpu.VMEM((levels * parts, slabs, lanes), F32),
            pltpu.VMEM((parts, slabs, 2 * rows + 8 * levels, lanes), F32),
        ),
    )(runs, *pieces, *(phase[i] for i in range(3) for phase in found))
    new_temp = call(fill_kernel, struct(*dims))(factors, edges)
    returned = lax.all_to_all(reply, "gz", split_axis=0, concat_axis=0, tiled=True)
    new_velocity = call(functools.partial(kick_kernel, parts), struct(*atom_velocity.shape))(
        returned.reshape(slabs * rows, lanes), meta, starts, atom_velocity, atom_noise
    )
    return (new_temp, new_velocity)


def solution(mesh):
    placed = (
        P(None, ("gz", "gx"), None),
        P(None, ("gz", "gx"), None),
        P(("gz", "gx"), None),
        P(("gz", "gx"), None),
        P(("gz", "gx")),
        P("gz", "gx", None),
    )
    return jax.shard_map(
        body,
        mesh=mesh,
        in_specs=placed,
        out_specs=(P("gz", "gx", None), P(None, ("gz", "gx"), None)),
        check_vma=False,
    )
```

```python
import functools

import jax
import jax.numpy as jnp
from jax import lax
from jax.experimental import pallas as pl
from jax.experimental.pallas import tpu as pltpu
from jax.sharding import PartitionSpec as P

STIFFNESS = 10000.0
LATERAL = 0.1
COUPLE = 0.5
TWO_THIRDS = 2.0 / 3.0
KICK_RATE = 0.2
F32 = jnp.float32
BF16 = jnp.bfloat16
F8 = jnp.float8_e4m3fn
SCALE = 8.0
STEP = 16.0
PIECES = 3
PARTS = 4
ROUTE_LIMIT = 32 * 1024 * 1024
VMEM_LIMIT = 32 * 1024 * 1024
LOOK_COST = pl.CostEstimate(flops=2 * 10**9, bytes_accessed=10**7, transcendentals=0)


def quotient(value, size):
    if size & (size - 1) == 0:
        return lax.shift_right_logical(value, size.bit_length() - 1)
    return value // size


def iota(shape, dim):
    return lax.broadcasted_iota(jnp.int32, shape, dim)


def split(value, pieces):
    parts = []
    for _ in range(pieces):
        part = value.astype(BF16)
        parts.append(part)
        value = value - part.astype(F32)
    return parts


def split_small(value):
    value = value * SCALE
    parts = []
    for _ in range(PIECES):
        part = value.astype(F8)
        parts.append(part)
        value = (value - part.astype(F32)) * STEP
    return parts


def join_small(parts):
    total = parts[-1]
    for part in parts[-2::-1]:
        total = part + total * (1.0 / STEP)
    return total * (1.0 / SCALE)


def merge(left, right):
    g_a, sl_a, rl_a, s_a, r_a = left
    g_b, sl_b, rl_b, s_b, r_b = right
    excess = s_a + sl_b
    source = r_a + rl_b
    inverse = 1.0 / (g_a + g_b + excess)
    to_left = g_a * inverse
    to_right = g_b * inverse
    return (
        g_a * to_right,
        sl_a + to_left * excess,
        rl_a + to_left * source,
        s_b + to_right * excess,
        r_b + to_right * source,
    )


def prefix_step(state, segment):
    gate, sl, rl, s, r = segment
    excess = state[0] + sl
    source = state[1] + rl
    ratio = gate / (gate + excess)
    return (s + ratio * excess, r + ratio * source)


def suffix_step(state, segment):
    gate, sl, rl, s, r = segment
    excess = s + state[0]
    source = r + state[1]
    ratio = gate / (gate + excess)
    return (sl + ratio * excess, rl + ratio * source)


def route_kernel(
    dims, slabs, rows, parts, count_hbm, velocity_hbm, plane_hbm, column_hbm, send, meta, starts,
    velocity, plane, column, count, arrived,
):
    copies = [
        pltpu.make_async_copy(source, target, arrived.at[i])
        for i, (source, target) in enumerate(
            (
                (count_hbm, count),
                (plane_hbm, plane),
                (column_hbm, column),
                (velocity_hbm, velocity),
            )
        )
    ]
    for copy in copies:
        copy.start()
    planes, width_x, width_y = dims
    bricks, lanes = plane.shape
    part_rows = planes * width_x // parts
    lane = iota((bricks, lanes), 1)
    sub_b = iota((bricks, bricks), 0)
    lane_b = iota((bricks, bricks), 1)
    eye = sub_b == lane_b
    sub_l = iota((lanes, lanes), 0)
    lane_l = iota((lanes, lanes), 1)
    prefix = jnp.concatenate(
        [jnp.where(sub_l <= lane_l, 1.0, 0.0), jnp.ones((lanes, lanes), F32)], axis=1
    ).astype(BF16)
    copies[0].wait()
    count_row = jnp.broadcast_to(count[...].astype(F32), (bricks, bricks))
    count_col = jnp.sum(jnp.where(eye, count_row, 0.0), axis=1, keepdims=True).astype(jnp.int32)
    in_use = lane < count_col
    copies[1].wait()
    owner = quotient(plane[:, 0:1], planes)
    owner_f = jnp.broadcast_to(owner.astype(F32), (bricks, bricks))
    owner_row = jnp.sum(jnp.where(eye, owner_f, 0.0), axis=0, keepdims=True)
    same = owner_f == owner_row
    ahead = same & (lane_b < sub_b)
    peers = jnp.where(jnp.concatenate([same, ahead], axis=0), 1.0, 0.0).astype(BF16)
    copies[2].wait()
    col = column[...]
    x_cell = quotient(col, width_y)
    y_cell = col - x_cell * width_y
    row = x_cell * planes + plane[...] - owner * planes
    code = jnp.where(in_use, (row + 1) * width_y + y_cell, 0)
    part = jnp.where(in_use, quotient(row, part_rows), parts)
    inside = [jnp.where(part == c, 1.0, 0.0).astype(BF16) for c in range(parts)]
    sums = jnp.dot(jnp.concatenate(inside, axis=0), prefix, preferred_element_type=F32)
    ranks = [sums[c * bricks : (c + 1) * bricks, :lanes] for c in range(parts)]
    sizes = [sums[c * bricks : (c + 1) * bricks, lanes:] for c in range(parts)]
    earlier = [jnp.zeros_like(sizes[0])]
    for c in range(parts - 1):
        earlier.append(earlier[-1] + sizes[c])
    joint = jnp.dot(
        peers, jnp.concatenate(sizes, axis=1).astype(BF16), preferred_element_type=F32
    )
    copies[3].wait()
    vx, vy, vz = velocity[0], velocity[1], velocity[2]
    kinetic = 0.5 * (vx * vx + vy * vy + vz * vz)
    dense = jnp.zeros((bricks, lanes), F32)
    whole = jnp.zeros((bricks, lanes), F32)
    bases = []
    for c in range(parts):
        bases.append((dense, whole))
        size = joint[:bricks, c * lanes : (c + 1) * lanes]
        dense = dense + size
        whole = whole + jnp.floor((size + (lanes - 1)) * (1.0 / lanes)) * lanes
    begins = [
        owner * (rows * lanes)
        + (
            jnp.where(whole <= rows * lanes, base[1], base[0])
            + joint[bricks:, c * lanes : (c + 1) * lanes]
        ).astype(jnp.int32)
        for c, base in enumerate(bases)
    ]
    shifts = [begin & (lanes - 1) for begin in begins]
    packed = ranks[0].astype(jnp.int32)
    run = jnp.zeros((bricks, lanes), jnp.int32)
    base = jnp.zeros((bricks, lanes), F32)
    lane_f = lane.astype(F32)
    for c in range(1, parts):
        packed = packed | (ranks[c].astype(jnp.int32) << (8 * c))
        run = jnp.where(lane_f >= earlier[c], 8 * c, run)
        base = jnp.where(lane_f >= earlier[c], earlier[c], base)
    wanted = lane - base.astype(jnp.int32)
    found = jnp.zeros((bricks, lanes), jnp.int32)
    step = lanes // 2
    while step:
        at = jnp.take_along_axis(packed, found + (step - 1), axis=1)
        at = lax.shift_right_logical(at, run) & 255
        found = jnp.where(at <= wanted, found + step, found)
        step //= 2
    kinetic = jnp.take_along_axis(kinetic, found, axis=1)
    code = jnp.take_along_axis(code, found, axis=1)
    zero = jnp.zeros((bricks, lanes), BF16)
    slot = iota((slabs * rows, bricks), 0).astype(F32).astype(BF16)
    values = []
    spots = []
    place = jnp.full((bricks, lanes), -1, jnp.int32)
    table = jnp.zeros((bricks, lanes), jnp.int32)
    for c in range(parts):
        table = jnp.where(lane == c, begins[c], table)
        place = jnp.where(
            part == c, (begins[c] + ranks[c].astype(jnp.int32) - 1) * parts + c, place
        )
        turn = (lane - shifts[c]) & (lanes - 1)
        valid = turn.astype(F32) < sizes[c]
        turn = (turn + earlier[c].astype(jnp.int32)) & (lanes - 1)
        kin = jnp.where(valid, jnp.take_along_axis(kinetic, turn, axis=1), 0.0)
        cell = jnp.where(valid, jnp.take_along_axis(code, turn, axis=1), 0)
        cell_row = quotient(cell, width_y)
        cell_y = cell - cell_row * width_y
        pieces = split(kin, 2) + [cell_row.astype(F32).astype(BF16), cell_y.astype(F32).astype(BF16)]
        first = lane >= shifts[c]
        values.append(jnp.concatenate([jnp.where(first, p, zero) for p in pieces], axis=1))
        values.append(jnp.concatenate([jnp.where(first, zero, p) for p in pieces], axis=1))
        begin_row = jnp.sum(
            jnp.where(eye, begins[c].astype(F32), 0.0), axis=0, keepdims=True
        ).astype(jnp.int32)
        target = quotient(begin_row, lanes).astype(F32)
        spots.append(slot == target.astype(BF16))
        spots.append(slot == (target + 1.0).astype(BF16))
    starts[...] = table
    meta[...] = place
    one = jnp.ones((), BF16)
    moved = jnp.dot(
        jnp.concatenate([jnp.where(spot, one, jnp.zeros((), BF16)) for spot in spots], axis=1),
        jnp.concatenate(values, axis=0),
        preferred_element_type=F32,
    )
    send[:, 0] = (moved[:, :lanes] + moved[:, lanes : 2 * lanes]).reshape(slabs, rows, lanes)
    send[:, 1] = (moved[:, 2 * lanes : 3 * lanes] * width_y + moved[:, 3 * lanes :]).reshape(
        slabs, rows, lanes
    )


def decode(code, width_y):
    row = jnp.floor((code + 0.5) * (1.0 / width_y))
    return row, code - row * width_y


def find_runs(dims, parts, got, runs_vmem):
    planes, width_x, width_y = dims
    slabs, _, rows, lanes = got.shape
    part_rows = planes * width_x // parts
    codes = got[:, 1]
    beyond = float((parts * part_rows + 1) * width_y + 1)
    lead = codes[:, :, 0:1]
    used = lead > 0.0
    lead = jnp.where(used, lead, beyond)
    top = jnp.where(used, jnp.max(codes, axis=2, keepdims=True), beyond)
    longest = jnp.zeros((slabs, 1), F32)
    first = jnp.zeros((slabs, 1), F32)
    table = jnp.zeros((slabs, lanes), F32)
    lane = iota((slabs, lanes), 1)
    for c in range(parts):
        limit = float(((c + 1) * part_rows + 1) * width_y)
        last = jnp.sum(jnp.where(lead < limit, 1.0, 0.0), axis=1)
        longest = jnp.maximum(longest, last - first)
        table = jnp.where(lane == 2 * c, first, table)
        table = jnp.where(lane == 2 * c + 1, last, table)
        first = jnp.sum(jnp.where(top < limit, 1.0, 0.0), axis=1)
    longest = jnp.max(longest, axis=0, keepdims=True)
    runs_vmem[...] = jnp.where(lane == 2 * parts, longest, table).astype(jnp.int32)


def run_row(got, field, s, spot, last):
    rows = got.shape[2]
    loaded = got[s, field, pl.ds(jnp.minimum(spot, rows - 1), 1), :]
    return jnp.where(spot < last, loaded, 0.0)


def bin_kernel(dims, parts, got, _, totals, codes, runs_vmem, lhs, rhs):
    planes, width_x, width_y = dims
    slabs, _, rows, lanes = got.shape
    part_rows = planes * width_x // parts
    find_runs(dims, parts, got, runs_vmem)
    runs = runs_vmem[...]
    first = [[runs[s, 2 * c] for s in range(slabs)] for c in range(parts)]
    last = [[runs[s, 2 * c + 1] for s in range(slabs)] for c in range(parts)]
    longest = runs[0, 2 * parts]
    one = jnp.ones((), F8)
    zero = jnp.zeros((), F8)
    y_id = iota((width_y, lanes), 0).astype(F32).astype(BF16)
    totals[...] = jnp.zeros(totals.shape, F32)

    def add_rows(turn, carry):
        for c in range(parts):
            row_id = (iota((part_rows, lanes), 0) + (c * part_rows + 1)).astype(F32).astype(BF16)
            for s in range(slabs):
                spot = first[c][s] + turn
                pieces = split_small(run_row(got, 0, s, spot, last[c][s]))
                code = run_row(got, 1, s, spot, last[c][s])
                codes[turn * parts + c, pl.ds(s, 1), :] = code
                row, y_cell = decode(code, width_y)
                here = pl.ds(s * lanes, lanes)
                hit = row_id == row.astype(BF16)
                for i, piece in enumerate(pieces):
                    lhs[c, pl.ds(i * part_rows, part_rows), here] = jnp.where(hit, piece, zero)
                lhs[c, pl.ds(PIECES * part_rows, part_rows), here] = jnp.where(hit, one, zero)
                rhs[c, :, here] = jnp.where(y_id == y_cell.astype(BF16), one, zero)
        for c in range(parts):
            added = lax.dot_general(
                lhs[c], rhs[c], (((1,), (1,)), ((), ())), preferred_element_type=F32
            )
            for i in range(PIECES + 1):
                for h in range(width_y // lanes):
                    totals[i, h, pl.ds(c * part_rows, part_rows), :] += added[
                        i * part_rows : (i + 1) * part_rows, h * lanes : (h + 1) * lanes
                    ]
        return carry

    lax.fori_loop(0, longest, add_rows, 0)


def solve_kernel(dims, totals, temp, below, x_low, x_high, summary, factors):
    planes, width_x, width_y = dims
    lanes = totals.shape[3]

    def plane_terms(z):
        here = temp[z]
        x_minus = jnp.concatenate([x_low[z], here[:-1]], axis=0)
        x_plus = jnp.concatenate([here[1:], x_high[z]], axis=0)
        lateral = LATERAL * (
            x_minus
            + x_plus
            + pltpu.roll(here, 1, 1)
            + pltpu.roll(here, width_y - 1, 1)
            - 4.0 * here
        )
        at = pl.ds(z, width_x, stride=planes)
        sums = [
            jnp.concatenate([totals[i, h, at, :] for h in range(width_y // lanes)], axis=1)
            for i in range(PIECES + 1)
        ]
        energy = join_small(sums[:PIECES])
        count = sums[PIECES]
        return here + COUPLE * count, here * here + lateral + COUPLE * TWO_THIRDS * energy

    start = temp[0]
    gate = jnp.where(
        lax.axis_index("gz") > 0, STIFFNESS * (0.5 * (start + below[0])), jnp.zeros_like(start)
    )
    excess, source = plane_terms(0)
    left_excess = jnp.zeros_like(start)
    left_source = jnp.zeros_like(start)
    for z in range(planes - 1):
        face = STIFFNESS * (0.5 * (temp[z + 1] + temp[z]))
        inverse = 1.0 / (gate + face + excess)
        to_left = gate * inverse
        to_right = face * inverse
        factors[z, 0] = to_left
        factors[z, 1] = to_right
        factors[z, 2] = source * inverse
        next_excess, next_source = plane_terms(z + 1)
        left_excess = left_excess + to_left * excess
        left_source = left_source + to_left * source
        gate = gate * to_right
        excess = next_excess + to_right * excess
        source = next_source + to_right * source
    for i, value in enumerate((gate, left_excess, left_source, excess, source)):
        summary[i] = value


def load_five(ref):
    return tuple(ref[i] for i in range(5))


def merge_kernel(level, last, mine, other, _, total):
    upper = (lax.axis_index("gz") & (1 << level)) != 0
    own = load_five(mine)
    came = load_five(other)
    low = tuple(jnp.where(upper, b, a) for a, b in zip(own, came))
    high = tuple(jnp.where(upper, a, b) for a, b in zip(own, came))
    joined = merge(low, high)
    if not last:
        for i in range(5):
            total[i] = joined[i]
        return
    in_upper = (lax.axis_index("gz") & (1 << (level + 1))) != 0
    end = jnp.zeros_like(joined[0])
    closed = suffix_step((end, end), joined)
    total[0] = jnp.where(in_upper, closed[0], joined[3])
    total[1] = jnp.where(in_upper, closed[1], joined[4])


def table_kernel(dims, parts, factors, table, spread):
    planes, width_x, width_y = dims
    part_rows = planes * width_x // parts
    lanes = spread.shape[3]
    zeros = jnp.zeros((width_x, width_y), F32)
    state = (zeros, zeros, zeros + 1.0)
    for z in range(planes - 1, -1, -1):
        if z < planes - 1:
            to_left, to_right, fixed = factors[z, 0], factors[z, 1], factors[z, 2]
            state = (
                fixed + to_right * state[0],
                to_left + to_right * state[1],
                to_right * state[2],
            )
        for t in range(3):
            for h in range(spread.shape[1]):
                spread[t, h, pl.ds(z, width_x, stride=planes), :] = state[t][
                    :, h * lanes : (h + 1) * lanes
                ]
    for c in range(parts):
        for t in range(3):
            for h in range(spread.shape[1]):
                block = spread[t, h, pl.ds(c * part_rows, part_rows), :]
                for i, piece in enumerate(split_small(block)):
                    at = pl.ds((t * PIECES + i) * part_rows, part_rows)
                    table[c, at, pl.ds(h * lanes, lanes)] = piece


def look_kernel(dims, parts, levels, phase, codes, runs, *refs):
    if phase == 0:
        factors, found, keys, spots, table, spread, rhs = refs
        table_kernel(dims, parts, factors, table, spread)
    else:
        table, _, found, keys, spots, rhs = refs
    planes, width_x, width_y = dims
    _, slabs, lanes = codes.shape
    part_rows = planes * width_x // parts
    halves = width_y // lanes
    one = jnp.ones((), F8)
    zero = jnp.zeros((), F8)
    y_id = iota((width_y, lanes), 0).astype(F32).astype(BF16)
    order = levels - 1 - phase
    turns = runs[0:1, :][0, 2 * parts]

    def find_rows(step, carry):
        wanted = []
        for c in range(parts):
            block = step * parts + c
            row, y_cell = decode(codes[(step * levels + order) * parts + c], width_y)
            wanted.append(row)
            hot = y_cell.astype(BF16)
            for s in range(slabs):
                rhs[c, :, pl.ds(s * lanes, lanes)] = jnp.where(
                    y_id == hot[s : s + 1], one, zero
                )
            x_cell = jnp.floor((row - (c * part_rows + 0.5)) * (1.0 / planes))
            half = jnp.floor((y_cell + 0.5) * (1.0 / lanes))
            keys[block] = jnp.where(row > c * part_rows, x_cell * halves + half, -1.0)
            spots[block] = (y_cell - half * lanes).astype(jnp.int32)
        for c in range(parts):
            block = step * parts + c
            row_id = (iota((part_rows, lanes), 0) + (c * part_rows + 1)).astype(F32)
            picked = jnp.dot(table[c], rhs[c], preferred_element_type=F32)
            for s in range(slabs):
                hit = row_id == wanted[c][s : s + 1]
                for t in range(3):
                    pieces = [
                        picked[
                            (t * PIECES + i) * part_rows : (t * PIECES + i + 1) * part_rows,
                            s * lanes : (s + 1) * lanes,
                        ]
                        for i in range(PIECES)
                    ]
                    total = pieces[-1]
                    for piece in pieces[-2::-1]:
                        total = piece + total * (1.0 / STEP)
                    chosen = jnp.sum(jnp.where(hit, total, 0.0), axis=0, keepdims=True)
                    found[t, block, pl.ds(s, 1), :] = chosen * (1.0 / SCALE)
        return carry

    lax.fori_loop(0, quotient_up(turns - order, levels), find_rows, 0)


def quotient_up(value, size):
    return (value + (size - 1)) // size


def join_kernel(dims, parts, levels, runs_vmem, *refs):
    planes, width_x, width_y = dims
    own = load_five(refs[0])
    others = refs[1:levels]
    far = refs[levels]
    found = refs[levels + 1 : 2 * levels + 1]
    keys = refs[2 * levels + 1 : 3 * levels + 1]
    lane_of = refs[3 * levels + 1 : 4 * levels + 1]
    edges, reply, temps, spread = refs[4 * levels + 1 :]
    slabs, rows, lanes = reply.shape
    part_x = width_x // parts
    halves = width_y // lanes
    runs = runs_vmem[...]
    first = [[runs[s, 2 * c] for s in range(slabs)] for c in range(parts)]
    longest = runs[0, 2 * parts]
    spread[:, :, pl.ds(0, rows), :] = jnp.zeros((parts, slabs, rows, lanes), F32)
    index = lax.axis_index("gz")
    zeros = jnp.zeros_like(own[0])
    top = (index & (1 << (levels - 1))) != 0
    before = (jnp.where(top, far[0], zeros + 1.0), jnp.where(top, far[1], zeros))
    after = (jnp.where(top, zeros, far[0]), jnp.where(top, zeros, far[1]))
    for level in range(levels - 2, -1, -1):
        upper = (index & (1 << level)) != 0
        segment = load_five(others[level])
        with_before = prefix_step(before, segment)
        with_after = suffix_step(after, segment)
        before = tuple(jnp.where(upper, a, b) for a, b in zip(with_before, before))
        after = tuple(jnp.where(upper, b, a) for a, b in zip(with_after, after))
    through = prefix_step(before, own)
    value = (through[1] + after[1]) / (through[0] + after[0])
    edges[0] = (before[1] + own[2] + own[0] * value) / (before[0] + own[1] + own[0])
    edges[1] = value

    def fill_rows(step, carry):
        for phase in range(levels):
            done = step * levels + (levels - 1 - phase) < longest
            for c in range(parts):
                block = step * parts + c
                key = keys[phase][block]
                lane = lane_of[phase][block] & (lanes - 1)
                ends = [jnp.zeros((slabs, lanes), F32), jnp.zeros((slabs, lanes), F32)]
                for x in range(part_x):
                    for h in range(halves):
                        hit = key == float(x * halves + h)
                        for e in range(2):
                            line = edges[e, pl.ds(c * part_x + x, 1), pl.ds(h * lanes, lanes)]
                            line = jnp.broadcast_to(line, (slabs, lanes))
                            ends[e] = jnp.where(
                                hit, jnp.take_along_axis(line, lane, axis=1), ends[e]
                            )
                temps[phase * parts + c] = jnp.where(
                    done,
                    found[phase][0, block]
                    + found[phase][1, block] * ends[0]
                    + found[phase][2, block] * ends[1],
                    0.0,
                )
        for phase in range(levels):
            for c in range(parts):
                for s in range(slabs):
                    spot = first[c][s] + step * levels + (levels - 1 - phase)
                    spread[c, s, pl.ds(spot, 1), :] = temps[phase * parts + c, pl.ds(s, 1), :]
        return carry

    lax.fori_loop(0, quotient_up(longest, levels), fill_rows, 0)
    total = spread[0, :, pl.ds(0, rows), :]
    for c in range(1, parts):
        total = total + spread[c, :, pl.ds(0, rows), :]
    reply[...] = total


def fill_planes(factors, edges, new_temp):
    planes = new_temp.shape[0]
    edge = edges[0]
    value = edges[1]
    new_temp[planes - 1] = value
    for z in range(planes - 2, -1, -1):
        value = factors[z, 2] + factors[z, 0] * edge + factors[z, 1] * value
        new_temp[z] = value


def spot_kernel(parts, slots, lanes, starts, meta, velocity, noise, spots, base, push):
    in_use = meta[...] >= 0
    for i in range(3):
        base[i] = jnp.where(in_use, (1.0 - KICK_RATE) * velocity[i], 0.0)
        push[i] = jnp.where(in_use, noise[i], 0.0)
    bricks = starts.shape[0]
    slot = iota((bricks, slots), 1).astype(F32).astype(BF16)
    one = jnp.ones((), BF16)
    zero = jnp.zeros((), BF16)
    for c in range(parts):
        begin = jnp.broadcast_to(starts[:, c : c + 1], (bricks, slots))
        target = quotient(begin, lanes).astype(F32)
        for i in range(2):
            at = pl.ds((2 * c + i) * bricks, bricks)
            spots[at, :] = jnp.where(slot == (target + float(i)).astype(BF16), one, zero)


def kick_kernel(
    parts, returned, spots, meta, starts, base, push, factors, edges,
    out, new_temp, kicked, filled, left,
):
    fill_planes(factors, edges, filled)
    copies = [pltpu.make_async_copy(filled, new_temp, left.at[3])]
    copies[0].start()
    bricks, lanes = meta.shape
    packed = meta[...]
    lane = iota((bricks, lanes), 1)
    in_use = packed >= 0
    place = quotient(jnp.maximum(packed, 0), parts)
    part = jnp.maximum(packed, 0) - place * parts
    values = jnp.concatenate(split(returned[...], 2), axis=1)
    moved = jnp.dot(spots[...], values, preferred_element_type=F32)
    moved = moved[:, :lanes] + moved[:, lanes:]
    at = place & (lanes - 1)
    temp = jnp.zeros((bricks, lanes), F32)
    for c in range(parts):
        shift = jnp.broadcast_to(starts[:, c : c + 1], (bricks, lanes)) & (lanes - 1)
        here = moved[2 * c * bricks : (2 * c + 1) * bricks]
        after = moved[(2 * c + 1) * bricks : (2 * c + 2) * bricks]
        whole = jnp.where(lane >= shift, here, after)
        temp = jnp.where(part == c, jnp.take_along_axis(whole, at, axis=1), temp)
    root = jnp.where(in_use, jnp.sqrt(2.0 * KICK_RATE * temp), 0.0)
    for i in range(3):
        kicked[i] = base[i] + root * push[i]
        copies.append(pltpu.make_async_copy(kicked.at[i], out.at[i], left.at[i]))
        copies[-1].start()
    for copy in copies:
        copy.wait()


def call(kernel, out_shape, scratch=(), spaces=None, limit=VMEM_LIMIT, cost=None, outs=None):
    extra = {} if cost is None else {"cost_estimate": cost}
    if spaces is not None:
        extra["in_specs"] = [pl.BlockSpec(memory_space=m) for m in spaces]
    if outs is not None:
        extra["out_specs"] = tuple(pl.BlockSpec(memory_space=m) for m in outs)
    return pl.pallas_call(
        kernel,
        out_shape=out_shape,
        **extra,
        scratch_shapes=list(scratch),
        compiler_params=pltpu.CompilerParams(vmem_limit_bytes=limit),
    )


def struct(*shape, dtype=F32):
    return jax.ShapeDtypeStruct(shape, dtype)


def route_call(dims, slabs, rows, parts, velocity_shape, plane_shape):
    bricks, lanes = plane_shape
    return call(
        functools.partial(route_kernel, dims, slabs, rows, parts),
        (
            struct(slabs, 2, rows, lanes),
            struct(bricks, lanes, dtype=jnp.int32),
            struct(bricks, lanes, dtype=jnp.int32),
        ),
        (
            pltpu.VMEM(velocity_shape, F32),
            pltpu.VMEM(plane_shape, jnp.int32),
            pltpu.VMEM(plane_shape, jnp.int32),
            pltpu.VMEM((1, bricks), jnp.int32),
            pltpu.SemaphoreType.DMA((4,)),
        ),
        (pltpu.HBM,) * 4,
        ROUTE_LIMIT,
    )


def body(atom_velocity, atom_noise, atom_plane, atom_column, brick_count, electron_temp):
    dims = electron_temp.shape
    planes, width_x, width_y = dims
    cells = planes * width_x
    slabs = lax.axis_size("gz")
    groups = lax.axis_size("gx")
    levels = slabs.bit_length() - 1
    assert slabs == 1 << levels and levels > 0
    bricks, lanes = atom_plane.shape
    rows = 2 * bricks // slabs
    parts = PARTS
    assert width_x % parts == 0 and parts <= 4 and lanes <= 128
    send, meta, starts = route_call(
        dims, slabs, rows, parts, atom_velocity.shape, atom_plane.shape
    )(
        *(
            pltpu.with_memory_space_constraint(x, pltpu.HBM)
            for x in (brick_count.reshape(1, bricks), atom_velocity, atom_plane, atom_column)
        )
    )
    spots, base, push = call(
        functools.partial(spot_kernel, parts, slabs * rows, lanes),
        (
            struct(2 * parts * bricks, slabs * rows, dtype=BF16),
            struct(*atom_velocity.shape),
            struct(*atom_noise.shape),
        ),
    )(starts, meta, atom_velocity, atom_noise)
    got = lax.all_to_all(send, "gz", split_axis=0, concat_axis=0, tiled=True)
    below = lax.ppermute(electron_temp[-1:], "gz", [(i, i + 1) for i in range(slabs - 1)])
    x_low = lax.ppermute(
        electron_temp[:, -1:], "gx", [(i, (i + 1) % groups) for i in range(groups)]
    )
    x_high = lax.ppermute(
        electron_temp[:, :1], "gx", [((i + 1) % groups, i) for i in range(groups)]
    )
    totals, codes, runs = call(
        functools.partial(bin_kernel, dims, parts),
        (
            struct(PIECES + 1, width_y // lanes, cells, lanes),
            struct(parts * (rows + 1), slabs, lanes),
            struct(slabs, lanes, dtype=jnp.int32),
        ),
        (
            pltpu.VMEM((parts, (PIECES + 1) * cells // parts, slabs * lanes), F8),
            pltpu.VMEM((parts, width_y, slabs * lanes), F8),
        ),
    )(got, spots)
    total, factors = call(
        functools.partial(solve_kernel, dims),
        (struct(5, width_x, width_y), struct(planes - 1, 3, width_x, width_y)),
    )(totals, electron_temp, below, x_low, x_high)
    blocks = parts * quotient_up(rows, levels)
    found_shapes = (
        struct(3, blocks, slabs, lanes),
        struct(blocks, slabs, lanes),
        struct(blocks, slabs, lanes, dtype=jnp.int32),
    )
    table_shape = (parts, 3 * PIECES * cells // parts, width_y)
    pieces = [total]
    found = []
    for level in range(levels):
        other = lax.ppermute(total, "gz", [(i, i ^ (1 << level)) for i in range(slabs)])
        outs = call(
            functools.partial(look_kernel, dims, parts, levels, level),
            found_shapes + ((struct(*table_shape, dtype=F8),) if level == 0 else ()),
            (() if level else (pltpu.VMEM((3, width_y // lanes, cells, lanes), F32),))
            + (pltpu.VMEM((parts, width_y, slabs * lanes), F8),),
            cost=LOOK_COST,
        )(codes, runs, *((table, total) if level else (factors,)))
        if level == 0:
            table = outs[3]
        found.append(outs[:3])
        pieces.append(other)
        if level < levels - 1:
            last = level == levels - 2
            total = call(
                functools.partial(merge_kernel, level, last),
                struct(2 if last else 5, width_x, width_y),
            )(total, other, outs[1])
    edges, reply = call(
        functools.partial(join_kernel, dims, parts, levels),
        (struct(2, width_x, width_y), struct(slabs, rows, lanes)),
        (
            pltpu.VMEM((levels * parts, slabs, lanes), F32),
            pltpu.VMEM((parts, slabs, 2 * rows + 8 * levels, lanes), F32),
        ),
    )(runs, *pieces, *(phase[i] for i in range(3) for phase in found))
    returned = lax.all_to_all(reply, "gz", split_axis=0, concat_axis=0, tiled=True)
    new_velocity, new_temp = call(
        functools.partial(kick_kernel, parts),
        (struct(*atom_velocity.shape), struct(*dims)),
        (
            pltpu.VMEM(atom_velocity.shape, F32),
            pltpu.VMEM(dims, F32),
            pltpu.SemaphoreType.DMA((4,)),
        ),
        outs=(pltpu.HBM, pltpu.HBM),
    )(
        returned.reshape(slabs * rows, lanes), spots, meta, starts, base, push, factors,
        edges,
    )
    return (new_temp, new_velocity)


def solution(mesh):
    placed = (
        P(None, ("gz", "gx"), None),
        P(None, ("gz", "gx"), None),
        P(("gz", "gx"), None),
        P(("gz", "gx"), None),
        P(("gz", "gx")),
        P("gz", "gx", None),
    )
    return jax.shard_map(
        body,
        mesh=mesh,
        in_specs=placed,
        out_specs=(P("gz", "gx", None), P(None, ("gz", "gx"), None)),
        check_vma=False,
    )
```

```python
import functools

import jax
import jax.numpy as jnp
from jax import lax
from jax.experimental import pallas as pl
from jax.experimental.pallas import tpu as pltpu
from jax.sharding import PartitionSpec as P

STIFFNESS = 10000.0
LATERAL = 0.1
COUPLE = 0.5
TWO_THIRDS = 2.0 / 3.0
KICK_RATE = 0.2
F32 = jnp.float32
BF16 = jnp.bfloat16
F8 = jnp.float8_e4m3fn
SCALE = 8.0
STEP = 16.0
PIECES = 3
PARTS = 4
ROUTE_LIMIT = 32 * 1024 * 1024
VMEM_LIMIT = 32 * 1024 * 1024
LOOK_COST = pl.CostEstimate(flops=2 * 10**9, bytes_accessed=10**7, transcendentals=0)


def quotient(value, size):
    if size & (size - 1) == 0:
        return lax.shift_right_logical(value, size.bit_length() - 1)
    return value // size


def iota(shape, dim):
    return lax.broadcasted_iota(jnp.int32, shape, dim)


def split(value, pieces):
    parts = []
    for _ in range(pieces):
        part = value.astype(BF16)
        parts.append(part)
        value = value - part.astype(F32)
    return parts


def split_small(value):
    value = value * SCALE
    parts = []
    for _ in range(PIECES):
        part = value.astype(F8)
        parts.append(part)
        value = (value - part.astype(F32)) * STEP
    return parts


def join_small(parts):
    total = parts[-1]
    for part in parts[-2::-1]:
        total = part + total * (1.0 / STEP)
    return total * (1.0 / SCALE)


def merge(left, right):
    g_a, sl_a, rl_a, s_a, r_a = left
    g_b, sl_b, rl_b, s_b, r_b = right
    excess = s_a + sl_b
    source = r_a + rl_b
    inverse = 1.0 / (g_a + g_b + excess)
    to_left = g_a * inverse
    to_right = g_b * inverse
    return (
        g_a * to_right,
        sl_a + to_left * excess,
        rl_a + to_left * source,
        s_b + to_right * excess,
        r_b + to_right * source,
    )


def prefix_step(state, segment):
    gate, sl, rl, s, r = segment
    excess = state[0] + sl
    source = state[1] + rl
    ratio = gate / (gate + excess)
    return (s + ratio * excess, r + ratio * source)


def suffix_step(state, segment):
    gate, sl, rl, s, r = segment
    excess = s + state[0]
    source = r + state[1]
    ratio = gate / (gate + excess)
    return (sl + ratio * excess, rl + ratio * source)


def route_kernel(
    dims, slabs, rows, parts, count_hbm, velocity_hbm, plane_hbm, column_hbm, send, meta, starts,
    velocity, plane, column, count, arrived,
):
    copies = [
        pltpu.make_async_copy(source, target, arrived.at[i])
        for i, (source, target) in enumerate(
            (
                (count_hbm, count),
                (plane_hbm, plane),
                (column_hbm, column),
                (velocity_hbm, velocity),
            )
        )
    ]
    for copy in copies:
        copy.start()
    planes, width_x, width_y = dims
    bricks, lanes = plane.shape
    part_rows = planes * width_x // parts
    lane = iota((bricks, lanes), 1)
    sub_b = iota((bricks, bricks), 0)
    lane_b = iota((bricks, bricks), 1)
    eye = sub_b == lane_b
    sub_l = iota((lanes, lanes), 0)
    lane_l = iota((lanes, lanes), 1)
    prefix = jnp.concatenate(
        [jnp.where(sub_l <= lane_l, 1.0, 0.0), jnp.ones((lanes, lanes), F32)], axis=1
    ).astype(BF16)
    copies[0].wait()
    count_row = jnp.broadcast_to(count[...].astype(F32), (bricks, bricks))
    count_col = jnp.sum(jnp.where(eye, count_row, 0.0), axis=1, keepdims=True).astype(jnp.int32)
    in_use = lane < count_col
    copies[1].wait()
    owner = quotient(plane[:, 0:1], planes)
    owner_f = jnp.broadcast_to(owner.astype(F32), (bricks, bricks))
    owner_row = jnp.sum(jnp.where(eye, owner_f, 0.0), axis=0, keepdims=True)
    same = owner_f == owner_row
    ahead = same & (lane_b < sub_b)
    peers = jnp.where(jnp.concatenate([same, ahead], axis=0), 1.0, 0.0).astype(BF16)
    copies[2].wait()
    col = column[...]
    x_cell = quotient(col, width_y)
    y_cell = col - x_cell * width_y
    row = x_cell * planes + plane[...] - owner * planes
    code = jnp.where(in_use, (row + 1) * width_y + y_cell, 0)
    part = jnp.where(in_use, quotient(row, part_rows), parts)
    inside = [jnp.where(part == c, 1.0, 0.0).astype(BF16) for c in range(parts)]
    sums = jnp.dot(jnp.concatenate(inside, axis=0), prefix, preferred_element_type=F32)
    ranks = [sums[c * bricks : (c + 1) * bricks, :lanes] for c in range(parts)]
    sizes = [sums[c * bricks : (c + 1) * bricks, lanes:] for c in range(parts)]
    earlier = [jnp.zeros_like(sizes[0])]
    for c in range(parts - 1):
        earlier.append(earlier[-1] + sizes[c])
    joint = jnp.dot(
        peers, jnp.concatenate(sizes, axis=1).astype(BF16), preferred_element_type=F32
    )
    copies[3].wait()
    vx, vy, vz = velocity[0], velocity[1], velocity[2]
    kinetic = 0.5 * (vx * vx + vy * vy + vz * vz)
    dense = jnp.zeros((bricks, lanes), F32)
    whole = jnp.zeros((bricks, lanes), F32)
    bases = []
    for c in range(parts):
        bases.append((dense, whole))
        size = joint[:bricks, c * lanes : (c + 1) * lanes]
        dense = dense + size
        whole = whole + jnp.floor((size + (lanes - 1)) * (1.0 / lanes)) * lanes
    begins = [
        owner * (rows * lanes)
        + (
            jnp.where(whole <= rows * lanes, base[1], base[0])
            + joint[bricks:, c * lanes : (c + 1) * lanes]
        ).astype(jnp.int32)
        for c, base in enumerate(bases)
    ]
    shifts = [begin & (lanes - 1) for begin in begins]
    packed = ranks[0].astype(jnp.int32)
    run = jnp.zeros((bricks, lanes), jnp.int32)
    base = jnp.zeros((bricks, lanes), F32)
    lane_f = lane.astype(F32)
    for c in range(1, parts):
        packed = packed | (ranks[c].astype(jnp.int32) << (8 * c))
        run = jnp.where(lane_f >= earlier[c], 8 * c, run)
        base = jnp.where(lane_f >= earlier[c], earlier[c], base)
    wanted = lane - base.astype(jnp.int32)
    found = jnp.zeros((bricks, lanes), jnp.int32)
    step = lanes
    while step > 1:
        ways = 4 if step >= 4 else 2
        step //= ways
        gain = jnp.zeros((bricks, lanes), jnp.int32)
        for way in range(1, ways):
            at = jnp.take_along_axis(packed, found + (way * step - 1), axis=1)
            at = lax.shift_right_logical(at, run) & 255
            gain = jnp.where(at <= wanted, way * step, gain)
        found = found + gain
    kinetic = jnp.take_along_axis(kinetic, found, axis=1)
    code = jnp.take_along_axis(code, found, axis=1)
    zero = jnp.zeros((bricks, lanes), BF16)
    slot = iota((slabs * rows, bricks), 0).astype(F32).astype(BF16)
    values = []
    spots = []
    place = jnp.full((bricks, lanes), -1, jnp.int32)
    table = jnp.zeros((bricks, lanes), jnp.int32)
    for c in range(parts):
        table = jnp.where(lane == c, begins[c], table)
        place = jnp.where(
            part == c, (begins[c] + ranks[c].astype(jnp.int32) - 1) * parts + c, place
        )
        turn = (lane - shifts[c]) & (lanes - 1)
        valid = turn.astype(F32) < sizes[c]
        turn = (turn + earlier[c].astype(jnp.int32)) & (lanes - 1)
        kin = jnp.where(valid, jnp.take_along_axis(kinetic, turn, axis=1), 0.0)
        cell = jnp.where(valid, jnp.take_along_axis(code, turn, axis=1), 0)
        cell_row = quotient(cell, width_y)
        cell_y = cell - cell_row * width_y
        pieces = split(kin, 2) + [cell_row.astype(F32).astype(BF16), cell_y.astype(F32).astype(BF16)]
        first = lane >= shifts[c]
        values.append(jnp.concatenate([jnp.where(first, p, zero) for p in pieces], axis=1))
        values.append(jnp.concatenate([jnp.where(first, zero, p) for p in pieces], axis=1))
        begin_row = jnp.sum(
            jnp.where(eye, begins[c].astype(F32), 0.0), axis=0, keepdims=True
        ).astype(jnp.int32)
        target = quotient(begin_row, lanes).astype(F32)
        spots.append(slot == target.astype(BF16))
        spots.append(slot == (target + 1.0).astype(BF16))
    starts[...] = table
    meta[...] = place
    one = jnp.ones((), BF16)
    moved = jnp.dot(
        jnp.concatenate([jnp.where(spot, one, jnp.zeros((), BF16)) for spot in spots], axis=1),
        jnp.concatenate(values, axis=0),
        preferred_element_type=F32,
    )
    send[:, 0] = (moved[:, :lanes] + moved[:, lanes : 2 * lanes]).reshape(slabs, rows, lanes)
    send[:, 1] = (moved[:, 2 * lanes : 3 * lanes] * width_y + moved[:, 3 * lanes :]).reshape(
        slabs, rows, lanes
    )


def decode(code, width_y):
    row = jnp.floor((code + 0.5) * (1.0 / width_y))
    return row, code - row * width_y


def find_runs(dims, parts, got, runs_vmem):
    planes, width_x, width_y = dims
    slabs, _, rows, lanes = got.shape
    part_rows = planes * width_x // parts
    codes = got[:, 1]
    beyond = float((parts * part_rows + 1) * width_y + 1)
    lead = codes[:, :, 0:1]
    used = lead > 0.0
    lead = jnp.where(used, lead, beyond)
    top = jnp.where(used, jnp.max(codes, axis=2, keepdims=True), beyond)
    longest = jnp.zeros((slabs, 1), F32)
    first = jnp.zeros((slabs, 1), F32)
    table = jnp.zeros((slabs, lanes), F32)
    lane = iota((slabs, lanes), 1)
    for c in range(parts):
        limit = float(((c + 1) * part_rows + 1) * width_y)
        last = jnp.sum(jnp.where(lead < limit, 1.0, 0.0), axis=1)
        longest = jnp.maximum(longest, last - first)
        table = jnp.where(lane == 2 * c, first, table)
        table = jnp.where(lane == 2 * c + 1, last, table)
        first = jnp.sum(jnp.where(top < limit, 1.0, 0.0), axis=1)
    longest = jnp.max(longest, axis=0, keepdims=True)
    runs_vmem[...] = jnp.where(lane == 2 * parts, longest, table).astype(jnp.int32)


def run_row(got, field, s, spot, last):
    rows = got.shape[2]
    loaded = got[s, field, pl.ds(jnp.minimum(spot, rows - 1), 1), :]
    return jnp.where(spot < last, loaded, 0.0)


def bin_kernel(dims, parts, got, _, totals, codes, runs_vmem, lhs, rhs):
    planes, width_x, width_y = dims
    slabs, _, rows, lanes = got.shape
    part_rows = planes * width_x // parts
    find_runs(dims, parts, got, runs_vmem)
    runs = runs_vmem[...]
    first = [[runs[s, 2 * c] for s in range(slabs)] for c in range(parts)]
    last = [[runs[s, 2 * c + 1] for s in range(slabs)] for c in range(parts)]
    longest = runs[0, 2 * parts]
    one = jnp.ones((), F8)
    zero = jnp.zeros((), F8)
    y_id = iota((width_y, lanes), 0).astype(F32).astype(BF16)
    totals[...] = jnp.zeros(totals.shape, F32)

    def add_rows(turn, carry):
        for c in range(parts):
            row_id = (iota((part_rows, lanes), 0) + (c * part_rows + 1)).astype(F32).astype(BF16)
            for s in range(slabs):
                spot = first[c][s] + turn
                pieces = split_small(run_row(got, 0, s, spot, last[c][s]))
                code = run_row(got, 1, s, spot, last[c][s])
                codes[turn * parts + c, pl.ds(s, 1), :] = code
                row, y_cell = decode(code, width_y)
                here = pl.ds(s * lanes, lanes)
                hit = row_id == row.astype(BF16)
                for i, piece in enumerate(pieces):
                    lhs[c, pl.ds(i * part_rows, part_rows), here] = jnp.where(hit, piece, zero)
                lhs[c, pl.ds(PIECES * part_rows, part_rows), here] = jnp.where(hit, one, zero)
                rhs[c, :, here] = jnp.where(y_id == y_cell.astype(BF16), one, zero)
        for c in range(parts):
            added = lax.dot_general(
                lhs[c], rhs[c], (((1,), (1,)), ((), ())), preferred_element_type=F32
            )
            pieces = [added[i * part_rows : (i + 1) * part_rows] for i in range(PIECES + 1)]
            for i, value in enumerate((join_small(pieces[:PIECES]), pieces[PIECES])):
                for h in range(width_y // lanes):
                    totals[i, h, pl.ds(c * part_rows, part_rows), :] += value[
                        :, h * lanes : (h + 1) * lanes
                    ]
        return carry

    lax.fori_loop(0, longest, add_rows, 0)


def solve_kernel(dims, totals, temp, below, x_low, x_high, summary, factors):
    planes, width_x, width_y = dims
    lanes = totals.shape[3]

    def plane_terms(z):
        here = temp[z]
        x_minus = jnp.concatenate([x_low[z], here[:-1]], axis=0)
        x_plus = jnp.concatenate([here[1:], x_high[z]], axis=0)
        lateral = LATERAL * (
            x_minus
            + x_plus
            + pltpu.roll(here, 1, 1)
            + pltpu.roll(here, width_y - 1, 1)
            - 4.0 * here
        )
        at = pl.ds(z, width_x, stride=planes)
        sums = [
            jnp.concatenate([totals[i, h, at, :] for h in range(width_y // lanes)], axis=1)
            for i in range(2)
        ]
        energy, count = sums
        return here + COUPLE * count, here * here + lateral + COUPLE * TWO_THIRDS * energy

    start = temp[0]
    gate = jnp.where(
        lax.axis_index("gz") > 0, STIFFNESS * (0.5 * (start + below[0])), jnp.zeros_like(start)
    )
    excess, source = plane_terms(0)
    left_excess = jnp.zeros_like(start)
    left_source = jnp.zeros_like(start)
    for z in range(planes - 1):
        face = STIFFNESS * (0.5 * (temp[z + 1] + temp[z]))
        inverse = 1.0 / (gate + face + excess)
        to_left = gate * inverse
        to_right = face * inverse
        factors[z, 0] = to_left
        factors[z, 1] = to_right
        factors[z, 2] = source * inverse
        next_excess, next_source = plane_terms(z + 1)
        left_excess = left_excess + to_left * excess
        left_source = left_source + to_left * source
        gate = gate * to_right
        excess = next_excess + to_right * excess
        source = next_source + to_right * source
    for i, value in enumerate((gate, left_excess, left_source, excess, source)):
        summary[i] = value


def load_five(ref):
    return tuple(ref[i] for i in range(5))


def merge_kernel(level, last, mine, other, _, total):
    upper = (lax.axis_index("gz") & (1 << level)) != 0
    own = load_five(mine)
    came = load_five(other)
    low = tuple(jnp.where(upper, b, a) for a, b in zip(own, came))
    high = tuple(jnp.where(upper, a, b) for a, b in zip(own, came))
    joined = merge(low, high)
    if not last:
        for i in range(5):
            total[i] = joined[i]
        return
    in_upper = (lax.axis_index("gz") & (1 << (level + 1))) != 0
    end = jnp.zeros_like(joined[0])
    closed = suffix_step((end, end), joined)
    total[0] = jnp.where(in_upper, closed[0], joined[3])
    total[1] = jnp.where(in_upper, closed[1], joined[4])


def table_kernel(dims, parts, factors, table, spread):
    planes, width_x, width_y = dims
    part_rows = planes * width_x // parts
    lanes = spread.shape[3]
    zeros = jnp.zeros((width_x, width_y), F32)
    state = (zeros, zeros, zeros + 1.0)
    for z in range(planes - 1, -1, -1):
        if z < planes - 1:
            to_left, to_right, fixed = factors[z, 0], factors[z, 1], factors[z, 2]
            state = (
                fixed + to_right * state[0],
                to_left + to_right * state[1],
                to_right * state[2],
            )
        for t in range(3):
            for h in range(spread.shape[1]):
                spread[t, h, pl.ds(z, width_x, stride=planes), :] = state[t][
                    :, h * lanes : (h + 1) * lanes
                ]
    for c in range(parts):
        for t in range(3):
            for h in range(spread.shape[1]):
                block = spread[t, h, pl.ds(c * part_rows, part_rows), :]
                for i, piece in enumerate(split_small(block)):
                    at = pl.ds((t * PIECES + i) * part_rows, part_rows)
                    table[c, at, pl.ds(h * lanes, lanes)] = piece


def look_kernel(dims, parts, levels, phase, codes, runs, *refs):
    if phase == 0:
        factors, found, keys, spots, table, spread, rhs = refs
        table_kernel(dims, parts, factors, table, spread)
    else:
        table, _, found, keys, spots, rhs = refs
    planes, width_x, width_y = dims
    _, slabs, lanes = codes.shape
    part_rows = planes * width_x // parts
    halves = width_y // lanes
    one = jnp.ones((), F8)
    zero = jnp.zeros((), F8)
    y_id = iota((width_y, lanes), 0).astype(F32).astype(BF16)
    order = levels - 1 - phase
    turns = runs[0:1, :][0, 2 * parts]

    def find_rows(step, carry):
        wanted = []
        for c in range(parts):
            block = step * parts + c
            row, y_cell = decode(codes[(step * levels + order) * parts + c], width_y)
            wanted.append(row)
            hot = y_cell.astype(BF16)
            for s in range(slabs):
                rhs[c, :, pl.ds(s * lanes, lanes)] = jnp.where(
                    y_id == hot[s : s + 1], one, zero
                )
            x_cell = jnp.floor((row - (c * part_rows + 0.5)) * (1.0 / planes))
            half = jnp.floor((y_cell + 0.5) * (1.0 / lanes))
            keys[block] = jnp.where(row > c * part_rows, x_cell * halves + half, -1.0)
            spots[block] = (y_cell - half * lanes).astype(jnp.int32)
        for c in range(parts):
            block = step * parts + c
            row_id = (iota((part_rows, lanes), 0) + (c * part_rows + 1)).astype(F32)
            picked = jnp.dot(table[c], rhs[c], preferred_element_type=F32)
            for s in range(slabs):
                hit = row_id == wanted[c][s : s + 1]
                for t in range(3):
                    pieces = [
                        picked[
                            (t * PIECES + i) * part_rows : (t * PIECES + i + 1) * part_rows,
                            s * lanes : (s + 1) * lanes,
                        ]
                        for i in range(PIECES)
                    ]
                    total = pieces[-1]
                    for piece in pieces[-2::-1]:
                        total = piece + total * (1.0 / STEP)
                    chosen = jnp.sum(jnp.where(hit, total, 0.0), axis=0, keepdims=True)
                    found[t, block, pl.ds(s, 1), :] = chosen * (1.0 / SCALE)
        return carry

    lax.fori_loop(0, quotient_up(turns - order, levels), find_rows, 0)


def quotient_up(value, size):
    return (value + (size - 1)) // size


def join_kernel(dims, parts, levels, runs_vmem, *refs):
    planes, width_x, width_y = dims
    own = load_five(refs[0])
    others = refs[1:levels]
    far = refs[levels]
    found = refs[levels + 1 : 2 * levels + 1]
    keys = refs[2 * levels + 1 : 3 * levels + 1]
    lane_of = refs[3 * levels + 1 : 4 * levels + 1]
    edges, reply, temps, spread = refs[4 * levels + 1 :]
    slabs, rows, lanes = reply.shape
    part_x = width_x // parts
    halves = width_y // lanes
    runs = runs_vmem[...]
    first = [[runs[s, 2 * c] for s in range(slabs)] for c in range(parts)]
    longest = runs[0, 2 * parts]
    spread[:, :, pl.ds(0, rows), :] = jnp.zeros((parts, slabs, rows, lanes), F32)
    index = lax.axis_index("gz")
    zeros = jnp.zeros_like(own[0])
    top = (index & (1 << (levels - 1))) != 0
    before = (jnp.where(top, far[0], zeros + 1.0), jnp.where(top, far[1], zeros))
    after = (jnp.where(top, zeros, far[0]), jnp.where(top, zeros, far[1]))
    for level in range(levels - 2, -1, -1):
        upper = (index & (1 << level)) != 0
        segment = load_five(others[level])
        with_before = prefix_step(before, segment)
        with_after = suffix_step(after, segment)
        before = tuple(jnp.where(upper, a, b) for a, b in zip(with_before, before))
        after = tuple(jnp.where(upper, b, a) for a, b in zip(with_after, after))
    through = prefix_step(before, own)
    value = (through[1] + after[1]) / (through[0] + after[0])
    edges[0] = (before[1] + own[2] + own[0] * value) / (before[0] + own[1] + own[0])
    edges[1] = value

    def fill_rows(step, carry):
        for phase in range(levels):
            done = step * levels + (levels - 1 - phase) < longest
            for c in range(parts):
                block = step * parts + c
                key = keys[phase][block]
                lane = lane_of[phase][block] & (lanes - 1)
                ends = [jnp.zeros((slabs, lanes), F32), jnp.zeros((slabs, lanes), F32)]
                for x in range(part_x):
                    for h in range(halves):
                        hit = key == float(x * halves + h)
                        for e in range(2):
                            line = edges[e, pl.ds(c * part_x + x, 1), pl.ds(h * lanes, lanes)]
                            line = jnp.broadcast_to(line, (slabs, lanes))
                            ends[e] = jnp.where(
                                hit, jnp.take_along_axis(line, lane, axis=1), ends[e]
                            )
                temps[phase * parts + c] = jnp.where(
                    done,
                    found[phase][0, block]
                    + found[phase][1, block] * ends[0]
                    + found[phase][2, block] * ends[1],
                    0.0,
                )
        for phase in range(levels):
            for c in range(parts):
                for s in range(slabs):
                    spot = first[c][s] + step * levels + (levels - 1 - phase)
                    spread[c, s, pl.ds(spot, 1), :] = temps[phase * parts + c, pl.ds(s, 1), :]
        return carry

    lax.fori_loop(0, quotient_up(longest, levels), fill_rows, 0)
    total = spread[0, :, pl.ds(0, rows), :]
    for c in range(1, parts):
        total = total + spread[c, :, pl.ds(0, rows), :]
    reply[...] = total


def fill_planes(factors, edges, new_temp):
    planes = new_temp.shape[0]
    edge = edges[0]
    value = edges[1]
    new_temp[planes - 1] = value
    for z in range(planes - 2, -1, -1):
        value = factors[z, 2] + factors[z, 0] * edge + factors[z, 1] * value
        new_temp[z] = value


def spot_kernel(parts, slots, lanes, starts, meta, velocity, noise, spots, base, push):
    in_use = meta[...] >= 0
    for i in range(3):
        base[i] = jnp.where(in_use, (1.0 - KICK_RATE) * velocity[i], 0.0)
        push[i] = jnp.where(in_use, noise[i], 0.0)
    bricks = starts.shape[0]
    slot = iota((bricks, slots), 1).astype(F32).astype(BF16)
    one = jnp.ones((), BF16)
    zero = jnp.zeros((), BF16)
    for c in range(parts):
        begin = jnp.broadcast_to(starts[:, c : c + 1], (bricks, slots))
        target = quotient(begin, lanes).astype(F32)
        for i in range(2):
            at = pl.ds((2 * c + i) * bricks, bricks)
            spots[at, :] = jnp.where(slot == (target + float(i)).astype(BF16), one, zero)


def kick_kernel(
    parts, returned, spots, meta, starts, base, push, factors, edges,
    out, new_temp, kicked, filled, left,
):
    fill_planes(factors, edges, filled)
    copies = [pltpu.make_async_copy(filled, new_temp, left.at[3])]
    copies[0].start()
    bricks, lanes = meta.shape
    packed = meta[...]
    lane = iota((bricks, lanes), 1)
    in_use = packed >= 0
    place = quotient(jnp.maximum(packed, 0), parts)
    part = jnp.maximum(packed, 0) - place * parts
    values = jnp.concatenate(split(returned[...], 2), axis=1)
    moved = jnp.dot(spots[...], values, preferred_element_type=F32)
    moved = moved[:, :lanes] + moved[:, lanes:]
    at = place & (lanes - 1)
    temp = jnp.zeros((bricks, lanes), F32)
    for c in range(parts):
        shift = jnp.broadcast_to(starts[:, c : c + 1], (bricks, lanes)) & (lanes - 1)
        here = moved[2 * c * bricks : (2 * c + 1) * bricks]
        after = moved[(2 * c + 1) * bricks : (2 * c + 2) * bricks]
        whole = jnp.where(lane >= shift, here, after)
        temp = jnp.where(part == c, jnp.take_along_axis(whole, at, axis=1), temp)
    root = jnp.where(in_use, jnp.sqrt(2.0 * KICK_RATE * temp), 0.0)
    for i in range(3):
        kicked[i] = base[i] + root * push[i]
        copies.append(pltpu.make_async_copy(kicked.at[i], out.at[i], left.at[i]))
        copies[-1].start()
    for copy in copies:
        copy.wait()


def call(kernel, out_shape, scratch=(), spaces=None, limit=VMEM_LIMIT, cost=None, outs=None):
    extra = {} if cost is None else {"cost_estimate": cost}
    if spaces is not None:
        extra["in_specs"] = [pl.BlockSpec(memory_space=m) for m in spaces]
    if outs is not None:
        extra["out_specs"] = tuple(pl.BlockSpec(memory_space=m) for m in outs)
    return pl.pallas_call(
        kernel,
        out_shape=out_shape,
        **extra,
        scratch_shapes=list(scratch),
        compiler_params=pltpu.CompilerParams(vmem_limit_bytes=limit),
    )


def struct(*shape, dtype=F32):
    return jax.ShapeDtypeStruct(shape, dtype)


def route_call(dims, slabs, rows, parts, velocity_shape, plane_shape):
    bricks, lanes = plane_shape
    return call(
        functools.partial(route_kernel, dims, slabs, rows, parts),
        (
            struct(slabs, 2, rows, lanes),
            struct(bricks, lanes, dtype=jnp.int32),
            struct(bricks, lanes, dtype=jnp.int32),
        ),
        (
            pltpu.VMEM(velocity_shape, F32),
            pltpu.VMEM(plane_shape, jnp.int32),
            pltpu.VMEM(plane_shape, jnp.int32),
            pltpu.VMEM((1, bricks), jnp.int32),
            pltpu.SemaphoreType.DMA((4,)),
        ),
        (pltpu.HBM,) * 4,
        ROUTE_LIMIT,
    )


def body(atom_velocity, atom_noise, atom_plane, atom_column, brick_count, electron_temp):
    dims = electron_temp.shape
    planes, width_x, width_y = dims
    cells = planes * width_x
    slabs = lax.axis_size("gz")
    groups = lax.axis_size("gx")
    levels = slabs.bit_length() - 1
    assert slabs == 1 << levels and levels > 0
    bricks, lanes = atom_plane.shape
    rows = 2 * bricks // slabs
    parts = PARTS
    assert width_x % parts == 0 and parts <= 4 and lanes <= 128
    send, meta, starts = route_call(
        dims, slabs, rows, parts, atom_velocity.shape, atom_plane.shape
    )(
        *(
            pltpu.with_memory_space_constraint(x, pltpu.HBM)
            for x in (brick_count.reshape(1, bricks), atom_velocity, atom_plane, atom_column)
        )
    )
    spots, base, push = call(
        functools.partial(spot_kernel, parts, slabs * rows, lanes),
        (
            struct(2 * parts * bricks, slabs * rows, dtype=BF16),
            struct(*atom_velocity.shape),
            struct(*atom_noise.shape),
        ),
    )(starts, meta, atom_velocity, atom_noise)
    got = lax.all_to_all(send, "gz", split_axis=0, concat_axis=0, tiled=True)
    below = lax.ppermute(electron_temp[-1:], "gz", [(i, i + 1) for i in range(slabs - 1)])
    x_low = lax.ppermute(
        electron_temp[:, -1:], "gx", [(i, (i + 1) % groups) for i in range(groups)]
    )
    x_high = lax.ppermute(
        electron_temp[:, :1], "gx", [((i + 1) % groups, i) for i in range(groups)]
    )
    totals, codes, runs = call(
        functools.partial(bin_kernel, dims, parts),
        (
            struct(2, width_y // lanes, cells, lanes),
            struct(parts * (rows + 1), slabs, lanes),
            struct(slabs, lanes, dtype=jnp.int32),
        ),
        (
            pltpu.VMEM((parts, (PIECES + 1) * cells // parts, slabs * lanes), F8),
            pltpu.VMEM((parts, width_y, slabs * lanes), F8),
        ),
    )(got, spots)
    total, factors = call(
        functools.partial(solve_kernel, dims),
        (struct(5, width_x, width_y), struct(planes - 1, 3, width_x, width_y)),
    )(totals, electron_temp, below, x_low, x_high)
    blocks = parts * quotient_up(rows, levels)
    found_shapes = (
        struct(3, blocks, slabs, lanes),
        struct(blocks, slabs, lanes),
        struct(blocks, slabs, lanes, dtype=jnp.int32),
    )
    table_shape = (parts, 3 * PIECES * cells // parts, width_y)
    pieces = [total]
    found = []
    for level in range(levels):
        other = lax.ppermute(total, "gz", [(i, i ^ (1 << level)) for i in range(slabs)])
        outs = call(
            functools.partial(look_kernel, dims, parts, levels, level),
            found_shapes + ((struct(*table_shape, dtype=F8),) if level == 0 else ()),
            (() if level else (pltpu.VMEM((3, width_y // lanes, cells, lanes), F32),))
            + (pltpu.VMEM((parts, width_y, slabs * lanes), F8),),
            cost=LOOK_COST,
        )(codes, runs, *((table, total) if level else (factors,)))
        if level == 0:
            table = outs[3]
        found.append(outs[:3])
        pieces.append(other)
        if level < levels - 1:
            last = level == levels - 2
            total = call(
                functools.partial(merge_kernel, level, last),
                struct(2 if last else 5, width_x, width_y),
            )(total, other, outs[1])
    edges, reply = call(
        functools.partial(join_kernel, dims, parts, levels),
        (struct(2, width_x, width_y), struct(slabs, rows, lanes)),
        (
            pltpu.VMEM((levels * parts, slabs, lanes), F32),
            pltpu.VMEM((parts, slabs, 2 * rows + 8 * levels, lanes), F32),
        ),
    )(runs, *pieces, *(phase[i] for i in range(3) for phase in found))
    returned = lax.all_to_all(reply, "gz", split_axis=0, concat_axis=0, tiled=True)
    new_velocity, new_temp = call(
        functools.partial(kick_kernel, parts),
        (struct(*atom_velocity.shape), struct(*dims)),
        (
            pltpu.VMEM(atom_velocity.shape, F32),
            pltpu.VMEM(dims, F32),
            pltpu.SemaphoreType.DMA((4,)),
        ),
        outs=(pltpu.HBM, pltpu.HBM),
    )(
        returned.reshape(slabs * rows, lanes), spots, meta, starts, base, push, factors,
        edges,
    )
    return (new_temp, new_velocity)


def solution(mesh):
    placed = (
        P(None, ("gz", "gx"), None),
        P(None, ("gz", "gx"), None),
        P(("gz", "gx"), None),
        P(("gz", "gx"), None),
        P(("gz", "gx")),
        P("gz", "gx", None),
    )
    return jax.shard_map(
        body,
        mesh=mesh,
        in_specs=placed,
        out_specs=(P("gz", "gx", None), P(None, ("gz", "gx"), None)),
        check_vma=False,
    )
```

```python
import functools

import jax
import jax.numpy as jnp
from jax import lax
from jax.experimental import pallas as pl
from jax.experimental.pallas import tpu as pltpu
from jax.sharding import PartitionSpec as P

STIFFNESS = 10000.0
LATERAL = 0.1
COUPLE = 0.5
TWO_THIRDS = 2.0 / 3.0
KICK_RATE = 0.2
F32 = jnp.float32
BF16 = jnp.bfloat16
F8 = jnp.float8_e4m3fn
SCALE = 8.0
STEP = 16.0
PIECES = 3
PARTS = 4
AT_ONCE = 3
ROUTE_LIMIT = 32 * 1024 * 1024
VMEM_LIMIT = 32 * 1024 * 1024
LOOK_COST = pl.CostEstimate(flops=2 * 10**9, bytes_accessed=10**7, transcendentals=0)


def quotient(value, size):
    if size & (size - 1) == 0:
        return lax.shift_right_logical(value, size.bit_length() - 1)
    return value // size


def iota(shape, dim):
    return lax.broadcasted_iota(jnp.int32, shape, dim)


def split(value, pieces):
    parts = []
    for _ in range(pieces):
        part = value.astype(BF16)
        parts.append(part)
        value = value - part.astype(F32)
    return parts


def split_small(value):
    value = value * SCALE
    parts = []
    for _ in range(PIECES):
        part = value.astype(F8)
        parts.append(part)
        value = (value - part.astype(F32)) * STEP
    return parts


def join_small(parts):
    total = parts[-1]
    for part in parts[-2::-1]:
        total = part + total * (1.0 / STEP)
    return total * (1.0 / SCALE)


def merge(left, right):
    g_a, sl_a, rl_a, s_a, r_a = left
    g_b, sl_b, rl_b, s_b, r_b = right
    excess = s_a + sl_b
    source = r_a + rl_b
    inverse = 1.0 / (g_a + g_b + excess)
    to_left = g_a * inverse
    to_right = g_b * inverse
    return (
        g_a * to_right,
        sl_a + to_left * excess,
        rl_a + to_left * source,
        s_b + to_right * excess,
        r_b + to_right * source,
    )


def prefix_step(state, segment):
    gate, sl, rl, s, r = segment
    excess = state[0] + sl
    source = state[1] + rl
    ratio = gate / (gate + excess)
    return (s + ratio * excess, r + ratio * source)


def suffix_step(state, segment):
    gate, sl, rl, s, r = segment
    excess = s + state[0]
    source = r + state[1]
    ratio = gate / (gate + excess)
    return (sl + ratio * excess, rl + ratio * source)


def route_kernel(
    dims, slabs, rows, parts, count_hbm, velocity_hbm, plane_hbm, column_hbm, send, meta, starts,
    velocity, plane, column, count, arrived,
):
    copies = [
        pltpu.make_async_copy(source, target, arrived.at[i])
        for i, (source, target) in enumerate(
            (
                (count_hbm, count),
                (plane_hbm, plane),
                (column_hbm, column),
                (velocity_hbm, velocity),
            )
        )
    ]
    for copy in copies:
        copy.start()
    planes, width_x, width_y = dims
    bricks, lanes = plane.shape
    part_rows = planes * width_x // parts
    lane = iota((bricks, lanes), 1)
    sub_b = iota((bricks, bricks), 0)
    lane_b = iota((bricks, bricks), 1)
    eye = sub_b == lane_b
    sub_l = iota((lanes, lanes), 0)
    lane_l = iota((lanes, lanes), 1)
    prefix = jnp.concatenate(
        [jnp.where(sub_l <= lane_l, 1.0, 0.0), jnp.ones((lanes, lanes), F32)], axis=1
    ).astype(BF16)
    copies[0].wait()
    count_row = jnp.broadcast_to(count[...].astype(F32), (bricks, bricks))
    count_col = jnp.sum(jnp.where(eye, count_row, 0.0), axis=1, keepdims=True).astype(jnp.int32)
    in_use = lane < count_col
    copies[1].wait()
    owner = quotient(plane[:, 0:1], planes)
    owner_f = jnp.broadcast_to(owner.astype(F32), (bricks, bricks))
    owner_row = jnp.sum(jnp.where(eye, owner_f, 0.0), axis=0, keepdims=True)
    same = owner_f == owner_row
    ahead = same & (lane_b < sub_b)
    peers = jnp.where(jnp.concatenate([same, ahead], axis=0), 1.0, 0.0).astype(BF16)
    copies[2].wait()
    col = column[...]
    x_cell = quotient(col, width_y)
    y_cell = col - x_cell * width_y
    row = x_cell * planes + plane[...] - owner * planes
    code = jnp.where(in_use, (row + 1) * width_y + y_cell, 0)
    part = jnp.where(in_use, quotient(row, part_rows), parts)
    inside = [jnp.where(part == c, 1.0, 0.0).astype(BF16) for c in range(parts)]
    sums = jnp.dot(jnp.concatenate(inside, axis=0), prefix, preferred_element_type=F32)
    ranks = [sums[c * bricks : (c + 1) * bricks, :lanes] for c in range(parts)]
    sizes = [sums[c * bricks : (c + 1) * bricks, lanes:] for c in range(parts)]
    earlier = [jnp.zeros_like(sizes[0])]
    for c in range(parts - 1):
        earlier.append(earlier[-1] + sizes[c])
    joint = jnp.dot(
        peers, jnp.concatenate(sizes, axis=1).astype(BF16), preferred_element_type=F32
    )
    copies[3].wait()
    vx, vy, vz = velocity[0], velocity[1], velocity[2]
    kinetic = 0.5 * (vx * vx + vy * vy + vz * vz)
    dense = jnp.zeros((bricks, lanes), F32)
    whole = jnp.zeros((bricks, lanes), F32)
    bases = []
    for c in range(parts):
        bases.append((dense, whole))
        size = joint[:bricks, c * lanes : (c + 1) * lanes]
        dense = dense + size
        whole = whole + jnp.floor((size + (lanes - 1)) * (1.0 / lanes)) * lanes
    begins = [
        owner * (rows * lanes)
        + (
            jnp.where(whole <= rows * lanes, base[1], base[0])
            + joint[bricks:, c * lanes : (c + 1) * lanes]
        ).astype(jnp.int32)
        for c, base in enumerate(bases)
    ]
    shifts = [begin & (lanes - 1) for begin in begins]
    packed = ranks[0].astype(jnp.int32)
    run = jnp.zeros((bricks, lanes), jnp.int32)
    base = jnp.zeros((bricks, lanes), F32)
    lane_f = lane.astype(F32)
    for c in range(1, parts):
        packed = packed | (ranks[c].astype(jnp.int32) << (8 * c))
        run = jnp.where(lane_f >= earlier[c], 8 * c, run)
        base = jnp.where(lane_f >= earlier[c], earlier[c], base)
    wanted = lane - base.astype(jnp.int32)
    found = jnp.zeros((bricks, lanes), jnp.int32)
    step = lanes
    while step > 1:
        ways = 4 if step >= 4 else 2
        step //= ways
        gain = jnp.zeros((bricks, lanes), jnp.int32)
        for way in range(1, ways):
            at = jnp.take_along_axis(packed, found + (way * step - 1), axis=1)
            at = lax.shift_right_logical(at, run) & 255
            gain = jnp.where(at <= wanted, way * step, gain)
        found = found + gain
    kinetic = jnp.take_along_axis(kinetic, found, axis=1)
    code = jnp.take_along_axis(code, found, axis=1)
    zero = jnp.zeros((bricks, lanes), BF16)
    slot = iota((slabs * rows, bricks), 0).astype(F32).astype(BF16)
    values = []
    spots = []
    place = jnp.full((bricks, lanes), -1, jnp.int32)
    table = jnp.zeros((bricks, lanes), jnp.int32)
    for c in range(parts):
        table = jnp.where(lane == c, begins[c], table)
        place = jnp.where(
            part == c, (begins[c] + ranks[c].astype(jnp.int32) - 1) * parts + c, place
        )
        turn = (lane - shifts[c]) & (lanes - 1)
        valid = turn.astype(F32) < sizes[c]
        turn = (turn + earlier[c].astype(jnp.int32)) & (lanes - 1)
        kin = jnp.where(valid, jnp.take_along_axis(kinetic, turn, axis=1), 0.0)
        cell = jnp.where(valid, jnp.take_along_axis(code, turn, axis=1), 0)
        cell_row = quotient(cell, width_y)
        cell_y = cell - cell_row * width_y
        pieces = split(kin, 2) + [cell_row.astype(F32).astype(BF16), cell_y.astype(F32).astype(BF16)]
        first = lane >= shifts[c]
        values.append(jnp.concatenate([jnp.where(first, p, zero) for p in pieces], axis=1))
        values.append(jnp.concatenate([jnp.where(first, zero, p) for p in pieces], axis=1))
        begin_row = jnp.sum(
            jnp.where(eye, begins[c].astype(F32), 0.0), axis=0, keepdims=True
        ).astype(jnp.int32)
        target = quotient(begin_row, lanes).astype(F32)
        spots.append(slot == target.astype(BF16))
        spots.append(slot == (target + 1.0).astype(BF16))
    starts[...] = table
    meta[...] = place
    one = jnp.ones((), BF16)
    moved = jnp.dot(
        jnp.concatenate([jnp.where(spot, one, jnp.zeros((), BF16)) for spot in spots], axis=1),
        jnp.concatenate(values, axis=0),
        preferred_element_type=F32,
    )
    send[:, 0] = (moved[:, :lanes] + moved[:, lanes : 2 * lanes]).reshape(slabs, rows, lanes)
    send[:, 1] = (moved[:, 2 * lanes : 3 * lanes] * width_y + moved[:, 3 * lanes :]).reshape(
        slabs, rows, lanes
    )


def decode(code, width_y):
    row = jnp.floor((code + 0.5) * (1.0 / width_y))
    return row, code - row * width_y


def find_runs(dims, parts, got, runs_vmem):
    planes, width_x, width_y = dims
    slabs, _, rows, lanes = got.shape
    part_rows = planes * width_x // parts
    codes = got[:, 1]
    beyond = float((parts * part_rows + 1) * width_y + 1)
    lead = codes[:, :, 0:1]
    used = lead > 0.0
    lead = jnp.where(used, lead, beyond)
    top = jnp.where(used, jnp.max(codes, axis=2, keepdims=True), beyond)
    longest = jnp.zeros((slabs, 1), F32)
    first = jnp.zeros((slabs, 1), F32)
    table = jnp.zeros((slabs, lanes), F32)
    lane = iota((slabs, lanes), 1)
    for c in range(parts):
        limit = float(((c + 1) * part_rows + 1) * width_y)
        last = jnp.sum(jnp.where(lead < limit, 1.0, 0.0), axis=1)
        longest = jnp.maximum(longest, last - first)
        table = jnp.where(lane == 2 * c, first, table)
        table = jnp.where(lane == 2 * c + 1, last, table)
        first = jnp.sum(jnp.where(top < limit, 1.0, 0.0), axis=1)
    longest = jnp.max(longest, axis=0, keepdims=True)
    runs_vmem[...] = jnp.where(lane == 2 * parts, longest, table).astype(jnp.int32)


def run_row(got, field, s, spot, last):
    rows = got.shape[2]
    loaded = got[s, field, pl.ds(jnp.minimum(spot, rows - 1), 1), :]
    return jnp.where(spot < last, loaded, 0.0)


def bin_kernel(dims, parts, got, _, totals, codes, runs_vmem, lhs, rhs):
    planes, width_x, width_y = dims
    slabs, _, rows, lanes = got.shape
    part_rows = planes * width_x // parts
    find_runs(dims, parts, got, runs_vmem)
    runs = runs_vmem[...]
    first = [[runs[s, 2 * c] for s in range(slabs)] for c in range(parts)]
    last = [[runs[s, 2 * c + 1] for s in range(slabs)] for c in range(parts)]
    longest = runs[0, 2 * parts]
    one = jnp.ones((), F8)
    zero = jnp.zeros((), F8)
    y_id = iota((width_y, lanes), 0).astype(F32).astype(BF16)
    totals[...] = jnp.zeros(totals.shape, F32)

    def add_rows(begin, at_once):
        for c in range(parts):
            row_id = (iota((part_rows, lanes), 0) + (c * part_rows + 1)).astype(F32).astype(BF16)
            for i in range(at_once * slabs):
                s = i % slabs
                turn = begin + i // slabs
                spot = first[c][s] + turn
                pieces = split_small(run_row(got, 0, s, spot, last[c][s]))
                code = run_row(got, 1, s, spot, last[c][s])
                codes[turn * parts + c, pl.ds(s, 1), :] = code
                row, y_cell = decode(code, width_y)
                here = pl.ds(i * lanes, lanes)
                hit = row_id == row.astype(BF16)
                for j, piece in enumerate(pieces):
                    lhs[c, pl.ds(j * part_rows, part_rows), here] = jnp.where(hit, piece, zero)
                lhs[c, pl.ds(PIECES * part_rows, part_rows), here] = jnp.where(hit, one, zero)
                rhs[c, :, here] = jnp.where(y_id == y_cell.astype(BF16), one, zero)
        for c in range(parts):
            width = pl.ds(0, at_once * slabs * lanes)
            added = lax.dot_general(
                lhs[c, :, width],
                rhs[c, :, width],
                (((1,), (1,)), ((), ())),
                preferred_element_type=F32,
            )
            pieces = [added[i * part_rows : (i + 1) * part_rows] for i in range(PIECES + 1)]
            for i, value in enumerate((join_small(pieces[:PIECES]), pieces[PIECES])):
                for h in range(width_y // lanes):
                    totals[i, h, pl.ds(c * part_rows, part_rows), :] += value[
                        :, h * lanes : (h + 1) * lanes
                    ]

    def many_turns(step, carry):
        add_rows(step * AT_ONCE, AT_ONCE)
        return carry

    def one_turn(turn, carry):
        add_rows(turn, 1)
        return carry

    steps = longest // AT_ONCE
    lax.fori_loop(0, steps, many_turns, 0)
    lax.fori_loop(steps * AT_ONCE, longest, one_turn, 0)


def solve_kernel(dims, totals, temp, below, x_low, x_high, summary, factors):
    planes, width_x, width_y = dims
    lanes = totals.shape[3]

    def plane_terms(z):
        here = temp[z]
        x_minus = jnp.concatenate([x_low[z], here[:-1]], axis=0)
        x_plus = jnp.concatenate([here[1:], x_high[z]], axis=0)
        lateral = LATERAL * (
            x_minus
            + x_plus
            + pltpu.roll(here, 1, 1)
            + pltpu.roll(here, width_y - 1, 1)
            - 4.0 * here
        )
        at = pl.ds(z, width_x, stride=planes)
        sums = [
            jnp.concatenate([totals[i, h, at, :] for h in range(width_y // lanes)], axis=1)
            for i in range(2)
        ]
        energy, count = sums
        return here + COUPLE * count, here * here + lateral + COUPLE * TWO_THIRDS * energy

    start = temp[0]
    gate = jnp.where(
        lax.axis_index("gz") > 0, STIFFNESS * (0.5 * (start + below[0])), jnp.zeros_like(start)
    )
    excess, source = plane_terms(0)
    left_excess = jnp.zeros_like(start)
    left_source = jnp.zeros_like(start)
    for z in range(planes - 1):
        face = STIFFNESS * (0.5 * (temp[z + 1] + temp[z]))
        inverse = 1.0 / (gate + face + excess)
        to_left = gate * inverse
        to_right = face * inverse
        factors[z, 0] = to_left
        factors[z, 1] = to_right
        factors[z, 2] = source * inverse
        next_excess, next_source = plane_terms(z + 1)
        left_excess = left_excess + to_left * excess
        left_source = left_source + to_left * source
        gate = gate * to_right
        excess = next_excess + to_right * excess
        source = next_source + to_right * source
    for i, value in enumerate((gate, left_excess, left_source, excess, source)):
        summary[i] = value


def load_five(ref):
    return tuple(ref[i] for i in range(5))


def merge_kernel(level, last, mine, other, _, total):
    upper = (lax.axis_index("gz") & (1 << level)) != 0
    own = load_five(mine)
    came = load_five(other)
    low = tuple(jnp.where(upper, b, a) for a, b in zip(own, came))
    high = tuple(jnp.where(upper, a, b) for a, b in zip(own, came))
    joined = merge(low, high)
    if not last:
        for i in range(5):
            total[i] = joined[i]
        return
    in_upper = (lax.axis_index("gz") & (1 << (level + 1))) != 0
    end = jnp.zeros_like(joined[0])
    closed = suffix_step((end, end), joined)
    total[0] = jnp.where(in_upper, closed[0], joined[3])
    total[1] = jnp.where(in_upper, closed[1], joined[4])


def table_kernel(dims, parts, factors, table, spread):
    planes, width_x, width_y = dims
    part_rows = planes * width_x // parts
    lanes = spread.shape[3]
    zeros = jnp.zeros((width_x, width_y), F32)
    state = (zeros, zeros, zeros + 1.0)
    for z in range(planes - 1, -1, -1):
        if z < planes - 1:
            to_left, to_right, fixed = factors[z, 0], factors[z, 1], factors[z, 2]
            state = (
                fixed + to_right * state[0],
                to_left + to_right * state[1],
                to_right * state[2],
            )
        for t in range(3):
            for h in range(spread.shape[1]):
                spread[t, h, pl.ds(z, width_x, stride=planes), :] = state[t][
                    :, h * lanes : (h + 1) * lanes
                ]
    for c in range(parts):
        for t in range(3):
            for h in range(spread.shape[1]):
                block = spread[t, h, pl.ds(c * part_rows, part_rows), :]
                for i, piece in enumerate(split_small(block)):
                    at = pl.ds((t * PIECES + i) * part_rows, part_rows)
                    table[c, at, pl.ds(h * lanes, lanes)] = piece


def look_kernel(dims, parts, levels, phase, codes, runs, *refs):
    if phase == 0:
        factors, found, keys, spots, table, spread, rhs = refs
        table_kernel(dims, parts, factors, table, spread)
    else:
        table, _, found, keys, spots, rhs = refs
    planes, width_x, width_y = dims
    _, slabs, lanes = codes.shape
    part_rows = planes * width_x // parts
    halves = width_y // lanes
    one = jnp.ones((), F8)
    zero = jnp.zeros((), F8)
    y_id = iota((width_y, lanes), 0).astype(F32).astype(BF16)
    order = levels - 1 - phase
    turns = runs[0:1, :][0, 2 * parts]

    def find_rows(step, carry):
        wanted = []
        for c in range(parts):
            block = step * parts + c
            row, y_cell = decode(codes[(step * levels + order) * parts + c], width_y)
            wanted.append(row)
            hot = y_cell.astype(BF16)
            for s in range(slabs):
                rhs[c, :, pl.ds(s * lanes, lanes)] = jnp.where(
                    y_id == hot[s : s + 1], one, zero
                )
            x_cell = jnp.floor((row - (c * part_rows + 0.5)) * (1.0 / planes))
            half = jnp.floor((y_cell + 0.5) * (1.0 / lanes))
            keys[block] = jnp.where(row > c * part_rows, x_cell * halves + half, -1.0)
            spots[block] = (y_cell - half * lanes).astype(jnp.int32)
        for c in range(parts):
            block = step * parts + c
            row_id = (iota((part_rows, lanes), 0) + (c * part_rows + 1)).astype(F32)
            picked = jnp.dot(table[c], rhs[c], preferred_element_type=F32)
            for s in range(slabs):
                hit = row_id == wanted[c][s : s + 1]
                for t in range(3):
                    pieces = [
                        picked[
                            (t * PIECES + i) * part_rows : (t * PIECES + i + 1) * part_rows,
                            s * lanes : (s + 1) * lanes,
                        ]
                        for i in range(PIECES)
                    ]
                    total = pieces[-1]
                    for piece in pieces[-2::-1]:
                        total = piece + total * (1.0 / STEP)
                    chosen = jnp.sum(jnp.where(hit, total, 0.0), axis=0, keepdims=True)
                    found[t, block, pl.ds(s, 1), :] = chosen * (1.0 / SCALE)
        return carry

    lax.fori_loop(0, quotient_up(turns - order, levels), find_rows, 0)


def quotient_up(value, size):
    return (value + (size - 1)) // size


def join_kernel(dims, parts, levels, runs_vmem, *refs):
    planes, width_x, width_y = dims
    own = load_five(refs[0])
    others = refs[1:levels]
    far = refs[levels]
    found = refs[levels + 1 : 2 * levels + 1]
    keys = refs[2 * levels + 1 : 3 * levels + 1]
    lane_of = refs[3 * levels + 1 : 4 * levels + 1]
    edges, reply, temps, spread = refs[4 * levels + 1 :]
    slabs, rows, lanes = reply.shape
    part_x = width_x // parts
    halves = width_y // lanes
    runs = runs_vmem[...]
    first = [[runs[s, 2 * c] for s in range(slabs)] for c in range(parts)]
    longest = runs[0, 2 * parts]
    spread[:, :, pl.ds(0, rows), :] = jnp.zeros((parts, slabs, rows, lanes), F32)
    index = lax.axis_index("gz")
    zeros = jnp.zeros_like(own[0])
    top = (index & (1 << (levels - 1))) != 0
    before = (jnp.where(top, far[0], zeros + 1.0), jnp.where(top, far[1], zeros))
    after = (jnp.where(top, zeros, far[0]), jnp.where(top, zeros, far[1]))
    for level in range(levels - 2, -1, -1):
        upper = (index & (1 << level)) != 0
        segment = load_five(others[level])
        with_before = prefix_step(before, segment)
        with_after = suffix_step(after, segment)
        before = tuple(jnp.where(upper, a, b) for a, b in zip(with_before, before))
        after = tuple(jnp.where(upper, b, a) for a, b in zip(with_after, after))
    through = prefix_step(before, own)
    value = (through[1] + after[1]) / (through[0] + after[0])
    edges[0] = (before[1] + own[2] + own[0] * value) / (before[0] + own[1] + own[0])
    edges[1] = value

    def fill_rows(step, carry):
        for phase in range(levels):
            done = step * levels + (levels - 1 - phase) < longest
            for c in range(parts):
                block = step * parts + c
                key = keys[phase][block]
                lane = lane_of[phase][block] & (lanes - 1)
                ends = [jnp.zeros((slabs, lanes), F32), jnp.zeros((slabs, lanes), F32)]
                for x in range(part_x):
                    for h in range(halves):
                        hit = key == float(x * halves + h)
                        for e in range(2):
                            line = edges[e, pl.ds(c * part_x + x, 1), pl.ds(h * lanes, lanes)]
                            line = jnp.broadcast_to(line, (slabs, lanes))
                            ends[e] = jnp.where(
                                hit, jnp.take_along_axis(line, lane, axis=1), ends[e]
                            )
                temps[phase * parts + c] = jnp.where(
                    done,
                    found[phase][0, block]
                    + found[phase][1, block] * ends[0]
                    + found[phase][2, block] * ends[1],
                    0.0,
                )
        for phase in range(levels):
            for c in range(parts):
                for s in range(slabs):
                    spot = first[c][s] + step * levels + (levels - 1 - phase)
                    spread[c, s, pl.ds(spot, 1), :] = temps[phase * parts + c, pl.ds(s, 1), :]
        return carry

    lax.fori_loop(0, quotient_up(longest, levels), fill_rows, 0)
    total = spread[0, :, pl.ds(0, rows), :]
    for c in range(1, parts):
        total = total + spread[c, :, pl.ds(0, rows), :]
    reply[...] = total


def fill_planes(factors, edges, new_temp):
    planes = new_temp.shape[0]
    edge = edges[0]
    value = edges[1]
    new_temp[planes - 1] = value
    for z in range(planes - 2, -1, -1):
        value = factors[z, 2] + factors[z, 0] * edge + factors[z, 1] * value
        new_temp[z] = value


def spot_kernel(parts, slots, lanes, starts, meta, velocity, noise, spots, base, push):
    in_use = meta[...] >= 0
    for i in range(3):
        base[i] = jnp.where(in_use, (1.0 - KICK_RATE) * velocity[i], 0.0)
        push[i] = jnp.where(in_use, noise[i], 0.0)
    bricks = starts.shape[0]
    slot = iota((bricks, slots), 1).astype(F32).astype(BF16)
    one = jnp.ones((), BF16)
    zero = jnp.zeros((), BF16)
    for c in range(parts):
        begin = jnp.broadcast_to(starts[:, c : c + 1], (bricks, slots))
        target = quotient(begin, lanes).astype(F32)
        for i in range(2):
            at = pl.ds((2 * c + i) * bricks, bricks)
            spots[at, :] = jnp.where(slot == (target + float(i)).astype(BF16), one, zero)


def kick_kernel(
    parts, returned, spots, meta, starts, base, push, factors, edges,
    out, new_temp, kicked, filled, left,
):
    fill_planes(factors, edges, filled)
    copies = [pltpu.make_async_copy(filled, new_temp, left.at[3])]
    copies[0].start()
    bricks, lanes = meta.shape
    packed = meta[...]
    lane = iota((bricks, lanes), 1)
    in_use = packed >= 0
    place = quotient(jnp.maximum(packed, 0), parts)
    part = jnp.maximum(packed, 0) - place * parts
    values = jnp.concatenate(split(returned[...], 2), axis=1)
    moved = jnp.dot(spots[...], values, preferred_element_type=F32)
    moved = moved[:, :lanes] + moved[:, lanes:]
    at = place & (lanes - 1)
    temp = jnp.zeros((bricks, lanes), F32)
    for c in range(parts):
        shift = jnp.broadcast_to(starts[:, c : c + 1], (bricks, lanes)) & (lanes - 1)
        here = moved[2 * c * bricks : (2 * c + 1) * bricks]
        after = moved[(2 * c + 1) * bricks : (2 * c + 2) * bricks]
        whole = jnp.where(lane >= shift, here, after)
        temp = jnp.where(part == c, jnp.take_along_axis(whole, at, axis=1), temp)
    root = jnp.where(in_use, jnp.sqrt(2.0 * KICK_RATE * temp), 0.0)
    for i in range(3):
        kicked[i] = base[i] + root * push[i]
        copies.append(pltpu.make_async_copy(kicked.at[i], out.at[i], left.at[i]))
        copies[-1].start()
    for copy in copies:
        copy.wait()


def call(kernel, out_shape, scratch=(), spaces=None, limit=VMEM_LIMIT, cost=None, outs=None):
    extra = {} if cost is None else {"cost_estimate": cost}
    if spaces is not None:
        extra["in_specs"] = [pl.BlockSpec(memory_space=m) for m in spaces]
    if outs is not None:
        extra["out_specs"] = tuple(pl.BlockSpec(memory_space=m) for m in outs)
    return pl.pallas_call(
        kernel,
        out_shape=out_shape,
        **extra,
        scratch_shapes=list(scratch),
        compiler_params=pltpu.CompilerParams(vmem_limit_bytes=limit),
    )


def struct(*shape, dtype=F32):
    return jax.ShapeDtypeStruct(shape, dtype)


def route_call(dims, slabs, rows, parts, velocity_shape, plane_shape):
    bricks, lanes = plane_shape
    return call(
        functools.partial(route_kernel, dims, slabs, rows, parts),
        (
            struct(slabs, 2, rows, lanes),
            struct(bricks, lanes, dtype=jnp.int32),
            struct(bricks, lanes, dtype=jnp.int32),
        ),
        (
            pltpu.VMEM(velocity_shape, F32),
            pltpu.VMEM(plane_shape, jnp.int32),
            pltpu.VMEM(plane_shape, jnp.int32),
            pltpu.VMEM((1, bricks), jnp.int32),
            pltpu.SemaphoreType.DMA((4,)),
        ),
        (pltpu.HBM,) * 4,
        ROUTE_LIMIT,
    )


def body(atom_velocity, atom_noise, atom_plane, atom_column, brick_count, electron_temp):
    dims = electron_temp.shape
    planes, width_x, width_y = dims
    cells = planes * width_x
    slabs = lax.axis_size("gz")
    groups = lax.axis_size("gx")
    levels = slabs.bit_length() - 1
    assert slabs == 1 << levels and levels > 0
    bricks, lanes = atom_plane.shape
    rows = 2 * bricks // slabs
    parts = PARTS
    assert width_x % parts == 0 and parts <= 4 and lanes <= 128
    send, meta, starts = route_call(
        dims, slabs, rows, parts, atom_velocity.shape, atom_plane.shape
    )(
        *(
            pltpu.with_memory_space_constraint(x, pltpu.HBM)
            for x in (brick_count.reshape(1, bricks), atom_velocity, atom_plane, atom_column)
        )
    )
    spots, base, push = call(
        functools.partial(spot_kernel, parts, slabs * rows, lanes),
        (
            struct(2 * parts * bricks, slabs * rows, dtype=BF16),
            struct(*atom_velocity.shape),
            struct(*atom_noise.shape),
        ),
    )(starts, meta, atom_velocity, atom_noise)
    got = lax.all_to_all(send, "gz", split_axis=0, concat_axis=0, tiled=True)
    below = lax.ppermute(electron_temp[-1:], "gz", [(i, i + 1) for i in range(slabs - 1)])
    x_low = lax.ppermute(
        electron_temp[:, -1:], "gx", [(i, (i + 1) % groups) for i in range(groups)]
    )
    x_high = lax.ppermute(
        electron_temp[:, :1], "gx", [((i + 1) % groups, i) for i in range(groups)]
    )
    totals, codes, runs = call(
        functools.partial(bin_kernel, dims, parts),
        (
            struct(2, width_y // lanes, cells, lanes),
            struct(parts * (rows + 1), slabs, lanes),
            struct(slabs, lanes, dtype=jnp.int32),
        ),
        (
            pltpu.VMEM((parts, (PIECES + 1) * cells // parts, AT_ONCE * slabs * lanes), F8),
            pltpu.VMEM((parts, width_y, AT_ONCE * slabs * lanes), F8),
        ),
    )(got, spots)
    total, factors = call(
        functools.partial(solve_kernel, dims),
        (struct(5, width_x, width_y), struct(planes - 1, 3, width_x, width_y)),
    )(totals, electron_temp, below, x_low, x_high)
    blocks = parts * quotient_up(rows, levels)
    found_shapes = (
        struct(3, blocks, slabs, lanes),
        struct(blocks, slabs, lanes),
        struct(blocks, slabs, lanes, dtype=jnp.int32),
    )
    table_shape = (parts, 3 * PIECES * cells // parts, width_y)
    pieces = [total]
    found = []
    for level in range(levels):
        other = lax.ppermute(total, "gz", [(i, i ^ (1 << level)) for i in range(slabs)])
        outs = call(
            functools.partial(look_kernel, dims, parts, levels, level),
            found_shapes + ((struct(*table_shape, dtype=F8),) if level == 0 else ()),
            (() if level else (pltpu.VMEM((3, width_y // lanes, cells, lanes), F32),))
            + (pltpu.VMEM((parts, width_y, slabs * lanes), F8),),
            cost=LOOK_COST,
        )(codes, runs, *((table, total) if level else (factors,)))
        if level == 0:
            table = outs[3]
        found.append(outs[:3])
        pieces.append(other)
        if level < levels - 1:
            last = level == levels - 2
            total = call(
                functools.partial(merge_kernel, level, last),
                struct(2 if last else 5, width_x, width_y),
            )(total, other, outs[1])
    edges, reply = call(
        functools.partial(join_kernel, dims, parts, levels),
        (struct(2, width_x, width_y), struct(slabs, rows, lanes)),
        (
            pltpu.VMEM((levels * parts, slabs, lanes), F32),
            pltpu.VMEM((parts, slabs, 2 * rows + 8 * levels, lanes), F32),
        ),
    )(runs, *pieces, *(phase[i] for i in range(3) for phase in found))
    returned = lax.all_to_all(reply, "gz", split_axis=0, concat_axis=0, tiled=True)
    new_velocity, new_temp = call(
        functools.partial(kick_kernel, parts),
        (struct(*atom_velocity.shape), struct(*dims)),
        (
            pltpu.VMEM(atom_velocity.shape, F32),
            pltpu.VMEM(dims, F32),
            pltpu.SemaphoreType.DMA((4,)),
        ),
        outs=(pltpu.HBM, pltpu.HBM),
    )(
        returned.reshape(slabs * rows, lanes), spots, meta, starts, base, push, factors,
        edges,
    )
    return (new_temp, new_velocity)


def solution(mesh):
    placed = (
        P(None, ("gz", "gx"), None),
        P(None, ("gz", "gx"), None),
        P(("gz", "gx"), None),
        P(("gz", "gx"), None),
        P(("gz", "gx")),
        P("gz", "gx", None),
    )
    return jax.shard_map(
        body,
        mesh=mesh,
        in_specs=placed,
        out_specs=(P("gz", "gx", None), P(None, ("gz", "gx"), None)),
        check_vma=False,
    )
```

```python
import functools

import jax
import jax.numpy as jnp
from jax import lax
from jax.experimental import pallas as pl
from jax.experimental.pallas import tpu as pltpu
from jax.sharding import PartitionSpec as P

STIFFNESS = 10000.0
LATERAL = 0.1
COUPLE = 0.5
TWO_THIRDS = 2.0 / 3.0
KICK_RATE = 0.2
F32 = jnp.float32
BF16 = jnp.bfloat16
F8 = jnp.float8_e4m3fn
SCALE = 8.0
STEP = 16.0
PIECES = 3
PARTS = 4
AT_ONCE = 6
ROUTE_LIMIT = 32 * 1024 * 1024
VMEM_LIMIT = 32 * 1024 * 1024
LOOK_COST = pl.CostEstimate(flops=2 * 10**9, bytes_accessed=10**7, transcendentals=0)


def quotient(value, size):
    if size & (size - 1) == 0:
        return lax.shift_right_logical(value, size.bit_length() - 1)
    return value // size


def iota(shape, dim):
    return lax.broadcasted_iota(jnp.int32, shape, dim)


def split(value, pieces):
    parts = []
    for _ in range(pieces):
        part = value.astype(BF16)
        parts.append(part)
        value = value - part.astype(F32)
    return parts


def split_small(value):
    value = value * SCALE
    parts = []
    for _ in range(PIECES):
        part = value.astype(F8)
        parts.append(part)
        value = (value - part.astype(F32)) * STEP
    return parts


def join_small(parts):
    total = parts[-1]
    for part in parts[-2::-1]:
        total = part + total * (1.0 / STEP)
    return total * (1.0 / SCALE)


def merge(left, right):
    g_a, sl_a, rl_a, s_a, r_a = left
    g_b, sl_b, rl_b, s_b, r_b = right
    excess = s_a + sl_b
    source = r_a + rl_b
    inverse = 1.0 / (g_a + g_b + excess)
    to_left = g_a * inverse
    to_right = g_b * inverse
    return (
        g_a * to_right,
        sl_a + to_left * excess,
        rl_a + to_left * source,
        s_b + to_right * excess,
        r_b + to_right * source,
    )


def prefix_step(state, segment):
    gate, sl, rl, s, r = segment
    excess = state[0] + sl
    source = state[1] + rl
    ratio = gate / (gate + excess)
    return (s + ratio * excess, r + ratio * source)


def suffix_step(state, segment):
    gate, sl, rl, s, r = segment
    excess = s + state[0]
    source = r + state[1]
    ratio = gate / (gate + excess)
    return (sl + ratio * excess, rl + ratio * source)


def route_kernel(
    dims, slabs, rows, parts, count_hbm, velocity_hbm, plane_hbm, column_hbm, send, meta, starts,
    velocity, plane, column, count, arrived,
):
    copies = [
        pltpu.make_async_copy(source, target, arrived.at[i])
        for i, (source, target) in enumerate(
            (
                (count_hbm, count),
                (plane_hbm, plane),
                (column_hbm, column),
                (velocity_hbm, velocity),
            )
        )
    ]
    for copy in copies:
        copy.start()
    planes, width_x, width_y = dims
    bricks, lanes = plane.shape
    part_rows = planes * width_x // parts
    lane = iota((bricks, lanes), 1)
    sub_b = iota((bricks, bricks), 0)
    lane_b = iota((bricks, bricks), 1)
    eye = sub_b == lane_b
    sub_l = iota((lanes, lanes), 0)
    lane_l = iota((lanes, lanes), 1)
    prefix = jnp.concatenate(
        [jnp.where(sub_l <= lane_l, 1.0, 0.0), jnp.ones((lanes, lanes), F32)], axis=1
    ).astype(BF16)
    copies[0].wait()
    count_row = jnp.broadcast_to(count[...].astype(F32), (bricks, bricks))
    count_col = jnp.sum(jnp.where(eye, count_row, 0.0), axis=1, keepdims=True).astype(jnp.int32)
    in_use = lane < count_col
    copies[1].wait()
    owner = quotient(plane[:, 0:1], planes)
    owner_f = jnp.broadcast_to(owner.astype(F32), (bricks, bricks))
    owner_row = jnp.sum(jnp.where(eye, owner_f, 0.0), axis=0, keepdims=True)
    same = owner_f == owner_row
    ahead = same & (lane_b < sub_b)
    peers = jnp.where(jnp.concatenate([same, ahead], axis=0), 1.0, 0.0).astype(BF16)
    copies[2].wait()
    col = column[...]
    x_cell = quotient(col, width_y)
    y_cell = col - x_cell * width_y
    row = x_cell * planes + plane[...] - owner * planes
    code = jnp.where(in_use, (row + 1) * width_y + y_cell, 0)
    part = jnp.where(in_use, quotient(row, part_rows), parts)
    inside = [jnp.where(part == c, 1.0, 0.0).astype(BF16) for c in range(parts)]
    sums = jnp.dot(jnp.concatenate(inside, axis=0), prefix, preferred_element_type=F32)
    ranks = [sums[c * bricks : (c + 1) * bricks, :lanes] for c in range(parts)]
    sizes = [sums[c * bricks : (c + 1) * bricks, lanes:] for c in range(parts)]
    earlier = [jnp.zeros_like(sizes[0])]
    for c in range(parts - 1):
        earlier.append(earlier[-1] + sizes[c])
    joint = jnp.dot(
        peers, jnp.concatenate(sizes, axis=1).astype(BF16), preferred_element_type=F32
    )
    copies[3].wait()
    vx, vy, vz = velocity[0], velocity[1], velocity[2]
    kinetic = 0.5 * (vx * vx + vy * vy + vz * vz)
    dense = jnp.zeros((bricks, lanes), F32)
    whole = jnp.zeros((bricks, lanes), F32)
    bases = []
    for c in range(parts):
        bases.append((dense, whole))
        size = joint[:bricks, c * lanes : (c + 1) * lanes]
        dense = dense + size
        whole = whole + jnp.floor((size + (lanes - 1)) * (1.0 / lanes)) * lanes
    begins = [
        owner * (rows * lanes)
        + (
            jnp.where(whole <= rows * lanes, base[1], base[0])
            + joint[bricks:, c * lanes : (c + 1) * lanes]
        ).astype(jnp.int32)
        for c, base in enumerate(bases)
    ]
    shifts = [begin & (lanes - 1) for begin in begins]
    packed = ranks[0].astype(jnp.int32)
    run = jnp.zeros((bricks, lanes), jnp.int32)
    base = jnp.zeros((bricks, lanes), F32)
    lane_f = lane.astype(F32)
    for c in range(1, parts):
        packed = packed | (ranks[c].astype(jnp.int32) << (8 * c))
        run = jnp.where(lane_f >= earlier[c], 8 * c, run)
        base = jnp.where(lane_f >= earlier[c], earlier[c], base)
    wanted = lane - base.astype(jnp.int32)
    found = jnp.zeros((bricks, lanes), jnp.int32)
    step = lanes
    while step > 1:
        ways = 4 if step >= 4 else 2
        step //= ways
        gain = jnp.zeros((bricks, lanes), jnp.int32)
        for way in range(1, ways):
            at = jnp.take_along_axis(packed, found + (way * step - 1), axis=1)
            at = lax.shift_right_logical(at, run) & 255
            gain = jnp.where(at <= wanted, way * step, gain)
        found = found + gain
    kinetic = jnp.take_along_axis(kinetic, found, axis=1)
    code = jnp.take_along_axis(code, found, axis=1)
    zero = jnp.zeros((bricks, lanes), BF16)
    slot = iota((slabs * rows, bricks), 0).astype(F32).astype(BF16)
    values = []
    spots = []
    place = jnp.full((bricks, lanes), -1, jnp.int32)
    table = jnp.zeros((bricks, lanes), jnp.int32)
    for c in range(parts):
        table = jnp.where(lane == c, begins[c], table)
        place = jnp.where(
            part == c, (begins[c] + ranks[c].astype(jnp.int32) - 1) * parts + c, place
        )
        turn = (lane - shifts[c]) & (lanes - 1)
        valid = turn.astype(F32) < sizes[c]
        turn = (turn + earlier[c].astype(jnp.int32)) & (lanes - 1)
        kin = jnp.where(valid, jnp.take_along_axis(kinetic, turn, axis=1), 0.0)
        cell = jnp.where(valid, jnp.take_along_axis(code, turn, axis=1), 0)
        cell_row = quotient(cell, width_y)
        cell_y = cell - cell_row * width_y
        pieces = split(kin, 2) + [cell_row.astype(F32).astype(BF16), cell_y.astype(F32).astype(BF16)]
        first = lane >= shifts[c]
        values.append(jnp.concatenate([jnp.where(first, p, zero) for p in pieces], axis=1))
        values.append(jnp.concatenate([jnp.where(first, zero, p) for p in pieces], axis=1))
        begin_row = jnp.sum(
            jnp.where(eye, begins[c].astype(F32), 0.0), axis=0, keepdims=True
        ).astype(jnp.int32)
        target = quotient(begin_row, lanes).astype(F32)
        spots.append(slot == target.astype(BF16))
        spots.append(slot == (target + 1.0).astype(BF16))
    starts[...] = table
    meta[...] = place
    one = jnp.ones((), BF16)
    moved = jnp.dot(
        jnp.concatenate([jnp.where(spot, one, jnp.zeros((), BF16)) for spot in spots], axis=1),
        jnp.concatenate(values, axis=0),
        preferred_element_type=F32,
    )
    send[:, 0] = (moved[:, :lanes] + moved[:, lanes : 2 * lanes]).reshape(slabs, rows, lanes)
    send[:, 1] = (moved[:, 2 * lanes : 3 * lanes] * width_y + moved[:, 3 * lanes :]).reshape(
        slabs, rows, lanes
    )


def decode(code, width_y):
    row = jnp.floor((code + 0.5) * (1.0 / width_y))
    return row, code - row * width_y


def find_runs(dims, parts, got, runs_vmem):
    planes, width_x, width_y = dims
    slabs, _, rows, lanes = got.shape
    part_rows = planes * width_x // parts
    codes = got[:, 1]
    beyond = float((parts * part_rows + 1) * width_y + 1)
    lead = codes[:, :, 0:1]
    used = lead > 0.0
    lead = jnp.where(used, lead, beyond)
    top = jnp.where(used, jnp.max(codes, axis=2, keepdims=True), beyond)
    longest = jnp.zeros((slabs, 1), F32)
    first = jnp.zeros((slabs, 1), F32)
    table = jnp.zeros((slabs, lanes), F32)
    lane = iota((slabs, lanes), 1)
    for c in range(parts):
        limit = float(((c + 1) * part_rows + 1) * width_y)
        last = jnp.sum(jnp.where(lead < limit, 1.0, 0.0), axis=1)
        longest = jnp.maximum(longest, last - first)
        table = jnp.where(lane == 2 * c, first, table)
        table = jnp.where(lane == 2 * c + 1, last, table)
        first = jnp.sum(jnp.where(top < limit, 1.0, 0.0), axis=1)
    longest = jnp.max(longest, axis=0, keepdims=True)
    runs_vmem[...] = jnp.where(lane == 2 * parts, longest, table).astype(jnp.int32)


def run_row(got, field, s, spot, last):
    rows = got.shape[2]
    loaded = got[s, field, pl.ds(jnp.minimum(spot, rows - 1), 1), :]
    return jnp.where(spot < last, loaded, 0.0)


def bin_kernel(dims, parts, got, _, totals, codes, runs_vmem, lhs, rhs):
    planes, width_x, width_y = dims
    slabs, _, rows, lanes = got.shape
    part_rows = planes * width_x // parts
    find_runs(dims, parts, got, runs_vmem)
    runs = runs_vmem[...]
    first = [[runs[s, 2 * c] for s in range(slabs)] for c in range(parts)]
    last = [[runs[s, 2 * c + 1] for s in range(slabs)] for c in range(parts)]
    longest = runs[0, 2 * parts]
    one = jnp.ones((), F8)
    zero = jnp.zeros((), F8)
    y_id = iota((width_y, lanes), 0).astype(F32).astype(BF16)
    totals[...] = jnp.zeros(totals.shape, F32)

    def add_rows(begin, at_once):
        for c in range(parts):
            row_id = (iota((part_rows, lanes), 0) + (c * part_rows + 1)).astype(F32).astype(BF16)
            for i in range(at_once * slabs):
                s = i % slabs
                turn = begin + i // slabs
                spot = first[c][s] + turn
                pieces = split_small(run_row(got, 0, s, spot, last[c][s]))
                code = run_row(got, 1, s, spot, last[c][s])
                codes[turn * parts + c, pl.ds(s, 1), :] = code
                row, y_cell = decode(code, width_y)
                here = pl.ds(i * lanes, lanes)
                hit = row_id == row.astype(BF16)
                for j, piece in enumerate(pieces):
                    lhs[c, pl.ds(j * part_rows, part_rows), here] = jnp.where(hit, piece, zero)
                lhs[c, pl.ds(PIECES * part_rows, part_rows), here] = jnp.where(hit, one, zero)
                rhs[c, :, here] = jnp.where(y_id == y_cell.astype(BF16), one, zero)
        for c in range(parts):
            width = pl.ds(0, at_once * slabs * lanes)
            added = lax.dot_general(
                lhs[c, :, width],
                rhs[c, :, width],
                (((1,), (1,)), ((), ())),
                preferred_element_type=F32,
            )
            pieces = [added[i * part_rows : (i + 1) * part_rows] for i in range(PIECES + 1)]
            for i, value in enumerate((join_small(pieces[:PIECES]), pieces[PIECES])):
                for h in range(width_y // lanes):
                    totals[i, h, pl.ds(c * part_rows, part_rows), :] += value[
                        :, h * lanes : (h + 1) * lanes
                    ]

    def many_turns(step, carry):
        add_rows(step * AT_ONCE, AT_ONCE)
        return carry

    def one_turn(turn, carry):
        add_rows(turn, 1)
        return carry

    steps = longest // AT_ONCE
    lax.fori_loop(0, steps, many_turns, 0)
    lax.fori_loop(steps * AT_ONCE, longest, one_turn, 0)


def solve_kernel(dims, totals, temp, below, x_low, x_high, summary, factors):
    planes, width_x, width_y = dims
    lanes = totals.shape[3]

    def plane_terms(z):
        here = temp[z]
        x_minus = jnp.concatenate([x_low[z], here[:-1]], axis=0)
        x_plus = jnp.concatenate([here[1:], x_high[z]], axis=0)
        lateral = LATERAL * (
            x_minus
            + x_plus
            + pltpu.roll(here, 1, 1)
            + pltpu.roll(here, width_y - 1, 1)
            - 4.0 * here
        )
        at = pl.ds(z, width_x, stride=planes)
        sums = [
            jnp.concatenate([totals[i, h, at, :] for h in range(width_y // lanes)], axis=1)
            for i in range(2)
        ]
        energy, count = sums
        return here + COUPLE * count, here * here + lateral + COUPLE * TWO_THIRDS * energy

    start = temp[0]
    gate = jnp.where(
        lax.axis_index("gz") > 0, STIFFNESS * (0.5 * (start + below[0])), jnp.zeros_like(start)
    )
    excess, source = plane_terms(0)
    left_excess = jnp.zeros_like(start)
    left_source = jnp.zeros_like(start)
    for z in range(planes - 1):
        face = STIFFNESS * (0.5 * (temp[z + 1] + temp[z]))
        inverse = 1.0 / (gate + face + excess)
        to_left = gate * inverse
        to_right = face * inverse
        factors[z, 0] = to_left
        factors[z, 1] = to_right
        factors[z, 2] = source * inverse
        next_excess, next_source = plane_terms(z + 1)
        left_excess = left_excess + to_left * excess
        left_source = left_source + to_left * source
        gate = gate * to_right
        excess = next_excess + to_right * excess
        source = next_source + to_right * source
    for i, value in enumerate((gate, left_excess, left_source, excess, source)):
        summary[i] = value


def load_five(ref):
    return tuple(ref[i] for i in range(5))


def merge_kernel(level, last, mine, other, _, total):
    upper = (lax.axis_index("gz") & (1 << level)) != 0
    own = load_five(mine)
    came = load_five(other)
    low = tuple(jnp.where(upper, b, a) for a, b in zip(own, came))
    high = tuple(jnp.where(upper, a, b) for a, b in zip(own, came))
    joined = merge(low, high)
    if not last:
        for i in range(5):
            total[i] = joined[i]
        return
    in_upper = (lax.axis_index("gz") & (1 << (level + 1))) != 0
    end = jnp.zeros_like(joined[0])
    closed = suffix_step((end, end), joined)
    total[0] = jnp.where(in_upper, closed[0], joined[3])
    total[1] = jnp.where(in_upper, closed[1], joined[4])


def table_kernel(dims, parts, factors, table, spread):
    planes, width_x, width_y = dims
    part_rows = planes * width_x // parts
    lanes = spread.shape[3]
    zeros = jnp.zeros((width_x, width_y), F32)
    state = (zeros, zeros, zeros + 1.0)
    for z in range(planes - 1, -1, -1):
        if z < planes - 1:
            to_left, to_right, fixed = factors[z, 0], factors[z, 1], factors[z, 2]
            state = (
                fixed + to_right * state[0],
                to_left + to_right * state[1],
                to_right * state[2],
            )
        for t in range(3):
            for h in range(spread.shape[1]):
                spread[t, h, pl.ds(z, width_x, stride=planes), :] = state[t][
                    :, h * lanes : (h + 1) * lanes
                ]
    for c in range(parts):
        for t in range(3):
            for h in range(spread.shape[1]):
                block = spread[t, h, pl.ds(c * part_rows, part_rows), :]
                for i, piece in enumerate(split_small(block)):
                    at = pl.ds((t * PIECES + i) * part_rows, part_rows)
                    table[c, at, pl.ds(h * lanes, lanes)] = piece


def look_kernel(dims, parts, levels, phase, codes, runs, *refs):
    if phase == 0:
        factors, found, keys, spots, table, spread, rhs = refs
        table_kernel(dims, parts, factors, table, spread)
    else:
        table, _, found, keys, spots, rhs = refs
    planes, width_x, width_y = dims
    _, slabs, lanes = codes.shape
    part_rows = planes * width_x // parts
    halves = width_y // lanes
    one = jnp.ones((), F8)
    zero = jnp.zeros((), F8)
    y_id = iota((width_y, lanes), 0).astype(F32).astype(BF16)
    order = levels - 1 - phase
    turns = runs[0:1, :][0, 2 * parts]

    def find_rows(step, carry):
        wanted = []
        for c in range(parts):
            block = step * parts + c
            row, y_cell = decode(codes[(step * levels + order) * parts + c], width_y)
            wanted.append(row)
            hot = y_cell.astype(BF16)
            for s in range(slabs):
                rhs[c, :, pl.ds(s * lanes, lanes)] = jnp.where(
                    y_id == hot[s : s + 1], one, zero
                )
            x_cell = jnp.floor((row - (c * part_rows + 0.5)) * (1.0 / planes))
            half = jnp.floor((y_cell + 0.5) * (1.0 / lanes))
            keys[block] = jnp.where(row > c * part_rows, x_cell * halves + half, -1.0)
            spots[block] = (y_cell - half * lanes).astype(jnp.int32)
        for c in range(parts):
            block = step * parts + c
            row_id = (iota((part_rows, lanes), 0) + (c * part_rows + 1)).astype(F32)
            picked = jnp.dot(table[c], rhs[c], preferred_element_type=F32)
            for s in range(slabs):
                hit = row_id == wanted[c][s : s + 1]
                for t in range(3):
                    pieces = [
                        picked[
                            (t * PIECES + i) * part_rows : (t * PIECES + i + 1) * part_rows,
                            s * lanes : (s + 1) * lanes,
                        ]
                        for i in range(PIECES)
                    ]
                    total = pieces[-1]
                    for piece in pieces[-2::-1]:
                        total = piece + total * (1.0 / STEP)
                    chosen = jnp.sum(jnp.where(hit, total, 0.0), axis=0, keepdims=True)
                    found[t, block, pl.ds(s, 1), :] = chosen * (1.0 / SCALE)
        return carry

    lax.fori_loop(0, quotient_up(turns - order, levels), find_rows, 0)


def quotient_up(value, size):
    return (value + (size - 1)) // size


def join_kernel(dims, parts, levels, runs_vmem, *refs):
    planes, width_x, width_y = dims
    own = load_five(refs[0])
    others = refs[1:levels]
    far = refs[levels]
    found = refs[levels + 1 : 2 * levels + 1]
    keys = refs[2 * levels + 1 : 3 * levels + 1]
    lane_of = refs[3 * levels + 1 : 4 * levels + 1]
    edges, reply, temps, spread = refs[4 * levels + 1 :]
    slabs, rows, lanes = reply.shape
    part_x = width_x // parts
    halves = width_y // lanes
    runs = runs_vmem[...]
    first = [[runs[s, 2 * c] for s in range(slabs)] for c in range(parts)]
    longest = runs[0, 2 * parts]
    spread[:, :, pl.ds(0, rows), :] = jnp.zeros((parts, slabs, rows, lanes), F32)
    index = lax.axis_index("gz")
    zeros = jnp.zeros_like(own[0])
    top = (index & (1 << (levels - 1))) != 0
    before = (jnp.where(top, far[0], zeros + 1.0), jnp.where(top, far[1], zeros))
    after = (jnp.where(top, zeros, far[0]), jnp.where(top, zeros, far[1]))
    for level in range(levels - 2, -1, -1):
        upper = (index & (1 << level)) != 0
        segment = load_five(others[level])
        with_before = prefix_step(before, segment)
        with_after = suffix_step(after, segment)
        before = tuple(jnp.where(upper, a, b) for a, b in zip(with_before, before))
        after = tuple(jnp.where(upper, b, a) for a, b in zip(with_after, after))
    through = prefix_step(before, own)
    value = (through[1] + after[1]) / (through[0] + after[0])
    edges[0] = (before[1] + own[2] + own[0] * value) / (before[0] + own[1] + own[0])
    edges[1] = value

    def fill_rows(step, carry):
        for phase in range(levels):
            done = step * levels + (levels - 1 - phase) < longest
            for c in range(parts):
                block = step * parts + c
                key = keys[phase][block]
                lane = lane_of[phase][block] & (lanes - 1)
                ends = [jnp.zeros((slabs, lanes), F32), jnp.zeros((slabs, lanes), F32)]
                for x in range(part_x):
                    for h in range(halves):
                        hit = key == float(x * halves + h)
                        for e in range(2):
                            line = edges[e, pl.ds(c * part_x + x, 1), pl.ds(h * lanes, lanes)]
                            line = jnp.broadcast_to(line, (slabs, lanes))
                            ends[e] = jnp.where(
                                hit, jnp.take_along_axis(line, lane, axis=1), ends[e]
                            )
                temps[phase * parts + c] = jnp.where(
                    done,
                    found[phase][0, block]
                    + found[phase][1, block] * ends[0]
                    + found[phase][2, block] * ends[1],
                    0.0,
                )
        for phase in range(levels):
            for c in range(parts):
                for s in range(slabs):
                    spot = first[c][s] + step * levels + (levels - 1 - phase)
                    spread[c, s, pl.ds(spot, 1), :] = temps[phase * parts + c, pl.ds(s, 1), :]
        return carry

    lax.fori_loop(0, quotient_up(longest, levels), fill_rows, 0)
    total = spread[0, :, pl.ds(0, rows), :]
    for c in range(1, parts):
        total = total + spread[c, :, pl.ds(0, rows), :]
    reply[...] = total


def fill_planes(factors, edges, new_temp):
    planes = new_temp.shape[0]
    edge = edges[0]
    value = edges[1]
    new_temp[planes - 1] = value
    for z in range(planes - 2, -1, -1):
        value = factors[z, 2] + factors[z, 0] * edge + factors[z, 1] * value
        new_temp[z] = value


def spot_kernel(parts, slots, lanes, starts, meta, velocity, noise, spots, base, push):
    in_use = meta[...] >= 0
    for i in range(3):
        base[i] = jnp.where(in_use, (1.0 - KICK_RATE) * velocity[i], 0.0)
        push[i] = jnp.where(in_use, noise[i], 0.0)
    bricks = starts.shape[0]
    slot = iota((bricks, slots), 1).astype(F32).astype(BF16)
    one = jnp.ones((), BF16)
    zero = jnp.zeros((), BF16)
    for c in range(parts):
        begin = jnp.broadcast_to(starts[:, c : c + 1], (bricks, slots))
        target = quotient(begin, lanes).astype(F32)
        for i in range(2):
            at = pl.ds((2 * c + i) * bricks, bricks)
            spots[at, :] = jnp.where(slot == (target + float(i)).astype(BF16), one, zero)


def kick_kernel(
    parts, returned, spots, meta, starts, base, push, factors, edges,
    out, new_temp, kicked, filled, left,
):
    fill_planes(factors, edges, filled)
    copies = [pltpu.make_async_copy(filled, new_temp, left.at[3])]
    copies[0].start()
    bricks, lanes = meta.shape
    packed = meta[...]
    lane = iota((bricks, lanes), 1)
    in_use = packed >= 0
    place = quotient(jnp.maximum(packed, 0), parts)
    part = jnp.maximum(packed, 0) - place * parts
    values = jnp.concatenate(split(returned[...], 2), axis=1)
    moved = jnp.dot(spots[...], values, preferred_element_type=F32)
    moved = moved[:, :lanes] + moved[:, lanes:]
    at = place & (lanes - 1)
    temp = jnp.zeros((bricks, lanes), F32)
    for c in range(parts):
        shift = jnp.broadcast_to(starts[:, c : c + 1], (bricks, lanes)) & (lanes - 1)
        here = moved[2 * c * bricks : (2 * c + 1) * bricks]
        after = moved[(2 * c + 1) * bricks : (2 * c + 2) * bricks]
        whole = jnp.where(lane >= shift, here, after)
        temp = jnp.where(part == c, jnp.take_along_axis(whole, at, axis=1), temp)
    root = jnp.where(in_use, jnp.sqrt(2.0 * KICK_RATE * temp), 0.0)
    for i in range(3):
        kicked[i] = base[i] + root * push[i]
        copies.append(pltpu.make_async_copy(kicked.at[i], out.at[i], left.at[i]))
        copies[-1].start()
    for copy in copies:
        copy.wait()


def call(kernel, out_shape, scratch=(), spaces=None, limit=VMEM_LIMIT, cost=None, outs=None):
    extra = {} if cost is None else {"cost_estimate": cost}
    if spaces is not None:
        extra["in_specs"] = [pl.BlockSpec(memory_space=m) for m in spaces]
    if outs is not None:
        extra["out_specs"] = tuple(pl.BlockSpec(memory_space=m) for m in outs)
    return pl.pallas_call(
        kernel,
        out_shape=out_shape,
        **extra,
        scratch_shapes=list(scratch),
        compiler_params=pltpu.CompilerParams(vmem_limit_bytes=limit),
    )


def struct(*shape, dtype=F32):
    return jax.ShapeDtypeStruct(shape, dtype)


def route_call(dims, slabs, rows, parts, velocity_shape, plane_shape):
    bricks, lanes = plane_shape
    return call(
        functools.partial(route_kernel, dims, slabs, rows, parts),
        (
            struct(slabs, 2, rows, lanes),
            struct(bricks, lanes, dtype=jnp.int32),
            struct(bricks, lanes, dtype=jnp.int32),
        ),
        (
            pltpu.VMEM(velocity_shape, F32),
            pltpu.VMEM(plane_shape, jnp.int32),
            pltpu.VMEM(plane_shape, jnp.int32),
            pltpu.VMEM((1, bricks), jnp.int32),
            pltpu.SemaphoreType.DMA((4,)),
        ),
        (pltpu.HBM,) * 4,
        ROUTE_LIMIT,
    )


def body(atom_velocity, atom_noise, atom_plane, atom_column, brick_count, electron_temp):
    dims = electron_temp.shape
    planes, width_x, width_y = dims
    cells = planes * width_x
    slabs = lax.axis_size("gz")
    groups = lax.axis_size("gx")
    levels = slabs.bit_length() - 1
    assert slabs == 1 << levels and levels > 0
    bricks, lanes = atom_plane.shape
    rows = 2 * bricks // slabs
    parts = PARTS
    assert width_x % parts == 0 and parts <= 4 and lanes <= 128
    send, meta, starts = route_call(
        dims, slabs, rows, parts, atom_velocity.shape, atom_plane.shape
    )(
        *(
            pltpu.with_memory_space_constraint(x, pltpu.HBM)
            for x in (brick_count.reshape(1, bricks), atom_velocity, atom_plane, atom_column)
        )
    )
    spots, base, push = call(
        functools.partial(spot_kernel, parts, slabs * rows, lanes),
        (
            struct(2 * parts * bricks, slabs * rows, dtype=BF16),
            struct(*atom_velocity.shape),
            struct(*atom_noise.shape),
        ),
    )(starts, meta, atom_velocity, atom_noise)
    got = lax.all_to_all(send, "gz", split_axis=0, concat_axis=0, tiled=True)
    below = lax.ppermute(electron_temp[-1:], "gz", [(i, i + 1) for i in range(slabs - 1)])
    x_low = lax.ppermute(
        electron_temp[:, -1:], "gx", [(i, (i + 1) % groups) for i in range(groups)]
    )
    x_high = lax.ppermute(
        electron_temp[:, :1], "gx", [((i + 1) % groups, i) for i in range(groups)]
    )
    totals, codes, runs = call(
        functools.partial(bin_kernel, dims, parts),
        (
            struct(2, width_y // lanes, cells, lanes),
            struct(parts * (rows + 1), slabs, lanes),
            struct(slabs, lanes, dtype=jnp.int32),
        ),
        (
            pltpu.VMEM((parts, (PIECES + 1) * cells // parts, AT_ONCE * slabs * lanes), F8),
            pltpu.VMEM((parts, width_y, AT_ONCE * slabs * lanes), F8),
        ),
    )(got, spots)
    total, factors = call(
        functools.partial(solve_kernel, dims),
        (struct(5, width_x, width_y), struct(planes - 1, 3, width_x, width_y)),
    )(totals, electron_temp, below, x_low, x_high)
    blocks = parts * quotient_up(rows, levels)
    found_shapes = (
        struct(3, blocks, slabs, lanes),
        struct(blocks, slabs, lanes),
        struct(blocks, slabs, lanes, dtype=jnp.int32),
    )
    table_shape = (parts, 3 * PIECES * cells // parts, width_y)
    pieces = [total]
    found = []
    for level in range(levels):
        other = lax.ppermute(total, "gz", [(i, i ^ (1 << level)) for i in range(slabs)])
        outs = call(
            functools.partial(look_kernel, dims, parts, levels, level),
            found_shapes + ((struct(*table_shape, dtype=F8),) if level == 0 else ()),
            (() if level else (pltpu.VMEM((3, width_y // lanes, cells, lanes), F32),))
            + (pltpu.VMEM((parts, width_y, slabs * lanes), F8),),
            cost=LOOK_COST,
        )(codes, runs, *((table, total) if level else (factors,)))
        if level == 0:
            table = outs[3]
        found.append(outs[:3])
        pieces.append(other)
        if level < levels - 1:
            last = level == levels - 2
            total = call(
                functools.partial(merge_kernel, level, last),
                struct(2 if last else 5, width_x, width_y),
            )(total, other, outs[1])
    edges, reply = call(
        functools.partial(join_kernel, dims, parts, levels),
        (struct(2, width_x, width_y), struct(slabs, rows, lanes)),
        (
            pltpu.VMEM((levels * parts, slabs, lanes), F32),
            pltpu.VMEM((parts, slabs, 2 * rows + 8 * levels, lanes), F32),
        ),
    )(runs, *pieces, *(phase[i] for i in range(3) for phase in found))
    returned = lax.all_to_all(reply, "gz", split_axis=0, concat_axis=0, tiled=True)
    new_velocity, new_temp = call(
        functools.partial(kick_kernel, parts),
        (struct(*atom_velocity.shape), struct(*dims)),
        (
            pltpu.VMEM(atom_velocity.shape, F32),
            pltpu.VMEM(dims, F32),
            pltpu.SemaphoreType.DMA((4,)),
        ),
        outs=(pltpu.HBM, pltpu.HBM),
    )(
        returned.reshape(slabs * rows, lanes), spots, meta, starts, base, push, factors,
        edges,
    )
    return (new_temp, new_velocity)


def solution(mesh):
    placed = (
        P(None, ("gz", "gx"), None),
        P(None, ("gz", "gx"), None),
        P(("gz", "gx"), None),
        P(("gz", "gx"), None),
        P(("gz", "gx")),
        P("gz", "gx", None),
    )
    return jax.shard_map(
        body,
        mesh=mesh,
        in_specs=placed,
        out_specs=(P("gz", "gx", None), P(None, ("gz", "gx"), None)),
        check_vma=False,
    )
```

```python
import functools

import jax
import jax.numpy as jnp
from jax import lax
from jax.experimental import pallas as pl
from jax.experimental.pallas import tpu as pltpu
from jax.sharding import PartitionSpec as P

STIFFNESS = 10000.0
LATERAL = 0.1
COUPLE = 0.5
TWO_THIRDS = 2.0 / 3.0
KICK_RATE = 0.2
F32 = jnp.float32
BF16 = jnp.bfloat16
F8 = jnp.float8_e4m3fn
SCALE = 8.0
STEP = 16.0
PIECES = 3
PARTS = 4
AT_ONCE = 3
ROUTE_LIMIT = 32 * 1024 * 1024
VMEM_LIMIT = 32 * 1024 * 1024
LOOK_COST = pl.CostEstimate(flops=2 * 10**9, bytes_accessed=10**7, transcendentals=0)


def quotient(value, size):
    if size & (size - 1) == 0:
        return lax.shift_right_logical(value, size.bit_length() - 1)
    return value // size


def iota(shape, dim):
    return lax.broadcasted_iota(jnp.int32, shape, dim)


def split(value, pieces):
    parts = []
    for _ in range(pieces):
        part = value.astype(BF16)
        parts.append(part)
        value = value - part.astype(F32)
    return parts


def split_small(value):
    value = value * SCALE
    parts = []
    for _ in range(PIECES):
        part = value.astype(F8)
        parts.append(part)
        value = (value - part.astype(F32)) * STEP
    return parts


def join_small(parts):
    total = parts[-1]
    for part in parts[-2::-1]:
        total = part + total * (1.0 / STEP)
    return total * (1.0 / SCALE)


def merge(left, right):
    g_a, sl_a, rl_a, s_a, r_a = left
    g_b, sl_b, rl_b, s_b, r_b = right
    excess = s_a + sl_b
    source = r_a + rl_b
    inverse = 1.0 / (g_a + g_b + excess)
    to_left = g_a * inverse
    to_right = g_b * inverse
    return (
        g_a * to_right,
        sl_a + to_left * excess,
        rl_a + to_left * source,
        s_b + to_right * excess,
        r_b + to_right * source,
    )


def prefix_step(state, segment):
    gate, sl, rl, s, r = segment
    excess = state[0] + sl
    source = state[1] + rl
    ratio = gate / (gate + excess)
    return (s + ratio * excess, r + ratio * source)


def suffix_step(state, segment):
    gate, sl, rl, s, r = segment
    excess = s + state[0]
    source = r + state[1]
    ratio = gate / (gate + excess)
    return (sl + ratio * excess, rl + ratio * source)


def route_kernel(
    dims, slabs, rows, parts, count_hbm, velocity_hbm, plane_hbm, column_hbm, send, meta, starts,
    velocity, plane, column, count, arrived,
):
    copies = [
        pltpu.make_async_copy(source, target, arrived.at[i])
        for i, (source, target) in enumerate(
            (
                (count_hbm, count),
                (plane_hbm, plane),
                (column_hbm, column),
                (velocity_hbm, velocity),
            )
        )
    ]
    for copy in copies:
        copy.start()
    planes, width_x, width_y = dims
    bricks, lanes = plane.shape
    part_rows = planes * width_x // parts
    lane = iota((bricks, lanes), 1)
    sub_b = iota((bricks, bricks), 0)
    lane_b = iota((bricks, bricks), 1)
    eye = sub_b == lane_b
    sub_l = iota((lanes, lanes), 0)
    lane_l = iota((lanes, lanes), 1)
    prefix = jnp.concatenate(
        [jnp.where(sub_l <= lane_l, 1.0, 0.0), jnp.ones((lanes, lanes), F32)], axis=1
    ).astype(BF16)
    copies[0].wait()
    count_row = jnp.broadcast_to(count[...].astype(F32), (bricks, bricks))
    count_col = jnp.sum(jnp.where(eye, count_row, 0.0), axis=1, keepdims=True).astype(jnp.int32)
    in_use = lane < count_col
    copies[1].wait()
    owner = quotient(plane[:, 0:1], planes)
    owner_f = jnp.broadcast_to(owner.astype(F32), (bricks, bricks))
    owner_row = jnp.sum(jnp.where(eye, owner_f, 0.0), axis=0, keepdims=True)
    same = owner_f == owner_row
    ahead = same & (lane_b < sub_b)
    peers = jnp.where(jnp.concatenate([same, ahead], axis=0), 1.0, 0.0).astype(BF16)
    copies[2].wait()
    col = column[...]
    x_cell = quotient(col, width_y)
    y_cell = col - x_cell * width_y
    row = x_cell * planes + plane[...] - owner * planes
    code = jnp.where(in_use, (row + 1) * width_y + y_cell, 0)
    part = jnp.where(in_use, quotient(row, part_rows), parts)
    inside = [jnp.where(part == c, 1.0, 0.0).astype(BF16) for c in range(parts)]
    sums = jnp.dot(jnp.concatenate(inside, axis=0), prefix, preferred_element_type=F32)
    ranks = [sums[c * bricks : (c + 1) * bricks, :lanes] for c in range(parts)]
    sizes = [sums[c * bricks : (c + 1) * bricks, lanes:] for c in range(parts)]
    earlier = [jnp.zeros_like(sizes[0])]
    for c in range(parts - 1):
        earlier.append(earlier[-1] + sizes[c])
    joint = jnp.dot(
        peers, jnp.concatenate(sizes, axis=1).astype(BF16), preferred_element_type=F32
    )
    copies[3].wait()
    vx, vy, vz = velocity[0], velocity[1], velocity[2]
    kinetic = 0.5 * (vx * vx + vy * vy + vz * vz)
    dense = jnp.zeros((bricks, lanes), F32)
    whole = jnp.zeros((bricks, lanes), F32)
    bases = []
    for c in range(parts):
        bases.append((dense, whole))
        size = joint[:bricks, c * lanes : (c + 1) * lanes]
        dense = dense + size
        whole = whole + jnp.floor((size + (lanes - 1)) * (1.0 / lanes)) * lanes
    begins = [
        owner * (rows * lanes)
        + (
            jnp.where(whole <= rows * lanes, base[1], base[0])
            + joint[bricks:, c * lanes : (c + 1) * lanes]
        ).astype(jnp.int32)
        for c, base in enumerate(bases)
    ]
    shifts = [begin & (lanes - 1) for begin in begins]
    packed = ranks[0].astype(jnp.int32)
    run = jnp.zeros((bricks, lanes), jnp.int32)
    base = jnp.zeros((bricks, lanes), F32)
    lane_f = lane.astype(F32)
    for c in range(1, parts):
        packed = packed | (ranks[c].astype(jnp.int32) << (8 * c))
        run = jnp.where(lane_f >= earlier[c], 8 * c, run)
        base = jnp.where(lane_f >= earlier[c], earlier[c], base)
    wanted = lane - base.astype(jnp.int32)
    found = jnp.zeros((bricks, lanes), jnp.int32)
    step = lanes
    while step > 1:
        ways = 4 if step >= 4 else 2
        step //= ways
        gain = jnp.zeros((bricks, lanes), jnp.int32)
        for way in range(1, ways):
            at = jnp.take_along_axis(packed, found + (way * step - 1), axis=1)
            at = lax.shift_right_logical(at, run) & 255
            gain = jnp.where(at <= wanted, way * step, gain)
        found = found + gain
    kinetic = jnp.take_along_axis(kinetic, found, axis=1)
    code = jnp.take_along_axis(code, found, axis=1)
    zero = jnp.zeros((bricks, lanes), BF16)
    slot = iota((slabs * rows, bricks), 0).astype(F32).astype(BF16)
    values = []
    spots = []
    place = jnp.full((bricks, lanes), -1, jnp.int32)
    table = jnp.zeros((bricks, lanes), jnp.int32)
    for c in range(parts):
        table = jnp.where(lane == c, begins[c], table)
        place = jnp.where(
            part == c, (begins[c] + ranks[c].astype(jnp.int32) - 1) * parts + c, place
        )
        turn = (lane - shifts[c]) & (lanes - 1)
        valid = turn.astype(F32) < sizes[c]
        turn = (turn + earlier[c].astype(jnp.int32)) & (lanes - 1)
        kin = jnp.where(valid, jnp.take_along_axis(kinetic, turn, axis=1), 0.0)
        cell = jnp.where(valid, jnp.take_along_axis(code, turn, axis=1), 0)
        cell_row = quotient(cell, width_y)
        cell_y = cell - cell_row * width_y
        pieces = split(kin, 2) + [cell_row.astype(F32).astype(BF16), cell_y.astype(F32).astype(BF16)]
        first = lane >= shifts[c]
        values.append(jnp.concatenate([jnp.where(first, p, zero) for p in pieces], axis=1))
        values.append(jnp.concatenate([jnp.where(first, zero, p) for p in pieces], axis=1))
        begin_row = jnp.sum(
            jnp.where(eye, begins[c].astype(F32), 0.0), axis=0, keepdims=True
        ).astype(jnp.int32)
        target = quotient(begin_row, lanes).astype(F32)
        spots.append(slot == target.astype(BF16))
        spots.append(slot == (target + 1.0).astype(BF16))
    starts[...] = table
    meta[...] = place
    one = jnp.ones((), BF16)
    moved = jnp.dot(
        jnp.concatenate([jnp.where(spot, one, jnp.zeros((), BF16)) for spot in spots], axis=1),
        jnp.concatenate(values, axis=0),
        preferred_element_type=F32,
    )
    send[:, 0] = (moved[:, :lanes] + moved[:, lanes : 2 * lanes]).reshape(slabs, rows, lanes)
    send[:, 1] = (moved[:, 2 * lanes : 3 * lanes] * width_y + moved[:, 3 * lanes :]).reshape(
        slabs, rows, lanes
    )


def decode(code, width_y):
    row = jnp.floor((code + 0.5) * (1.0 / width_y))
    return row, code - row * width_y


def find_runs(dims, parts, got, runs_vmem):
    planes, width_x, width_y = dims
    slabs, _, rows, lanes = got.shape
    part_rows = planes * width_x // parts
    codes = got[:, 1]
    beyond = float((parts * part_rows + 1) * width_y + 1)
    lead = codes[:, :, 0:1]
    used = lead > 0.0
    lead = jnp.where(used, lead, beyond)
    top = jnp.where(used, jnp.max(codes, axis=2, keepdims=True), beyond)
    longest = jnp.zeros((slabs, 1), F32)
    first = jnp.zeros((slabs, 1), F32)
    table = jnp.zeros((slabs, lanes), F32)
    lane = iota((slabs, lanes), 1)
    for c in range(parts):
        limit = float(((c + 1) * part_rows + 1) * width_y)
        last = jnp.sum(jnp.where(lead < limit, 1.0, 0.0), axis=1)
        longest = jnp.maximum(longest, last - first)
        table = jnp.where(lane == 2 * c, first, table)
        table = jnp.where(lane == 2 * c + 1, last, table)
        first = jnp.sum(jnp.where(top < limit, 1.0, 0.0), axis=1)
    longest = jnp.max(longest, axis=0, keepdims=True)
    runs_vmem[...] = jnp.where(lane == 2 * parts, longest, table).astype(jnp.int32)


def run_row(got, field, s, spot, last):
    rows = got.shape[2]
    loaded = got[s, field, pl.ds(jnp.minimum(spot, rows - 1), 1), :]
    return jnp.where(spot < last, loaded, 0.0)


def bin_kernel(dims, parts, got, _, totals, codes, runs_vmem, lhs, rhs):
    planes, width_x, width_y = dims
    slabs, _, rows, lanes = got.shape
    part_rows = planes * width_x // parts
    find_runs(dims, parts, got, runs_vmem)
    runs = runs_vmem[...]
    first = [[runs[s, 2 * c] for s in range(slabs)] for c in range(parts)]
    last = [[runs[s, 2 * c + 1] for s in range(slabs)] for c in range(parts)]
    longest = runs[0, 2 * parts]
    one = jnp.ones((), F8)
    zero = jnp.zeros((), F8)
    y_id = iota((width_y, lanes), 0).astype(F32).astype(BF16)
    totals[...] = jnp.zeros(totals.shape, F32)

    def add_rows(step, carry):
        for c in range(parts):
            row_id = (iota((part_rows, lanes), 0) + (c * part_rows + 1)).astype(F32).astype(BF16)
            for i in range(AT_ONCE * slabs):
                s = i % slabs
                turn = step * AT_ONCE + i // slabs
                spot = first[c][s] + turn
                pieces = split_small(run_row(got, 0, s, spot, last[c][s]))
                code = run_row(got, 1, s, spot, last[c][s])
                codes[turn * parts + c, pl.ds(s, 1), :] = code
                row, y_cell = decode(code, width_y)
                here = pl.ds(i * lanes, lanes)
                hit = row_id == row.astype(BF16)
                for j, piece in enumerate(pieces):
                    lhs[c, pl.ds(j * part_rows, part_rows), here] = jnp.where(hit, piece, zero)
                lhs[c, pl.ds(PIECES * part_rows, part_rows), here] = jnp.where(hit, one, zero)
                rhs[c, :, here] = jnp.where(y_id == y_cell.astype(BF16), one, zero)
        for c in range(parts):
            added = lax.dot_general(
                lhs[c], rhs[c], (((1,), (1,)), ((), ())), preferred_element_type=F32
            )
            pieces = [added[i * part_rows : (i + 1) * part_rows] for i in range(PIECES + 1)]
            for i, value in enumerate((join_small(pieces[:PIECES]), pieces[PIECES])):
                for h in range(width_y // lanes):
                    totals[i, h, pl.ds(c * part_rows, part_rows), :] += value[
                        :, h * lanes : (h + 1) * lanes
                    ]
        return carry

    lax.fori_loop(0, quotient_up(longest, AT_ONCE), add_rows, 0)


def solve_kernel(dims, totals, temp, below, x_low, x_high, summary, factors):
    planes, width_x, width_y = dims
    lanes = totals.shape[3]

    def plane_terms(z):
        here = temp[z]
        x_minus = jnp.concatenate([x_low[z], here[:-1]], axis=0)
        x_plus = jnp.concatenate([here[1:], x_high[z]], axis=0)
        lateral = LATERAL * (
            x_minus
            + x_plus
            + pltpu.roll(here, 1, 1)
            + pltpu.roll(here, width_y - 1, 1)
            - 4.0 * here
        )
        at = pl.ds(z, width_x, stride=planes)
        sums = [
            jnp.concatenate([totals[i, h, at, :] for h in range(width_y // lanes)], axis=1)
            for i in range(2)
        ]
        energy, count = sums
        return here + COUPLE * count, here * here + lateral + COUPLE * TWO_THIRDS * energy

    start = temp[0]
    gate = jnp.where(
        lax.axis_index("gz") > 0, STIFFNESS * (0.5 * (start + below[0])), jnp.zeros_like(start)
    )
    excess, source = plane_terms(0)
    left_excess = jnp.zeros_like(start)
    left_source = jnp.zeros_like(start)
    for z in range(planes - 1):
        face = STIFFNESS * (0.5 * (temp[z + 1] + temp[z]))
        inverse = 1.0 / (gate + face + excess)
        to_left = gate * inverse
        to_right = face * inverse
        factors[z, 0] = to_left
        factors[z, 1] = to_right
        factors[z, 2] = source * inverse
        next_excess, next_source = plane_terms(z + 1)
        left_excess = left_excess + to_left * excess
        left_source = left_source + to_left * source
        gate = gate * to_right
        excess = next_excess + to_right * excess
        source = next_source + to_right * source
    for i, value in enumerate((gate, left_excess, left_source, excess, source)):
        summary[i] = value


def load_five(ref):
    return tuple(ref[i] for i in range(5))


def merge_kernel(level, last, mine, other, _, total):
    upper = (lax.axis_index("gz") & (1 << level)) != 0
    own = load_five(mine)
    came = load_five(other)
    low = tuple(jnp.where(upper, b, a) for a, b in zip(own, came))
    high = tuple(jnp.where(upper, a, b) for a, b in zip(own, came))
    joined = merge(low, high)
    if not last:
        for i in range(5):
            total[i] = joined[i]
        return
    in_upper = (lax.axis_index("gz") & (1 << (level + 1))) != 0
    end = jnp.zeros_like(joined[0])
    closed = suffix_step((end, end), joined)
    total[0] = jnp.where(in_upper, closed[0], joined[3])
    total[1] = jnp.where(in_upper, closed[1], joined[4])


def table_kernel(dims, parts, factors, table, spread):
    planes, width_x, width_y = dims
    part_rows = planes * width_x // parts
    lanes = spread.shape[3]
    zeros = jnp.zeros((width_x, width_y), F32)
    state = (zeros, zeros, zeros + 1.0)
    for z in range(planes - 1, -1, -1):
        if z < planes - 1:
            to_left, to_right, fixed = factors[z, 0], factors[z, 1], factors[z, 2]
            state = (
                fixed + to_right * state[0],
                to_left + to_right * state[1],
                to_right * state[2],
            )
        for t in range(3):
            for h in range(spread.shape[1]):
                spread[t, h, pl.ds(z, width_x, stride=planes), :] = state[t][
                    :, h * lanes : (h + 1) * lanes
                ]
    for c in range(parts):
        for t in range(3):
            for h in range(spread.shape[1]):
                block = spread[t, h, pl.ds(c * part_rows, part_rows), :]
                for i, piece in enumerate(split_small(block)):
                    at = pl.ds((t * PIECES + i) * part_rows, part_rows)
                    table[c, at, pl.ds(h * lanes, lanes)] = piece


def look_kernel(dims, parts, levels, phase, codes, runs, *refs):
    if phase == 0:
        factors, found, keys, spots, table, spread, rhs = refs
        table_kernel(dims, parts, factors, table, spread)
    else:
        table, _, found, keys, spots, rhs = refs
    planes, width_x, width_y = dims
    _, slabs, lanes = codes.shape
    part_rows = planes * width_x // parts
    halves = width_y // lanes
    one = jnp.ones((), F8)
    zero = jnp.zeros((), F8)
    y_id = iota((width_y, lanes), 0).astype(F32).astype(BF16)
    order = levels - 1 - phase
    turns = runs[0:1, :][0, 2 * parts]

    def find_rows(step, carry):
        wanted = []
        for c in range(parts):
            block = step * parts + c
            row, y_cell = decode(codes[(step * levels + order) * parts + c], width_y)
            wanted.append(row)
            hot = y_cell.astype(BF16)
            for s in range(slabs):
                rhs[c, :, pl.ds(s * lanes, lanes)] = jnp.where(
                    y_id == hot[s : s + 1], one, zero
                )
            x_cell = jnp.floor((row - (c * part_rows + 0.5)) * (1.0 / planes))
            half = jnp.floor((y_cell + 0.5) * (1.0 / lanes))
            keys[block] = jnp.where(row > c * part_rows, x_cell * halves + half, -1.0)
            spots[block] = (y_cell - half * lanes).astype(jnp.int32)
        for c in range(parts):
            block = step * parts + c
            row_id = (iota((part_rows, lanes), 0) + (c * part_rows + 1)).astype(F32)
            picked = jnp.dot(table[c], rhs[c], preferred_element_type=F32)
            for s in range(slabs):
                hit = row_id == wanted[c][s : s + 1]
                for t in range(3):
                    pieces = [
                        picked[
                            (t * PIECES + i) * part_rows : (t * PIECES + i + 1) * part_rows,
                            s * lanes : (s + 1) * lanes,
                        ]
                        for i in range(PIECES)
                    ]
                    total = pieces[-1]
                    for piece in pieces[-2::-1]:
                        total = piece + total * (1.0 / STEP)
                    chosen = jnp.sum(jnp.where(hit, total, 0.0), axis=0, keepdims=True)
                    found[t, block, pl.ds(s, 1), :] = chosen * (1.0 / SCALE)
        return carry

    lax.fori_loop(0, quotient_up(turns - order, levels), find_rows, 0)


def quotient_up(value, size):
    return (value + (size - 1)) // size


def join_kernel(dims, parts, levels, runs_vmem, *refs):
    planes, width_x, width_y = dims
    own = load_five(refs[0])
    others = refs[1:levels]
    far = refs[levels]
    found = refs[levels + 1 : 2 * levels + 1]
    keys = refs[2 * levels + 1 : 3 * levels + 1]
    lane_of = refs[3 * levels + 1 : 4 * levels + 1]
    edges, reply, temps, spread = refs[4 * levels + 1 :]
    slabs, rows, lanes = reply.shape
    part_x = width_x // parts
    halves = width_y // lanes
    runs = runs_vmem[...]
    first = [[runs[s, 2 * c] for s in range(slabs)] for c in range(parts)]
    longest = runs[0, 2 * parts]
    spread[:, :, pl.ds(0, rows), :] = jnp.zeros((parts, slabs, rows, lanes), F32)
    index = lax.axis_index("gz")
    zeros = jnp.zeros_like(own[0])
    top = (index & (1 << (levels - 1))) != 0
    before = (jnp.where(top, far[0], zeros + 1.0), jnp.where(top, far[1], zeros))
    after = (jnp.where(top, zeros, far[0]), jnp.where(top, zeros, far[1]))
    for level in range(levels - 2, -1, -1):
        upper = (index & (1 << level)) != 0
        segment = load_five(others[level])
        with_before = prefix_step(before, segment)
        with_after = suffix_step(after, segment)
        before = tuple(jnp.where(upper, a, b) for a, b in zip(with_before, before))
        after = tuple(jnp.where(upper, b, a) for a, b in zip(with_after, after))
    through = prefix_step(before, own)
    value = (through[1] + after[1]) / (through[0] + after[0])
    edges[0] = (before[1] + own[2] + own[0] * value) / (before[0] + own[1] + own[0])
    edges[1] = value

    def fill_rows(step, carry):
        for phase in range(levels):
            done = step * levels + (levels - 1 - phase) < longest
            for c in range(parts):
                block = step * parts + c
                key = keys[phase][block]
                lane = lane_of[phase][block] & (lanes - 1)
                ends = [jnp.zeros((slabs, lanes), F32), jnp.zeros((slabs, lanes), F32)]
                for x in range(part_x):
                    for h in range(halves):
                        hit = key == float(x * halves + h)
                        for e in range(2):
                            line = edges[e, pl.ds(c * part_x + x, 1), pl.ds(h * lanes, lanes)]
                            line = jnp.broadcast_to(line, (slabs, lanes))
                            ends[e] = jnp.where(
                                hit, jnp.take_along_axis(line, lane, axis=1), ends[e]
                            )
                temps[phase * parts + c] = jnp.where(
                    done,
                    found[phase][0, block]
                    + found[phase][1, block] * ends[0]
                    + found[phase][2, block] * ends[1],
                    0.0,
                )
        for phase in range(levels):
            for c in range(parts):
                for s in range(slabs):
                    spot = first[c][s] + step * levels + (levels - 1 - phase)
                    spread[c, s, pl.ds(spot, 1), :] = temps[phase * parts + c, pl.ds(s, 1), :]
        return carry

    lax.fori_loop(0, quotient_up(longest, levels), fill_rows, 0)
    total = spread[0, :, pl.ds(0, rows), :]
    for c in range(1, parts):
        total = total + spread[c, :, pl.ds(0, rows), :]
    reply[...] = total


def fill_planes(factors, edges, new_temp):
    planes = new_temp.shape[0]
    edge = edges[0]
    value = edges[1]
    new_temp[planes - 1] = value
    for z in range(planes - 2, -1, -1):
        value = factors[z, 2] + factors[z, 0] * edge + factors[z, 1] * value
        new_temp[z] = value


def spot_kernel(parts, slots, lanes, starts, meta, velocity, noise, spots, base, push):
    in_use = meta[...] >= 0
    for i in range(3):
        base[i] = jnp.where(in_use, (1.0 - KICK_RATE) * velocity[i], 0.0)
        push[i] = jnp.where(in_use, noise[i], 0.0)
    bricks = starts.shape[0]
    slot = iota((bricks, slots), 1).astype(F32).astype(BF16)
    one = jnp.ones((), BF16)
    zero = jnp.zeros((), BF16)
    for c in range(parts):
        begin = jnp.broadcast_to(starts[:, c : c + 1], (bricks, slots))
        target = quotient(begin, lanes).astype(F32)
        for i in range(2):
            at = pl.ds((2 * c + i) * bricks, bricks)
            spots[at, :] = jnp.where(slot == (target + float(i)).astype(BF16), one, zero)


def kick_kernel(
    parts, returned, spots, meta, starts, base, push, factors, edges,
    out, new_temp, kicked, filled, left,
):
    fill_planes(factors, edges, filled)
    copies = [pltpu.make_async_copy(filled, new_temp, left.at[3])]
    copies[0].start()
    bricks, lanes = meta.shape
    packed = meta[...]
    lane = iota((bricks, lanes), 1)
    in_use = packed >= 0
    place = quotient(jnp.maximum(packed, 0), parts)
    part = jnp.maximum(packed, 0) - place * parts
    values = jnp.concatenate(split(returned[...], 2), axis=1)
    moved = jnp.dot(spots[...], values, preferred_element_type=F32)
    moved = moved[:, :lanes] + moved[:, lanes:]
    at = place & (lanes - 1)
    temp = jnp.zeros((bricks, lanes), F32)
    for c in range(parts):
        shift = jnp.broadcast_to(starts[:, c : c + 1], (bricks, lanes)) & (lanes - 1)
        here = moved[2 * c * bricks : (2 * c + 1) * bricks]
        after = moved[(2 * c + 1) * bricks : (2 * c + 2) * bricks]
        whole = jnp.where(lane >= shift, here, after)
        temp = jnp.where(part == c, jnp.take_along_axis(whole, at, axis=1), temp)
    root = jnp.where(in_use, jnp.sqrt(2.0 * KICK_RATE * temp), 0.0)
    for i in range(3):
        kicked[i] = base[i] + root * push[i]
        copies.append(pltpu.make_async_copy(kicked.at[i], out.at[i], left.at[i]))
        copies[-1].start()
    for copy in copies:
        copy.wait()


def call(kernel, out_shape, scratch=(), spaces=None, limit=VMEM_LIMIT, cost=None, outs=None):
    extra = {} if cost is None else {"cost_estimate": cost}
    if spaces is not None:
        extra["in_specs"] = [pl.BlockSpec(memory_space=m) for m in spaces]
    if outs is not None:
        extra["out_specs"] = tuple(pl.BlockSpec(memory_space=m) for m in outs)
    return pl.pallas_call(
        kernel,
        out_shape=out_shape,
        **extra,
        scratch_shapes=list(scratch),
        compiler_params=pltpu.CompilerParams(vmem_limit_bytes=limit),
    )


def struct(*shape, dtype=F32):
    return jax.ShapeDtypeStruct(shape, dtype)


def route_call(dims, slabs, rows, parts, velocity_shape, plane_shape):
    bricks, lanes = plane_shape
    return call(
        functools.partial(route_kernel, dims, slabs, rows, parts),
        (
            struct(slabs, 2, rows, lanes),
            struct(bricks, lanes, dtype=jnp.int32),
            struct(bricks, lanes, dtype=jnp.int32),
        ),
        (
            pltpu.VMEM(velocity_shape, F32),
            pltpu.VMEM(plane_shape, jnp.int32),
            pltpu.VMEM(plane_shape, jnp.int32),
            pltpu.VMEM((1, bricks), jnp.int32),
            pltpu.SemaphoreType.DMA((4,)),
        ),
        (pltpu.HBM,) * 4,
        ROUTE_LIMIT,
    )


def body(atom_velocity, atom_noise, atom_plane, atom_column, brick_count, electron_temp):
    dims = electron_temp.shape
    planes, width_x, width_y = dims
    cells = planes * width_x
    slabs = lax.axis_size("gz")
    groups = lax.axis_size("gx")
    levels = slabs.bit_length() - 1
    assert slabs == 1 << levels and levels > 0
    bricks, lanes = atom_plane.shape
    rows = 2 * bricks // slabs
    parts = PARTS
    assert width_x % parts == 0 and parts <= 4 and lanes <= 128
    send, meta, starts = route_call(
        dims, slabs, rows, parts, atom_velocity.shape, atom_plane.shape
    )(
        *(
            pltpu.with_memory_space_constraint(x, pltpu.HBM)
            for x in (brick_count.reshape(1, bricks), atom_velocity, atom_plane, atom_column)
        )
    )
    spots, base, push = call(
        functools.partial(spot_kernel, parts, slabs * rows, lanes),
        (
            struct(2 * parts * bricks, slabs * rows, dtype=BF16),
            struct(*atom_velocity.shape),
            struct(*atom_noise.shape),
        ),
    )(starts, meta, atom_velocity, atom_noise)
    got = lax.all_to_all(send, "gz", split_axis=0, concat_axis=0, tiled=True)
    below = lax.ppermute(electron_temp[-1:], "gz", [(i, i + 1) for i in range(slabs - 1)])
    x_low = lax.ppermute(
        electron_temp[:, -1:], "gx", [(i, (i + 1) % groups) for i in range(groups)]
    )
    x_high = lax.ppermute(
        electron_temp[:, :1], "gx", [((i + 1) % groups, i) for i in range(groups)]
    )
    totals, codes, runs = call(
        functools.partial(bin_kernel, dims, parts),
        (
            struct(2, width_y // lanes, cells, lanes),
            struct(parts * (rows + AT_ONCE), slabs, lanes),
            struct(slabs, lanes, dtype=jnp.int32),
        ),
        (
            pltpu.VMEM((parts, (PIECES + 1) * cells // parts, AT_ONCE * slabs * lanes), F8),
            pltpu.VMEM((parts, width_y, AT_ONCE * slabs * lanes), F8),
        ),
    )(got, spots)
    total, factors = call(
        functools.partial(solve_kernel, dims),
        (struct(5, width_x, width_y), struct(planes - 1, 3, width_x, width_y)),
    )(totals, electron_temp, below, x_low, x_high)
    blocks = parts * quotient_up(rows, levels)
    found_shapes = (
        struct(3, blocks, slabs, lanes),
        struct(blocks, slabs, lanes),
        struct(blocks, slabs, lanes, dtype=jnp.int32),
    )
    table_shape = (parts, 3 * PIECES * cells // parts, width_y)
    pieces = [total]
    found = []
    for level in range(levels):
        other = lax.ppermute(total, "gz", [(i, i ^ (1 << level)) for i in range(slabs)])
        outs = call(
            functools.partial(look_kernel, dims, parts, levels, level),
            found_shapes + ((struct(*table_shape, dtype=F8),) if level == 0 else ()),
            (() if level else (pltpu.VMEM((3, width_y // lanes, cells, lanes), F32),))
            + (pltpu.VMEM((parts, width_y, slabs * lanes), F8),),
            cost=LOOK_COST,
        )(codes, runs, *((table, total) if level else (factors,)))
        if level == 0:
            table = outs[3]
        found.append(outs[:3])
        pieces.append(other)
        if level < levels - 1:
            last = level == levels - 2
            total = call(
                functools.partial(merge_kernel, level, last),
                struct(2 if last else 5, width_x, width_y),
            )(total, other, outs[1])
    edges, reply = call(
        functools.partial(join_kernel, dims, parts, levels),
        (struct(2, width_x, width_y), struct(slabs, rows, lanes)),
        (
            pltpu.VMEM((levels * parts, slabs, lanes), F32),
            pltpu.VMEM((parts, slabs, 2 * rows + 8 * levels, lanes), F32),
        ),
    )(runs, *pieces, *(phase[i] for i in range(3) for phase in found))
    returned = lax.all_to_all(reply, "gz", split_axis=0, concat_axis=0, tiled=True)
    new_velocity, new_temp = call(
        functools.partial(kick_kernel, parts),
        (struct(*atom_velocity.shape), struct(*dims)),
        (
            pltpu.VMEM(atom_velocity.shape, F32),
            pltpu.VMEM(dims, F32),
            pltpu.SemaphoreType.DMA((4,)),
        ),
        outs=(pltpu.HBM, pltpu.HBM),
    )(
        returned.reshape(slabs * rows, lanes), spots, meta, starts, base, push, factors,
        edges,
    )
    return (new_temp, new_velocity)


def solution(mesh):
    placed = (
        P(None, ("gz", "gx"), None),
        P(None, ("gz", "gx"), None),
        P(("gz", "gx"), None),
        P(("gz", "gx"), None),
        P(("gz", "gx")),
        P("gz", "gx", None),
    )
    return jax.shard_map(
        body,
        mesh=mesh,
        in_specs=placed,
        out_specs=(P("gz", "gx", None), P(None, ("gz", "gx"), None)),
        check_vma=False,
    )
```

```python
import functools

import jax
import jax.numpy as jnp
from jax import lax
from jax.experimental import pallas as pl
from jax.experimental.pallas import tpu as pltpu
from jax.sharding import PartitionSpec as P

STIFFNESS = 10000.0
LATERAL = 0.1
COUPLE = 0.5
TWO_THIRDS = 2.0 / 3.0
KICK_RATE = 0.2
F32 = jnp.float32
BF16 = jnp.bfloat16
F8 = jnp.float8_e4m3fn
SCALE = 8.0
STEP = 16.0
PIECES = 3
PARTS = 4
AT_ONCE = 3
ROUTE_LIMIT = 32 * 1024 * 1024
VMEM_LIMIT = 32 * 1024 * 1024
LOOK_COST = pl.CostEstimate(flops=2 * 10**9, bytes_accessed=10**7, transcendentals=0)


def quotient(value, size):
    if size & (size - 1) == 0:
        return lax.shift_right_logical(value, size.bit_length() - 1)
    return value // size


def iota(shape, dim):
    return lax.broadcasted_iota(jnp.int32, shape, dim)


def split(value, pieces):
    parts = []
    for _ in range(pieces):
        part = value.astype(BF16)
        parts.append(part)
        value = value - part.astype(F32)
    return parts


def split_small(value):
    value = value * SCALE
    parts = []
    for _ in range(PIECES):
        part = value.astype(F8)
        parts.append(part)
        value = (value - part.astype(F32)) * STEP
    return parts


def join_small(parts):
    total = parts[-1]
    for part in parts[-2::-1]:
        total = part + total * (1.0 / STEP)
    return total * (1.0 / SCALE)


def merge(left, right):
    g_a, sl_a, rl_a, s_a, r_a = left
    g_b, sl_b, rl_b, s_b, r_b = right
    excess = s_a + sl_b
    source = r_a + rl_b
    inverse = 1.0 / (g_a + g_b + excess)
    to_left = g_a * inverse
    to_right = g_b * inverse
    return (
        g_a * to_right,
        sl_a + to_left * excess,
        rl_a + to_left * source,
        s_b + to_right * excess,
        r_b + to_right * source,
    )


def prefix_step(state, segment):
    gate, sl, rl, s, r = segment
    excess = state[0] + sl
    source = state[1] + rl
    ratio = gate / (gate + excess)
    return (s + ratio * excess, r + ratio * source)


def suffix_step(state, segment):
    gate, sl, rl, s, r = segment
    excess = s + state[0]
    source = r + state[1]
    ratio = gate / (gate + excess)
    return (sl + ratio * excess, rl + ratio * source)


def route_kernel(
    dims, slabs, rows, parts, count_hbm, velocity_hbm, plane_hbm, column_hbm, send, meta, starts,
    velocity, plane, column, count, arrived,
):
    copies = [
        pltpu.make_async_copy(source, target, arrived.at[i])
        for i, (source, target) in enumerate(
            (
                (count_hbm, count),
                (plane_hbm, plane),
                (column_hbm, column),
                (velocity_hbm, velocity),
            )
        )
    ]
    for copy in copies:
        copy.start()
    planes, width_x, width_y = dims
    bricks, lanes = plane.shape
    part_rows = planes * width_x // parts
    lane = iota((bricks, lanes), 1)
    sub_b = iota((bricks, bricks), 0)
    lane_b = iota((bricks, bricks), 1)
    eye = sub_b == lane_b
    sub_l = iota((lanes, lanes), 0)
    lane_l = iota((lanes, lanes), 1)
    prefix = jnp.concatenate(
        [jnp.where(sub_l <= lane_l, 1.0, 0.0), jnp.ones((lanes, lanes), F32)], axis=1
    ).astype(BF16)
    copies[0].wait()
    count_row = jnp.broadcast_to(count[...].astype(F32), (bricks, bricks))
    count_col = jnp.sum(jnp.where(eye, count_row, 0.0), axis=1, keepdims=True).astype(jnp.int32)
    in_use = lane < count_col
    copies[1].wait()
    owner = quotient(plane[:, 0:1], planes)
    owner_f = jnp.broadcast_to(owner.astype(F32), (bricks, bricks))
    owner_row = jnp.sum(jnp.where(eye, owner_f, 0.0), axis=0, keepdims=True)
    same = owner_f == owner_row
    ahead = same & (lane_b < sub_b)
    peers = jnp.where(jnp.concatenate([same, ahead], axis=0), 1.0, 0.0).astype(BF16)
    copies[2].wait()
    col = column[...]
    x_cell = quotient(col, width_y)
    y_cell = col - x_cell * width_y
    row = x_cell * planes + plane[...] - owner * planes
    code = jnp.where(in_use, (row + 1) * width_y + y_cell, 0)
    part = jnp.where(in_use, quotient(row, part_rows), parts)
    inside = [jnp.where(part == c, 1.0, 0.0).astype(BF16) for c in range(parts)]
    sums = jnp.dot(jnp.concatenate(inside, axis=0), prefix, preferred_element_type=F32)
    ranks = [sums[c * bricks : (c + 1) * bricks, :lanes] for c in range(parts)]
    sizes = [sums[c * bricks : (c + 1) * bricks, lanes:] for c in range(parts)]
    earlier = [jnp.zeros_like(sizes[0])]
    for c in range(parts - 1):
        earlier.append(earlier[-1] + sizes[c])
    joint = jnp.dot(
        peers, jnp.concatenate(sizes, axis=1).astype(BF16), preferred_element_type=F32
    )
    copies[3].wait()
    vx, vy, vz = velocity[0], velocity[1], velocity[2]
    kinetic = 0.5 * (vx * vx + vy * vy + vz * vz)
    dense = jnp.zeros((bricks, lanes), F32)
    whole = jnp.zeros((bricks, lanes), F32)
    bases = []
    for c in range(parts):
        bases.append((dense, whole))
        size = joint[:bricks, c * lanes : (c + 1) * lanes]
        dense = dense + size
        whole = whole + jnp.floor((size + (lanes - 1)) * (1.0 / lanes)) * lanes
    begins = [
        owner * (rows * lanes)
        + (
            jnp.where(whole <= rows * lanes, base[1], base[0])
            + joint[bricks:, c * lanes : (c + 1) * lanes]
        ).astype(jnp.int32)
        for c, base in enumerate(bases)
    ]
    shifts = [begin & (lanes - 1) for begin in begins]
    packed = ranks[0].astype(jnp.int32)
    run = jnp.zeros((bricks, lanes), jnp.int32)
    base = jnp.zeros((bricks, lanes), F32)
    lane_f = lane.astype(F32)
    for c in range(1, parts):
        packed = packed | (ranks[c].astype(jnp.int32) << (8 * c))
        run = jnp.where(lane_f >= earlier[c], 8 * c, run)
        base = jnp.where(lane_f >= earlier[c], earlier[c], base)
    wanted = lane - base.astype(jnp.int32)
    found = jnp.zeros((bricks, lanes), jnp.int32)
    step = lanes
    while step > 1:
        ways = 4 if step >= 4 else 2
        step //= ways
        gain = jnp.zeros((bricks, lanes), jnp.int32)
        for way in range(1, ways):
            at = jnp.take_along_axis(packed, found + (way * step - 1), axis=1)
            at = lax.shift_right_logical(at, run) & 255
            gain = jnp.where(at <= wanted, way * step, gain)
        found = found + gain
    kinetic = jnp.take_along_axis(kinetic, found, axis=1)
    code = jnp.take_along_axis(code, found, axis=1)
    zero = jnp.zeros((bricks, lanes), BF16)
    slot = iota((slabs * rows, bricks), 0).astype(F32).astype(BF16)
    values = []
    spots = []
    place = jnp.full((bricks, lanes), -1, jnp.int32)
    table = jnp.zeros((bricks, lanes), jnp.int32)
    for c in range(parts):
        table = jnp.where(lane == c, begins[c], table)
        place = jnp.where(
            part == c, (begins[c] + ranks[c].astype(jnp.int32) - 1) * parts + c, place
        )
        turn = (lane - shifts[c]) & (lanes - 1)
        valid = turn.astype(F32) < sizes[c]
        turn = (turn + earlier[c].astype(jnp.int32)) & (lanes - 1)
        kin = jnp.where(valid, jnp.take_along_axis(kinetic, turn, axis=1), 0.0)
        cell = jnp.where(valid, jnp.take_along_axis(code, turn, axis=1), 0)
        cell_row = quotient(cell, width_y)
        cell_y = cell - cell_row * width_y
        pieces = split(kin, 2) + [cell_row.astype(F32).astype(BF16), cell_y.astype(F32).astype(BF16)]
        first = lane >= shifts[c]
        values.append(jnp.concatenate([jnp.where(first, p, zero) for p in pieces], axis=1))
        values.append(jnp.concatenate([jnp.where(first, zero, p) for p in pieces], axis=1))
        begin_row = jnp.sum(
            jnp.where(eye, begins[c].astype(F32), 0.0), axis=0, keepdims=True
        ).astype(jnp.int32)
        target = quotient(begin_row, lanes).astype(F32)
        spots.append(slot == target.astype(BF16))
        spots.append(slot == (target + 1.0).astype(BF16))
    starts[...] = table
    meta[...] = place
    one = jnp.ones((), BF16)
    moved = jnp.dot(
        jnp.concatenate([jnp.where(spot, one, jnp.zeros((), BF16)) for spot in spots], axis=1),
        jnp.concatenate(values, axis=0),
        preferred_element_type=F32,
    )
    send[:, 0] = (moved[:, :lanes] + moved[:, lanes : 2 * lanes]).reshape(slabs, rows, lanes)
    send[:, 1] = (moved[:, 2 * lanes : 3 * lanes] * width_y + moved[:, 3 * lanes :]).reshape(
        slabs, rows, lanes
    )


def decode(code, width_y):
    row = jnp.floor((code + 0.5) * (1.0 / width_y))
    return row, code - row * width_y


def find_runs(dims, parts, got, runs_vmem):
    planes, width_x, width_y = dims
    slabs, _, rows, lanes = got.shape
    part_rows = planes * width_x // parts
    codes = got[:, 1]
    beyond = float((parts * part_rows + 1) * width_y + 1)
    lead = codes[:, :, 0:1]
    used = lead > 0.0
    lead = jnp.where(used, lead, beyond)
    top = jnp.where(used, jnp.max(codes, axis=2, keepdims=True), beyond)
    longest = jnp.zeros((slabs, 1), F32)
    first = jnp.zeros((slabs, 1), F32)
    table = jnp.zeros((slabs, lanes), F32)
    lane = iota((slabs, lanes), 1)
    for c in range(parts):
        limit = float(((c + 1) * part_rows + 1) * width_y)
        last = jnp.sum(jnp.where(lead < limit, 1.0, 0.0), axis=1)
        longest = jnp.maximum(longest, last - first)
        table = jnp.where(lane == 2 * c, first, table)
        table = jnp.where(lane == 2 * c + 1, last, table)
        first = jnp.sum(jnp.where(top < limit, 1.0, 0.0), axis=1)
    longest = jnp.max(longest, axis=0, keepdims=True)
    runs_vmem[...] = jnp.where(lane == 2 * parts, longest, table).astype(jnp.int32)


def run_row(got, field, s, spot, last):
    rows = got.shape[2]
    loaded = got[s, field, pl.ds(jnp.minimum(spot, rows - 1), 1), :]
    return jnp.where(spot < last, loaded, 0.0)


def bin_kernel(dims, parts, got, _, totals, codes, runs_vmem, lhs, rhs):
    planes, width_x, width_y = dims
    slabs, _, rows, lanes = got.shape
    part_rows = planes * width_x // parts
    find_runs(dims, parts, got, runs_vmem)
    runs = runs_vmem[...]
    first = [[runs[s, 2 * c] for s in range(slabs)] for c in range(parts)]
    last = [[runs[s, 2 * c + 1] for s in range(slabs)] for c in range(parts)]
    longest = runs[0, 2 * parts]
    one = jnp.ones((), F8)
    zero = jnp.zeros((), F8)
    y_id = iota((width_y, lanes), 0).astype(F32).astype(BF16)
    totals[...] = jnp.zeros(totals.shape, F32)

    def add_rows(begin, at_once):
        for c in range(parts):
            row_id = (iota((part_rows, lanes), 0) + (c * part_rows + 1)).astype(F32).astype(BF16)
            for i in range(at_once * slabs):
                s = i % slabs
                turn = begin + i // slabs
                spot = first[c][s] + turn
                pieces = split_small(run_row(got, 0, s, spot, last[c][s]))
                code = run_row(got, 1, s, spot, last[c][s])
                codes[turn * parts + c, pl.ds(s, 1), :] = code
                row, y_cell = decode(code, width_y)
                here = pl.ds(i * lanes, lanes)
                hit = row_id == row.astype(BF16)
                for j, piece in enumerate(pieces):
                    lhs[c, pl.ds(j * part_rows, part_rows), here] = jnp.where(hit, piece, zero)
                lhs[c, pl.ds(PIECES * part_rows, part_rows), here] = jnp.where(hit, one, zero)
                rhs[c, :, here] = jnp.where(y_id == y_cell.astype(BF16), one, zero)
        for c in range(parts):
            width = pl.ds(0, at_once * slabs * lanes)
            added = lax.dot_general(
                lhs[c, :, width],
                rhs[c, :, width],
                (((1,), (1,)), ((), ())),
                preferred_element_type=F32,
            )
            pieces = [added[i * part_rows : (i + 1) * part_rows] for i in range(PIECES + 1)]
            for i, value in enumerate((join_small(pieces[:PIECES]), pieces[PIECES])):
                for h in range(width_y // lanes):
                    totals[i, h, pl.ds(c * part_rows, part_rows), :] += value[
                        :, h * lanes : (h + 1) * lanes
                    ]

    def many_turns(step, carry):
        add_rows(step * AT_ONCE, AT_ONCE)
        return carry

    def one_turn(turn, carry):
        add_rows(turn, 1)
        return carry

    steps = short_quotient(longest, AT_ONCE)
    lax.fori_loop(0, steps, many_turns, 0)
    lax.fori_loop(steps * AT_ONCE, longest, one_turn, 0)


def solve_kernel(dims, totals, temp, below, x_low, x_high, summary, factors):
    planes, width_x, width_y = dims
    lanes = totals.shape[3]

    def plane_terms(z):
        here = temp[z]
        x_minus = jnp.concatenate([x_low[z], here[:-1]], axis=0)
        x_plus = jnp.concatenate([here[1:], x_high[z]], axis=0)
        lateral = LATERAL * (
            x_minus
            + x_plus
            + pltpu.roll(here, 1, 1)
            + pltpu.roll(here, width_y - 1, 1)
            - 4.0 * here
        )
        at = pl.ds(z, width_x, stride=planes)
        sums = [
            jnp.concatenate([totals[i, h, at, :] for h in range(width_y // lanes)], axis=1)
            for i in range(2)
        ]
        energy, count = sums
        return here + COUPLE * count, here * here + lateral + COUPLE * TWO_THIRDS * energy

    start = temp[0]
    gate = jnp.where(
        lax.axis_index("gz") > 0, STIFFNESS * (0.5 * (start + below[0])), jnp.zeros_like(start)
    )
    excess, source = plane_terms(0)
    left_excess = jnp.zeros_like(start)
    left_source = jnp.zeros_like(start)
    for z in range(planes - 1):
        face = STIFFNESS * (0.5 * (temp[z + 1] + temp[z]))
        inverse = 1.0 / (gate + face + excess)
        to_left = gate * inverse
        to_right = face * inverse
        factors[z, 0] = to_left
        factors[z, 1] = to_right
        factors[z, 2] = source * inverse
        next_excess, next_source = plane_terms(z + 1)
        left_excess = left_excess + to_left * excess
        left_source = left_source + to_left * source
        gate = gate * to_right
        excess = next_excess + to_right * excess
        source = next_source + to_right * source
    for i, value in enumerate((gate, left_excess, left_source, excess, source)):
        summary[i] = value


def load_five(ref):
    return tuple(ref[i] for i in range(5))


def merge_kernel(level, last, mine, other, _, total):
    upper = (lax.axis_index("gz") & (1 << level)) != 0
    own = load_five(mine)
    came = load_five(other)
    low = tuple(jnp.where(upper, b, a) for a, b in zip(own, came))
    high = tuple(jnp.where(upper, a, b) for a, b in zip(own, came))
    joined = merge(low, high)
    if not last:
        for i in range(5):
            total[i] = joined[i]
        return
    in_upper = (lax.axis_index("gz") & (1 << (level + 1))) != 0
    end = jnp.zeros_like(joined[0])
    closed = suffix_step((end, end), joined)
    total[0] = jnp.where(in_upper, closed[0], joined[3])
    total[1] = jnp.where(in_upper, closed[1], joined[4])


def table_kernel(dims, parts, factors, table, spread):
    planes, width_x, width_y = dims
    part_rows = planes * width_x // parts
    lanes = spread.shape[3]
    zeros = jnp.zeros((width_x, width_y), F32)
    state = (zeros, zeros, zeros + 1.0)
    for z in range(planes - 1, -1, -1):
        if z < planes - 1:
            to_left, to_right, fixed = factors[z, 0], factors[z, 1], factors[z, 2]
            state = (
                fixed + to_right * state[0],
                to_left + to_right * state[1],
                to_right * state[2],
            )
        for t in range(3):
            for h in range(spread.shape[1]):
                spread[t, h, pl.ds(z, width_x, stride=planes), :] = state[t][
                    :, h * lanes : (h + 1) * lanes
                ]
    for c in range(parts):
        for t in range(3):
            for h in range(spread.shape[1]):
                block = spread[t, h, pl.ds(c * part_rows, part_rows), :]
                for i, piece in enumerate(split_small(block)):
                    at = pl.ds((t * PIECES + i) * part_rows, part_rows)
                    table[c, at, pl.ds(h * lanes, lanes)] = piece


def look_kernel(dims, parts, levels, phase, codes, runs, *refs):
    if phase == 0:
        factors, found, keys, spots, table, spread, rhs = refs
        table_kernel(dims, parts, factors, table, spread)
    else:
        table, _, found, keys, spots, rhs = refs
    planes, width_x, width_y = dims
    _, slabs, lanes = codes.shape
    part_rows = planes * width_x // parts
    halves = width_y // lanes
    one = jnp.ones((), F8)
    zero = jnp.zeros((), F8)
    y_id = iota((width_y, lanes), 0).astype(F32).astype(BF16)
    order = levels - 1 - phase
    turns = runs[0:1, :][0, 2 * parts]

    def find_rows(step, carry):
        wanted = []
        for c in range(parts):
            block = step * parts + c
            row, y_cell = decode(codes[(step * levels + order) * parts + c], width_y)
            wanted.append(row)
            hot = y_cell.astype(BF16)
            for s in range(slabs):
                rhs[c, :, pl.ds(s * lanes, lanes)] = jnp.where(
                    y_id == hot[s : s + 1], one, zero
                )
            x_cell = jnp.floor((row - (c * part_rows + 0.5)) * (1.0 / planes))
            half = jnp.floor((y_cell + 0.5) * (1.0 / lanes))
            keys[block] = jnp.where(row > c * part_rows, x_cell * halves + half, -1.0)
            spots[block] = (y_cell - half * lanes).astype(jnp.int32)
        for c in range(parts):
            block = step * parts + c
            row_id = (iota((part_rows, lanes), 0) + (c * part_rows + 1)).astype(F32)
            picked = jnp.dot(table[c], rhs[c], preferred_element_type=F32)
            for s in range(slabs):
                hit = row_id == wanted[c][s : s + 1]
                for t in range(3):
                    pieces = [
                        picked[
                            (t * PIECES + i) * part_rows : (t * PIECES + i + 1) * part_rows,
                            s * lanes : (s + 1) * lanes,
                        ]
                        for i in range(PIECES)
                    ]
                    total = pieces[-1]
                    for piece in pieces[-2::-1]:
                        total = piece + total * (1.0 / STEP)
                    chosen = jnp.sum(jnp.where(hit, total, 0.0), axis=0, keepdims=True)
                    found[t, block, pl.ds(s, 1), :] = chosen * (1.0 / SCALE)
        return carry

    lax.fori_loop(0, quotient_up(turns - order, levels), find_rows, 0)


def short_quotient(value, size):
    return (value * (-(-(1 << 16) // size))) >> 16


def quotient_up(value, size):
    return short_quotient(value + (size - 1), size)


def join_kernel(dims, parts, levels, runs_vmem, *refs):
    planes, width_x, width_y = dims
    own = load_five(refs[0])
    others = refs[1:levels]
    far = refs[levels]
    found = refs[levels + 1 : 2 * levels + 1]
    keys = refs[2 * levels + 1 : 3 * levels + 1]
    lane_of = refs[3 * levels + 1 : 4 * levels + 1]
    edges, reply, temps, spread = refs[4 * levels + 1 :]
    slabs, rows, lanes = reply.shape
    part_x = width_x // parts
    halves = width_y // lanes
    runs = runs_vmem[...]
    first = [[runs[s, 2 * c] for s in range(slabs)] for c in range(parts)]
    longest = runs[0, 2 * parts]
    spread[:, :, pl.ds(0, rows), :] = jnp.zeros((parts, slabs, rows, lanes), F32)
    index = lax.axis_index("gz")
    zeros = jnp.zeros_like(own[0])
    top = (index & (1 << (levels - 1))) != 0
    before = (jnp.where(top, far[0], zeros + 1.0), jnp.where(top, far[1], zeros))
    after = (jnp.where(top, zeros, far[0]), jnp.where(top, zeros, far[1]))
    for level in range(levels - 2, -1, -1):
        upper = (index & (1 << level)) != 0
        segment = load_five(others[level])
        with_before = prefix_step(before, segment)
        with_after = suffix_step(after, segment)
        before = tuple(jnp.where(upper, a, b) for a, b in zip(with_before, before))
        after = tuple(jnp.where(upper, b, a) for a, b in zip(with_after, after))
    through = prefix_step(before, own)
    value = (through[1] + after[1]) / (through[0] + after[0])
    edges[0] = (before[1] + own[2] + own[0] * value) / (before[0] + own[1] + own[0])
    edges[1] = value

    def fill_rows(step, carry):
        for phase in range(levels):
            done = step * levels + (levels - 1 - phase) < longest
            for c in range(parts):
                block = step * parts + c
                key = keys[phase][block]
                lane = lane_of[phase][block] & (lanes - 1)
                ends = [jnp.zeros((slabs, lanes), F32), jnp.zeros((slabs, lanes), F32)]
                for x in range(part_x):
                    for h in range(halves):
                        hit = key == float(x * halves + h)
                        for e in range(2):
                            line = edges[e, pl.ds(c * part_x + x, 1), pl.ds(h * lanes, lanes)]
                            line = jnp.broadcast_to(line, (slabs, lanes))
                            ends[e] = jnp.where(
                                hit, jnp.take_along_axis(line, lane, axis=1), ends[e]
                            )
                temps[phase * parts + c] = jnp.where(
                    done,
                    found[phase][0, block]
                    + found[phase][1, block] * ends[0]
                    + found[phase][2, block] * ends[1],
                    0.0,
                )
        for phase in range(levels):
            for c in range(parts):
                for s in range(slabs):
                    spot = first[c][s] + step * levels + (levels - 1 - phase)
                    spread[c, s, pl.ds(spot, 1), :] = temps[phase * parts + c, pl.ds(s, 1), :]
        return carry

    lax.fori_loop(0, quotient_up(longest, levels), fill_rows, 0)
    total = spread[0, :, pl.ds(0, rows), :]
    for c in range(1, parts):
        total = total + spread[c, :, pl.ds(0, rows), :]
    reply[...] = total


def fill_planes(factors, edges, new_temp):
    planes = new_temp.shape[0]
    edge = edges[0]
    value = edges[1]
    new_temp[planes - 1] = value
    for z in range(planes - 2, -1, -1):
        value = factors[z, 2] + factors[z, 0] * edge + factors[z, 1] * value
        new_temp[z] = value


def spot_kernel(parts, slots, lanes, starts, meta, velocity, noise, spots, base, push):
    in_use = meta[...] >= 0
    for i in range(3):
        base[i] = jnp.where(in_use, (1.0 - KICK_RATE) * velocity[i], 0.0)
        push[i] = jnp.where(in_use, noise[i], 0.0)
    bricks = starts.shape[0]
    slot = iota((bricks, slots), 1).astype(F32).astype(BF16)
    one = jnp.ones((), BF16)
    zero = jnp.zeros((), BF16)
    for c in range(parts):
        begin = jnp.broadcast_to(starts[:, c : c + 1], (bricks, slots))
        target = quotient(begin, lanes).astype(F32)
        for i in range(2):
            at = pl.ds((2 * c + i) * bricks, bricks)
            spots[at, :] = jnp.where(slot == (target + float(i)).astype(BF16), one, zero)


def kick_kernel(
    parts, returned, spots, meta, starts, base, push, factors, edges,
    out, new_temp, kicked, filled, left,
):
    fill_planes(factors, edges, filled)
    copies = [pltpu.make_async_copy(filled, new_temp, left.at[3])]
    copies[0].start()
    bricks, lanes = meta.shape
    packed = meta[...]
    lane = iota((bricks, lanes), 1)
    in_use = packed >= 0
    place = quotient(jnp.maximum(packed, 0), parts)
    part = jnp.maximum(packed, 0) - place * parts
    values = jnp.concatenate(split(returned[...], 2), axis=1)
    moved = jnp.dot(spots[...], values, preferred_element_type=F32)
    moved = moved[:, :lanes] + moved[:, lanes:]
    at = place & (lanes - 1)
    temp = jnp.zeros((bricks, lanes), F32)
    for c in range(parts):
        shift = jnp.broadcast_to(starts[:, c : c + 1], (bricks, lanes)) & (lanes - 1)
        here = moved[2 * c * bricks : (2 * c + 1) * bricks]
        after = moved[(2 * c + 1) * bricks : (2 * c + 2) * bricks]
        whole = jnp.where(lane >= shift, here, after)
        temp = jnp.where(part == c, jnp.take_along_axis(whole, at, axis=1), temp)
    root = jnp.where(in_use, jnp.sqrt(2.0 * KICK_RATE * temp), 0.0)
    for i in range(3):
        kicked[i] = base[i] + root * push[i]
        copies.append(pltpu.make_async_copy(kicked.at[i], out.at[i], left.at[i]))
        copies[-1].start()
    for copy in copies:
        copy.wait()


def call(kernel, out_shape, scratch=(), spaces=None, limit=VMEM_LIMIT, cost=None, outs=None):
    extra = {} if cost is None else {"cost_estimate": cost}
    if spaces is not None:
        extra["in_specs"] = [pl.BlockSpec(memory_space=m) for m in spaces]
    if outs is not None:
        extra["out_specs"] = tuple(pl.BlockSpec(memory_space=m) for m in outs)
    return pl.pallas_call(
        kernel,
        out_shape=out_shape,
        **extra,
        scratch_shapes=list(scratch),
        compiler_params=pltpu.CompilerParams(vmem_limit_bytes=limit),
    )


def struct(*shape, dtype=F32):
    return jax.ShapeDtypeStruct(shape, dtype)


def route_call(dims, slabs, rows, parts, velocity_shape, plane_shape):
    bricks, lanes = plane_shape
    return call(
        functools.partial(route_kernel, dims, slabs, rows, parts),
        (
            struct(slabs, 2, rows, lanes),
            struct(bricks, lanes, dtype=jnp.int32),
            struct(bricks, lanes, dtype=jnp.int32),
        ),
        (
            pltpu.VMEM(velocity_shape, F32),
            pltpu.VMEM(plane_shape, jnp.int32),
            pltpu.VMEM(plane_shape, jnp.int32),
            pltpu.VMEM((1, bricks), jnp.int32),
            pltpu.SemaphoreType.DMA((4,)),
        ),
        (pltpu.HBM,) * 4,
        ROUTE_LIMIT,
    )


def body(atom_velocity, atom_noise, atom_plane, atom_column, brick_count, electron_temp):
    dims = electron_temp.shape
    planes, width_x, width_y = dims
    cells = planes * width_x
    slabs = lax.axis_size("gz")
    groups = lax.axis_size("gx")
    levels = slabs.bit_length() - 1
    assert slabs == 1 << levels and levels > 0
    bricks, lanes = atom_plane.shape
    rows = 2 * bricks // slabs
    parts = PARTS
    assert width_x % parts == 0 and parts <= 4 and lanes <= 128
    send, meta, starts = route_call(
        dims, slabs, rows, parts, atom_velocity.shape, atom_plane.shape
    )(
        *(
            pltpu.with_memory_space_constraint(x, pltpu.HBM)
            for x in (brick_count.reshape(1, bricks), atom_velocity, atom_plane, atom_column)
        )
    )
    spots, base, push = call(
        functools.partial(spot_kernel, parts, slabs * rows, lanes),
        (
            struct(2 * parts * bricks, slabs * rows, dtype=BF16),
            struct(*atom_velocity.shape),
            struct(*atom_noise.shape),
        ),
    )(starts, meta, atom_velocity, atom_noise)
    got = lax.all_to_all(send, "gz", split_axis=0, concat_axis=0, tiled=True)
    below = lax.ppermute(electron_temp[-1:], "gz", [(i, i + 1) for i in range(slabs - 1)])
    x_low = lax.ppermute(
        electron_temp[:, -1:], "gx", [(i, (i + 1) % groups) for i in range(groups)]
    )
    x_high = lax.ppermute(
        electron_temp[:, :1], "gx", [((i + 1) % groups, i) for i in range(groups)]
    )
    totals, codes, runs = call(
        functools.partial(bin_kernel, dims, parts),
        (
            struct(2, width_y // lanes, cells, lanes),
            struct(parts * (rows + 1), slabs, lanes),
            struct(slabs, lanes, dtype=jnp.int32),
        ),
        (
            pltpu.VMEM((parts, (PIECES + 1) * cells // parts, AT_ONCE * slabs * lanes), F8),
            pltpu.VMEM((parts, width_y, AT_ONCE * slabs * lanes), F8),
        ),
    )(got, spots)
    total, factors = call(
        functools.partial(solve_kernel, dims),
        (struct(5, width_x, width_y), struct(planes - 1, 3, width_x, width_y)),
    )(totals, electron_temp, below, x_low, x_high)
    blocks = parts * quotient_up(rows, levels)
    found_shapes = (
        struct(3, blocks, slabs, lanes),
        struct(blocks, slabs, lanes),
        struct(blocks, slabs, lanes, dtype=jnp.int32),
    )
    table_shape = (parts, 3 * PIECES * cells // parts, width_y)
    pieces = [total]
    found = []
    for level in range(levels):
        other = lax.ppermute(total, "gz", [(i, i ^ (1 << level)) for i in range(slabs)])
        outs = call(
            functools.partial(look_kernel, dims, parts, levels, level),
            found_shapes + ((struct(*table_shape, dtype=F8),) if level == 0 else ()),
            (() if level else (pltpu.VMEM((3, width_y // lanes, cells, lanes), F32),))
            + (pltpu.VMEM((parts, width_y, slabs * lanes), F8),),
            cost=LOOK_COST,
        )(codes, runs, *((table, total) if level else (factors,)))
        if level == 0:
            table = outs[3]
        found.append(outs[:3])
        pieces.append(other)
        if level < levels - 1:
            last = level == levels - 2
            total = call(
                functools.partial(merge_kernel, level, last),
                struct(2 if last else 5, width_x, width_y),
            )(total, other, outs[1])
    edges, reply = call(
        functools.partial(join_kernel, dims, parts, levels),
        (struct(2, width_x, width_y), struct(slabs, rows, lanes)),
        (
            pltpu.VMEM((levels * parts, slabs, lanes), F32),
            pltpu.VMEM((parts, slabs, 2 * rows + 8 * levels, lanes), F32),
        ),
    )(runs, *pieces, *(phase[i] for i in range(3) for phase in found))
    returned = lax.all_to_all(reply, "gz", split_axis=0, concat_axis=0, tiled=True)
    new_velocity, new_temp = call(
        functools.partial(kick_kernel, parts),
        (struct(*atom_velocity.shape), struct(*dims)),
        (
            pltpu.VMEM(atom_velocity.shape, F32),
            pltpu.VMEM(dims, F32),
            pltpu.SemaphoreType.DMA((4,)),
        ),
        outs=(pltpu.HBM, pltpu.HBM),
    )(
        returned.reshape(slabs * rows, lanes), spots, meta, starts, base, push, factors,
        edges,
    )
    return (new_temp, new_velocity)


def solution(mesh):
    placed = (
        P(None, ("gz", "gx"), None),
        P(None, ("gz", "gx"), None),
        P(("gz", "gx"), None),
        P(("gz", "gx"), None),
        P(("gz", "gx")),
        P("gz", "gx", None),
    )
    return jax.shard_map(
        body,
        mesh=mesh,
        in_specs=placed,
        out_specs=(P("gz", "gx", None), P(None, ("gz", "gx"), None)),
        check_vma=False,
    )
```
